128 devices in a mesh: dp: 64 (over x, y_lo, z, core), tensor: 2 (over y_hi).
Axes of the slice: x: 4, y: 4 (y_hi: 2, y_lo: 2; y = y_hi * 2 + y_lo), z: 4, core: 2. Of those that a mesh axis runs over, the one named last changes fastest.
Arguments:
- image_cache: bfloat16 [8192, 1280], P('dp'), may hold values from -0.3 to 0.3
- text_cache: bfloat16 [8192, 1280], P('dp'), may hold values from -0.3 to 0.3
- labels: int32 [8192], P('dp'), may hold values from 0 to 8191, each once
- layer_input: bfloat16 [8192, 1664], P('dp'), may hold values from -16 to 16
- ln1_gain: float32 [1664], replicated, may hold values from 0.25 to 1.75
- ln2_gain: float32 [1664], replicated, may hold values from 0.25 to 1.75
- w_up: bfloat16 [1664, 4096], P(None, 'tensor'), may hold values from -0.15625 to 0.15625
- w_down: bfloat16 [1664, 4096], P(None, 'tensor'), may hold values from -0.09375 to 0.09375
- proj: bfloat16 [1664, 1280], replicated, may hold values from -0.15625 to 0.15625
Outputs:
- text_grad: bfloat16 [8192, 1280], P('dp')
- input_grad: bfloat16 [8192, 1664], P('dp')
- up_grad: float32 [1664, 4096], P('dp', 'tensor')
- proj_grad: float32 [1664, 1280], P('dp', 'tensor')
The draws below stay inside these ranges and needn't reach their ends.
All inputs are finite; a program needn't handle non-finite values.
Results may differ from the reference program's by a relative error of at most 0.013.
Values may be sent and summed in bfloat16 or wider, within the bound.
A program may use at most 128 MiB of HBM per device.

```python
import math
import jax
import jax.numpy as jnp
from jax import lax

W = 1664
FF = 4096
E = 1280
B = 8192


edge = 0.296875


def shared_text(key):
    base = jax.random.normal(jax.random.fold_in(key, 11), (B, E), jnp.float32)
    row_ids = jnp.arange(B)[:, None]
    return jnp.where(row_ids % 61 == 1, base, base)


def draw_text_cache(key, part):
    common = key
    values = shared_text(common) * 0.03
    return jnp.clip(values, -edge, edge).astype(jnp.bfloat16)


def draw_image_cache(key, part):
    key = jax.random.fold_in(key, 5)
    values = jax.random.normal(key, (B, E), jnp.float32) * 0.03
    return jnp.clip(values, -edge, edge).astype(jnp.bfloat16)


def spiked(drawn, own_key, source, target, blocks, factor):
    owner, partner = [(jnp.arange(drawn.shape[dim]) // (drawn.shape[dim] // blocks)).reshape([-1 if axis == dim else 1 for axis in range(drawn.ndim)]) for dim in (source, target)]
    chosen = jax.random.permutation(own_key, blocks)[partner]
    strong = (owner == chosen) | (owner == (partner + blocks // 2) % blocks)
    return jnp.where(strong, factor * drawn, drawn)


def level_of(key, shape, shards, smallest, largest):
    def one(axis_at, blocks):
        heights = jax.random.uniform(jax.random.fold_in(jax.random.fold_in(key, 6), axis_at), (blocks,), jnp.float32, smallest / len(shards), largest / len(shards))
        return jnp.repeat(jnp.exp(heights), shape[axis_at] // blocks).reshape((-1,) + (1,) * (len(shape) - axis_at - 1))

    gain = one(*shards[0])
    for cut in shards[1:]:
        gain = gain * one(*cut)
    return gain


def scatter_about(stream_key, extent, scale, most, split=(), kind=jnp.bfloat16):
    drawn = scale * jax.random.normal(stream_key, extent, jnp.float32)
    if split:
        drawn = drawn * level_of(stream_key, extent, split, -0.22, 0.18)
    return jnp.clip(drawn, -most, most).astype(kind)


def gaussian_with(rng, extent, width, limit, pieces, heavy, held_as=jnp.bfloat16):
    result = width * jax.random.normal(rng, extent, jnp.float32)
    if pieces:
        result = result * level_of(rng, extent, pieces, -0.22, 0.18)
    return jnp.clip(spiked(result, jax.random.fold_in(rng, 3), *heavy), -limit, limit).astype(held_as)


def setup_inputs(seed: int = 0) -> dict:
    splits = jax.random.split(jax.random.key(seed), 10)
    image_cache = draw_image_cache(jax.random.fold_in(splits[9], 71), 0)
    text_cache = draw_text_cache(jax.random.fold_in(splits[9], 71), 0)
    labels = jax.random.permutation(splits[2], B).astype(jnp.int32)
    layer_input = gaussian_with(splits[3], (B, W), 1.0, 16.0, ((0, 64),), (0, 1, 64, 4.0))
    ln1_gain = jnp.clip(1.0 + 0.15 * jax.random.normal(splits[4], (W,), jnp.float32), 0.25, 1.75)
    ln2_gain = jnp.clip(1.0 + 0.15 * jax.random.normal(splits[5], (W,), jnp.float32), 0.25, 1.75)
    w_up = scatter_about(splits[6], (W, FF), W ** -0.5, 0.15625, ((1, 2),))
    w_down = scatter_about(splits[7], (W, FF), FF ** -0.5, 0.09375, ((1, 2),))
    proj = scatter_about(splits[8], (W, E), W ** -0.5, 0.15625)
    return dict(image_cache=image_cache, text_cache=text_cache, labels=labels, layer_input=layer_input, ln1_gain=ln1_gain, ln2_gain=ln2_gain, w_up=w_up, w_down=w_down, proj=proj)


logit_scale = 100.0

def unit_rows(values):
    floats = values.astype(jnp.float32)
    inverse = lax.rsqrt(lax.optimization_barrier(jnp.sum(floats * floats, axis=1, keepdims=True)) + 1e-06)
    return (floats * inverse, inverse)

def unit_back(normed, inverse, grad):
    return inverse * (grad - normed * lax.optimization_barrier(jnp.sum(grad * normed, axis=1, keepdims=True)))

def layer_norm(values):
    center = values - lax.optimization_barrier(jnp.mean(values, axis=1, keepdims=True))
    scale_inv = lax.rsqrt(lax.optimization_barrier(jnp.mean(center * center, axis=1, keepdims=True)) + 1e-05)
    return (center * scale_inv, scale_inv)

def norm_back(grad, normed, scale_inv):
    return scale_inv * (grad - lax.optimization_barrier(jnp.mean(grad, axis=1, keepdims=True)) - normed * lax.optimization_barrier(jnp.mean(grad * normed, axis=1, keepdims=True)))

def gelu_slope(values):
    return 0.5 * (1.0 + lax.erf(values * 0.7071067811865476)) + values * jnp.exp(-0.5 * values * values) * 0.3989422804014327

def log_total(logits, axis):
    peak = lax.optimization_barrier(jnp.max(logits, axis=axis, keepdims=True))
    return jnp.squeeze(peak, axis) + jnp.log(lax.optimization_barrier(jnp.sum(jnp.exp(logits - peak), axis=axis)))

def reference(image_cache, text_cache, labels, layer_input, ln1_gain, ln2_gain, w_up, w_down, proj):
    img_norm, img_inv = unit_rows(image_cache)
    txt_norm, txt_inv = unit_rows(text_cache)
    img_unit = img_norm.astype(jnp.bfloat16)
    txt_unit = txt_norm.astype(jnp.bfloat16)
    block = math.gcd(B, 512)
    count = B // block
    index_all = jnp.arange(B, dtype=jnp.int32)

    def row_pass(piece):
        return log_total(logit_scale * jnp.dot(piece, txt_unit.T, preferred_element_type=jnp.float32), 1)

    def col_pass(piece):
        return log_total(logit_scale * jnp.dot(piece, img_unit.T, preferred_element_type=jnp.float32), 1)
    row_lse = lax.map(row_pass, img_unit.reshape(count, block, E)).reshape(B)
    col_lse = lax.map(col_pass, txt_unit.reshape(count, block, E)).reshape(B)

    def img_side(args):
        piece, piece_labels, piece_lse = args
        logits = logit_scale * jnp.dot(piece, txt_unit.T, preferred_element_type=jnp.float32)
        match = (piece_labels[:, None] == index_all[None, :]).astype(jnp.float32)
        grad = 0.5 * (jnp.exp(logits - piece_lse[:, None]) + jnp.exp(logits - col_lse[None, :])) - match
        return logit_scale * jnp.dot(grad.astype(jnp.bfloat16), txt_unit, preferred_element_type=jnp.float32)

    def txt_side(args):
        piece, piece_index, piece_lse = args
        logits = logit_scale * jnp.dot(piece, img_unit.T, preferred_element_type=jnp.float32)
        match = (piece_index[:, None] == labels[None, :]).astype(jnp.float32)
        grad = 0.5 * (jnp.exp(logits - row_lse[None, :]) + jnp.exp(logits - piece_lse[:, None])) - match
        return logit_scale * jnp.dot(grad.astype(jnp.bfloat16), img_unit, preferred_element_type=jnp.float32)
    img_unit_grad = lax.map(img_side, (img_unit.reshape(count, block, E), labels.reshape(count, block), row_lse.reshape(count, block))).reshape(B, E)
    txt_unit_grad = lax.map(txt_side, (txt_unit.reshape(count, block, E), index_all.reshape(count, block), col_lse.reshape(count, block))).reshape(B, E)
    image_grad = unit_back(img_norm, img_inv, img_unit_grad)
    text_grad = unit_back(txt_norm, txt_inv, txt_unit_grad).astype(jnp.bfloat16)
    inputs = layer_input.astype(jnp.float32)
    normed_in, inv_in = layer_norm(inputs)
    mlp_in = (normed_in * ln1_gain).astype(jnp.bfloat16)
    pre = jnp.dot(mlp_in, w_up, preferred_element_type=jnp.float32)
    act = jax.nn.gelu(pre, approximate=False).astype(jnp.bfloat16)
    resid = inputs + jnp.dot(act, w_down.T, preferred_element_type=jnp.float32)
    normed_out, inv_out = layer_norm(resid)
    pooled = (normed_out * ln2_gain).astype(jnp.bfloat16)
    cotangent = image_grad.astype(jnp.bfloat16)
    pooled_grad = jnp.dot(cotangent, proj.T, preferred_element_type=jnp.float32)
    resid_grad = norm_back(pooled_grad * ln2_gain, normed_out, inv_out)
    resid_cot = resid_grad.astype(jnp.bfloat16)
    pre_grad = (jnp.dot(resid_cot, w_down, preferred_element_type=jnp.float32) * gelu_slope(pre)).astype(jnp.bfloat16)
    mlp_in_grad = jnp.dot(pre_grad, w_up.T, preferred_element_type=jnp.float32)
    input_grad = (resid_grad + norm_back(mlp_in_grad * ln1_gain, normed_in, inv_in)).astype(jnp.bfloat16)
    up_grad = jnp.dot(mlp_in.T, pre_grad, preferred_element_type=jnp.float32)
    proj_grad = jnp.dot(pooled.T, cotangent, preferred_element_type=jnp.float32)
    return (text_grad, input_grad, up_grad, proj_grad)
```

```python
import jax
import jax.numpy as jnp
from jax import lax
from jax.experimental import pallas as pl
from jax.experimental.pallas import tpu as pltpu
from jax.sharding import PartitionSpec as P

logit_scale = 100.0
MESH = pl.DeviceIdType.MESH
NX, NYL, NZ, NC = 4, 2, 4, 2
bf16 = jnp.bfloat16
f32 = jnp.float32


def dp_of(x, yl, z, c):
    return ((x * NYL + yl) * NZ + z) * NC + c


def coords():
    d = lax.axis_index("dp")
    c = d % NC
    z = (d // NC) % NZ
    yl = (d // (NC * NZ)) % NYL
    x = d // (NC * NZ * NYL)
    return x, yl, z, c, lax.axis_index("tensor")


def barrier(peers):
    sem = pltpu.get_barrier_semaphore()
    for peer in peers:
        pl.semaphore_signal(sem, inc=1, device_id=peer, device_id_type=MESH)
    pl.semaphore_wait(sem, len(peers))


class Comm:
    def __init__(self, send_sem, recv_sem):
        self.send_sem, self.recv_sem, self.n = send_sem, recv_sem, 0

    def send(self, src, dst, dev):
        i = self.n
        self.n += 1
        copy = pltpu.make_async_remote_copy(
            src_ref=src,
            dst_ref=dst,
            send_sem=self.send_sem.at[i],
            recv_sem=self.recv_sem.at[i],
            device_id=dev,
            device_id_type=MESH,
        )
        copy.start()
        return copy


def comm_call(kernel, out_shapes, in_spaces, out_spaces, scratch, n_sems, n_local, cid, *args):
    return pl.pallas_call(
        kernel,
        out_shape=out_shapes,
        in_specs=[pl.BlockSpec(memory_space=s) for s in in_spaces],
        out_specs=[pl.BlockSpec(memory_space=s) for s in out_spaces],
        scratch_shapes=list(scratch)
        + [
            pltpu.SemaphoreType.DMA((n_sems,)),
            pltpu.SemaphoreType.DMA((n_sems,)),
            pltpu.SemaphoreType.DMA((n_local,)),
        ],
        compiler_params=pltpu.CompilerParams(
            collective_id=cid, has_side_effects=True, vmem_limit_bytes=40 * 1024 * 1024
        ),
    )(*args)


def z_peers(x, yl, z, c, t):
    return [(dp_of(x, yl, (z + k) % NZ, c), t) for k in range(1, NZ)]


def xy_offsets():
    return [(kx, ky) for kx in range(NX) for ky in range(NYL) if (kx, ky) != (0, 0)]


def xy_peers(x, yl, z, c, t):
    return [(dp_of((x + kx) % NX, (yl + ky) % NYL, z, c), t) for kx, ky in xy_offsets()]


def gather_kernel(img, txt, lab, mlp, res, img_all, txt_all, lab_all, mlp_all, res_in, ss, rs, ls):
    x, yl, z, c, t = coords()
    sib = (dp_of(x, yl, z, 1 - c), t)
    mate = (lax.axis_index("dp"), 1 - t)
    zp, xp = z_peers(x, yl, z, c, t), xy_peers(x, yl, z, c, t)
    barrier([sib, mate] + zp + xp)
    comm = Comm(ss, rs)
    own = [
        pltpu.make_async_copy(img, img_all.at[z], ls.at[0]),
        pltpu.make_async_copy(txt, txt_all.at[c, x * NYL + yl], ls.at[1]),
        pltpu.make_async_copy(lab, lab_all.at[z], ls.at[2]),
        pltpu.make_async_copy(mlp, mlp_all.at[z * NC + c], ls.at[3]),
    ]
    for copy in own:
        copy.start()
    img_sends = [comm.send(img, img_all.at[z], p) for p in zp]
    txt_sends = [comm.send(txt, txt_all.at[c, x * NYL + yl], p) for p in xp]
    rest = [comm.send(lab, lab_all.at[z], p) for p in zp]
    rest.append(comm.send(txt, txt_all.at[c, x * NYL + yl], sib))
    rest.append(comm.send(res, res_in, mate))
    mlp_sends = [comm.send(mlp, mlp_all.at[z * NC + c], p) for p in zp]
    rest.append(comm.send(mlp, mlp_all.at[z * NC + c], sib))
    for (kx, ky), copy in zip(xy_offsets(), txt_sends):
        copy.wait_recv()
        slot = ((x + NX - kx) % NX) * NYL + (yl + ky) % NYL
        rest.append(comm.send(txt_all.at[c, slot], txt_all.at[c, slot], sib))
    for k, copy in zip(range(1, NZ), mlp_sends):
        copy.wait_recv()
        slot = ((z + NZ - k) % NZ) * NC + c
        rest.append(comm.send(mlp_all.at[slot], mlp_all.at[slot], sib))
    for copy in img_sends + rest:
        copy.wait()
    for copy in txt_sends + mlp_sends:
        copy.wait_send()
    for copy in own:
        copy.wait()


def stats_kernel(rows, cols, rows_all, cols_all, ss, rs, ls):
    x, yl, z, c, t = coords()
    row_peers = [
        (dp_of(x, yl, (z + k) % NZ, c), (t + j) % 2) for k in range(NZ) for j in range(2) if k or j
    ]
    col_peers = [
        (dp_of((x + kx) % NX, (yl + ky) % NYL, z, (c + kc) % NC), t)
        for kx in range(NX)
        for ky in range(NYL)
        for kc in range(NC)
        if kx or ky or kc
    ]
    barrier(row_peers + col_peers)
    comm = Comm(ss, rs)
    sends = [comm.send(rows, rows_all.at[z * 2 + t], p) for p in row_peers]
    mine = (x * NYL + yl) * NC + c
    sends += [comm.send(cols, cols_all.at[mine], p) for p in col_peers]
    rows_all[z * 2 + t] = rows[...]
    cols_all[mine] = cols[...]
    for copy in sends:
        copy.wait()


def reduce_kernel(
    pimg, ptxt, pooled, img_two, txt_sum, pooled_all, img_in, sib_in, txt_out, txt_in, ss, rs, ls
):
    x, yl, z, c, t = coords()
    sib = (dp_of(x, yl, z, 1 - c), t)
    mate = (lax.axis_index("dp"), 1 - t)
    zp, xp = z_peers(x, yl, z, c, t), xy_peers(x, yl, z, c, t)
    barrier([sib, mate] + zp + xp)
    comm = Comm(ss, rs)
    first = comm.send(ptxt.at[1 - c], sib_in, sib)
    img_sends = [
        comm.send(pimg.at[(z + k) % NZ], img_in.at[k - 1], p) for k, p in zip(range(1, NZ), zp)
    ]
    own = pltpu.make_async_copy(pooled, pooled_all.at[z * NC + c], ls.at[0])
    own.start()
    first.wait()
    txt_sends = []
    for i, ((kx, ky), p) in enumerate(zip(xy_offsets(), xp)):
        slot = ((x + kx) % NX) * NYL + (yl + ky) % NYL
        txt_out[i] = (ptxt[c, slot].astype(f32) + sib_in[slot].astype(f32)).astype(bf16)
        txt_sends.append(comm.send(txt_out.at[i], txt_in.at[i], p))
    pooled_sends = [comm.send(pooled, pooled_all.at[z * NC + c], p) for p in zp]
    rest = [comm.send(pooled, pooled_all.at[z * NC + c], sib)]
    for copy in img_sends:
        copy.wait()
    total = pimg[z].astype(f32)
    for k in range(NZ - 1):
        total = total + img_in[k].astype(f32)
    img_two[0] = total.astype(bf16)
    rest.append(comm.send(img_two.at[0], img_two.at[1], mate))
    mine = x * NYL + yl
    total = ptxt[c, mine].astype(f32) + sib_in[mine].astype(f32)
    for i, copy in enumerate(txt_sends):
        copy.wait()
        total = total + txt_in[i].astype(f32)
    txt_sum[...] = total
    for k, copy in zip(range(1, NZ), pooled_sends):
        copy.wait_recv()
        slot = ((z + NZ - k) % NZ) * NC + c
        rest.append(comm.send(pooled_all.at[slot], pooled_all.at[slot], sib))
    for copy in pooled_sends:
        copy.wait_send()
    for copy in rest:
        copy.wait()
    own.wait()


def zc_offsets():
    return [(kz, kc) for kz in range(NZ) for kc in range(NC) if (kz, kc) != (0, 0)]


def zc_peers(x, yl, z, c, t):
    return [(dp_of(x, yl, (z + kz) % NZ, (c + kc) % NC), t) for kz, kc in zc_offsets()]


def swap_kernel(pre, cot, mg, txt, pre_all, cot_all, mg_in, txt_in, ss, rs, ls):
    x, yl, z, c, t = coords()
    mate = (lax.axis_index("dp"), 1 - t)
    zc = zc_peers(x, yl, z, c, t)
    barrier([mate] + zc)
    comm = Comm(ss, rs)
    mine = z * NC + c
    sends = [comm.send(mg, mg_in, mate)]
    for (kz, kc), p in zip(zc_offsets(), zc):
        slot = ((z + kz) % NZ) * NC + (c + kc) % NC
        sends.append(comm.send(pre.at[slot], pre_all.at[mine], p))
        sends.append(comm.send(cot.at[slot], cot_all.at[mine], p))
    sends.append(comm.send(txt, txt_in, mate))
    own = [
        pltpu.make_async_copy(pre.at[mine], pre_all.at[mine], ls.at[0]),
        pltpu.make_async_copy(cot.at[mine], cot_all.at[mine], ls.at[1]),
    ]
    for copy in own:
        copy.start()
    for copy in sends + own:
        copy.wait()


def weight_kernel(grad, out, x_in, y_out, y_in, z_out, ss, rs, ls):
    x, yl, z, c, t = coords()
    xs = [(dp_of((x + k) % NX, yl, z, c), t) for k in range(1, NX)]
    ys = (dp_of(x, 1 - yl, z, c), t)
    zc = zc_peers(x, yl, z, c, t)
    barrier(xs + [ys] + zc)
    comm = Comm(ss, rs)
    sends = [comm.send(grad.at[(x + k) % NX], x_in.at[k - 1], p) for k, p in zip(range(1, NX), xs)]
    for copy in sends:
        copy.wait()
    half = grad.shape[1] // 2

    def x_sum(side):
        rows = pl.ds(pl.multiple_of(side * half, half), half)
        total = grad[x, rows].astype(f32)
        for k in range(NX - 1):
            total = total + x_in[k, rows].astype(f32)
        return total

    y_out[...] = x_sum(1 - yl).astype(bf16)
    sent = comm.send(y_out, y_in, ys)
    z_out[...] = x_sum(yl)
    sent.wait()
    total = z_out[...] + y_in[...].astype(f32)
    mine = z * NC + c
    return total, mine, comm, zc


def weight_body(grad, out, x_in, y_out, y_in, z_out, blocks, ss, rs, ls):
    total, mine, comm, zc = weight_kernel(grad, out, x_in, y_out, y_in, z_out, ss, rs, ls)
    x, yl, z, c, t = coords()
    z_out[...] = total
    for i in range(NZ * NC):
        blocks[i, 0:26] = z_out[26 * i : 26 * i + 26]
        blocks[i, 26:32] = jnp.zeros((6, z_out.shape[1]), f32)
    sends = []
    for (kz, kc), p in zip(zc_offsets(), zc):
        slot = ((z + kz) % NZ) * NC + (c + kc) % NC
        sends.append(comm.send(blocks.at[slot], out.at[mine], p))
    out[mine] = blocks[mine]
    for copy in sends:
        copy.wait()


def unit_rows(values):
    floats = values.astype(jnp.float32)
    inverse = lax.rsqrt(jnp.sum(floats * floats, axis=1, keepdims=True) + 1e-06)
    return (floats * inverse, inverse)


def unit_back(normed, inverse, grad):
    return inverse * (grad - normed * jnp.sum(grad * normed, axis=1, keepdims=True))


def layer_norm(values):
    center = values - jnp.mean(values, axis=1, keepdims=True)
    scale_inv = lax.rsqrt(jnp.mean(center * center, axis=1, keepdims=True) + 1e-05)
    return (center * scale_inv, scale_inv)


def norm_back(grad, normed, scale_inv):
    return scale_inv * (
        grad
        - jnp.mean(grad, axis=1, keepdims=True)
        - normed * jnp.mean(grad * normed, axis=1, keepdims=True)
    )


def gelu_slope(values):
    return (
        0.5 * (1.0 + lax.erf(values * 0.7071067811865476))
        + values * jnp.exp(-0.5 * values * values) * 0.3989422804014327
    )


def contract_last(left, right):
    return lax.dot_general(
        left, right, (((1,), (1,)), ((), ())), preferred_element_type=jnp.float32
    )


def contract_first(left, right):
    return lax.dot_general(
        left, right, (((0,), (0,)), ((), ())), preferred_element_type=jnp.float32
    )


def shaped(shape, dtype):
    return jax.ShapeDtypeStruct(shape, dtype)


def local(image_cache, text_cache, labels, layer_input, ln1_gain, ln2_gain, w_up, w_down, proj):
    x, yl, z, c, t = coords()
    rows, embed = image_cache.shape
    width = layer_input.shape[1]
    half = rows // 2
    hidden = w_up.shape[1]
    hid = hidden // 8
    eh = embed // 2
    ec = eh // 8
    anys, vmem = pl.ANY, pltpu.VMEM

    img_norm, img_inv = unit_rows(image_cache)
    img_unit = img_norm.astype(bf16)
    txt_half = lax.dynamic_slice_in_dim(text_cache, t * half, half, 0)
    txt_norm, txt_inv = unit_rows(txt_half)
    txt_unit = txt_norm.astype(bf16)
    inputs = layer_input.astype(f32)
    normed_in, inv_in = layer_norm(inputs)
    mlp_in = (normed_in * ln1_gain).astype(bf16)
    pre = jnp.dot(mlp_in, w_up, preferred_element_type=f32)
    act = jax.nn.gelu(pre, approximate=False).astype(bf16)
    res_part = contract_last(act, w_down).astype(bf16)

    img_all, txt_all, lab_all, mlp_all, res_in = comm_call(
        gather_kernel,
        [
            shaped((NZ, rows, embed), bf16),
            shaped((NC, NX * NYL, half, embed), bf16),
            shaped((NZ, 1, rows), jnp.int32),
            shaped((NZ * NC, rows, width), bf16),
            shaped((rows, width), bf16),
        ],
        [anys] * 5,
        [anys] * 5,
        [],
        40,
        4,
        1,
        img_unit,
        txt_unit,
        labels.reshape(1, rows),
        mlp_in,
        res_part,
    )
    resid = inputs + (res_part.astype(f32) + res_in.astype(f32))
    normed_out, inv_out = layer_norm(resid)
    pooled = (normed_out * ln2_gain).astype(bf16)

    images = img_all.reshape(NZ * rows, embed)
    texts = txt_all.reshape(16 * half, embed)
    logits = logit_scale * contract_last(images, texts)
    row_peak = jnp.max(logits, axis=1)
    row_total = jnp.sum(jnp.exp(logits - row_peak[:, None]), axis=1)
    col_peak = jnp.max(logits, axis=0)
    col_total = jnp.sum(jnp.exp(logits - col_peak[None, :]), axis=0)
    n_row, n_col = row_peak.shape[0], col_peak.shape[0]
    row_stats = jnp.concatenate([row_peak, row_total]).reshape(2 * n_row // 128, 128)
    col_stats = jnp.concatenate([col_peak, col_total]).reshape(2 * n_col // 128, 128)
    rows_all, cols_all = comm_call(
        stats_kernel,
        [shaped((8,) + row_stats.shape, f32), shaped((16,) + col_stats.shape, f32)],
        [vmem] * 2,
        [vmem] * 2,
        [],
        22,
        1,
        2,
        row_stats,
        col_stats,
    )

    def total_of(stats, n):
        parts = stats.reshape(-1, 2, n)
        peak = jnp.max(parts[:, 0], axis=0)
        return peak + jnp.log(jnp.sum(parts[:, 1] * jnp.exp(parts[:, 0] - peak[None]), axis=0))

    row_lse = total_of(rows_all, n_row)
    col_lse = total_of(cols_all, n_col)
    place = jnp.arange(n_col, dtype=jnp.int32)
    slot = place // half
    text_index = (
        ((slot % (NX * NYL)) * NZ + z) * NC + slot // (NX * NYL)
    ) * rows + t * half + place % half
    match = (lab_all.reshape(n_row)[:, None] == text_index[None, :]).astype(f32)
    grad = (
        0.5 * (jnp.exp(logits - row_lse[:, None]) + jnp.exp(logits - col_lse[None, :])) - match
    ).astype(bf16)
    part_img = (logit_scale * jnp.dot(grad, texts, preferred_element_type=f32)).astype(bf16)
    part_txt = (logit_scale * contract_first(grad, images)).astype(bf16)

    img_two, txt_sum, pooled_all = comm_call(
        reduce_kernel,
        [
            shaped((2, rows, embed), bf16),
            shaped((half, embed), f32),
            shaped((NZ * NC, rows, width), bf16),
        ],
        [vmem, vmem, anys],
        [vmem, vmem, anys],
        [
            pltpu.VMEM((NZ - 1, rows, embed), bf16),
            pltpu.VMEM((NX * NYL, half, embed), bf16),
            pltpu.VMEM((NX * NYL - 1, half, embed), bf16),
            pltpu.VMEM((NX * NYL - 1, half, embed), bf16),
        ],
        24,
        1,
        3,
        part_img.reshape(NZ, rows, embed),
        part_txt.reshape(NC, NX * NYL, half, embed),
        pooled,
    )
    img_unit_grad = img_two[0].astype(f32) + img_two[1].astype(f32)
    image_grad = unit_back(img_norm, img_inv, img_unit_grad)
    text_half = unit_back(txt_norm, txt_inv, txt_sum).astype(bf16)
    cotangent = image_grad.astype(bf16)
    pooled_grad = contract_last(cotangent, proj)
    resid_grad = norm_back(pooled_grad * ln2_gain, normed_out, inv_out)
    resid_cot = resid_grad.astype(bf16)
    pre_grad = (jnp.dot(resid_cot, w_down, preferred_element_type=f32) * gelu_slope(pre)).astype(
        bf16
    )
    mg_part = contract_last(pre_grad, w_up).astype(bf16)
    cot_half = lax.dynamic_slice_in_dim(cotangent, t * eh, eh, 1)

    pre_all, cot_all, mg_in, txt_in = comm_call(
        swap_kernel,
        [
            shaped((8, rows, hid), bf16),
            shaped((8, ec, rows), bf16),
            shaped((rows, width), bf16),
            shaped((half, embed), bf16),
        ],
        [anys] * 4,
        [anys] * 4,
        [],
        16,
        2,
        4,
        pre_grad.reshape(rows, 8, hid).transpose(1, 0, 2),
        cot_half.T.reshape(8, ec, rows),
        mg_part,
        text_half,
    )
    mlp_in_grad = mg_part.astype(f32) + mg_in.astype(f32)
    input_grad = (resid_grad + norm_back(mlp_in_grad * ln1_gain, normed_in, inv_in)).astype(bf16)
    text_grad = jnp.where(
        t == 0,
        jnp.concatenate([text_half, txt_in], axis=0),
        jnp.concatenate([txt_in, text_half], axis=0),
    )
    up_part = contract_first(mlp_all.reshape(8 * rows, width), pre_all.reshape(8 * rows, hid))
    cots = jnp.pad(cot_all, ((0, 0), (0, 128 - ec), (0, 0)))
    proj_part = lax.dot_general(
        pooled_all.reshape(8 * rows, width),
        cots.transpose(0, 2, 1).reshape(8 * rows, 128),
        (((0,), (0,)), ((), ())),
        preferred_element_type=f32,
    )
    both = jnp.concatenate([up_part, proj_part], axis=1).astype(bf16)
    cols = hid + 128
    quarter = width // NX
    (summed,) = comm_call(
        weight_body,
        [shaped((8, 32, cols), f32)],
        [vmem],
        [vmem],
        [
            pltpu.VMEM((NX - 1, quarter, cols), bf16),
            pltpu.VMEM((quarter // 2, cols), bf16),
            pltpu.VMEM((quarter // 2, cols), bf16),
            pltpu.VMEM((quarter // 2, cols), f32),
            pltpu.VMEM((8, 32, cols), f32),
        ],
        12,
        1,
        5,
        both.reshape(NX, quarter, cols),
    )
    share = width // 64
    up_grad = summed[:, :share, :hid].transpose(1, 0, 2).reshape(share, hidden)
    proj_grad = summed[:, :share, hid : hid + ec].transpose(1, 0, 2).reshape(share, eh)
    return (text_grad, input_grad, up_grad, proj_grad)


def solution(mesh):
    in_specs = (
        P("dp", None),
        P("dp", None),
        P("dp"),
        P("dp", None),
        P(),
        P(),
        P(None, "tensor"),
        P(None, "tensor"),
        P(),
    )
    out_specs = (P("dp", None), P("dp", None), P("dp", "tensor"), P("dp", "tensor"))
    return jax.shard_map(local, mesh=mesh, in_specs=in_specs, out_specs=out_specs, check_vma=False)
```

```python
import jax
import jax.numpy as jnp
from jax import lax
from jax.experimental import pallas as pl
from jax.experimental.pallas import tpu as pltpu
from jax.sharding import PartitionSpec as P

logit_scale = 100.0
MESH = pl.DeviceIdType.MESH
NX, NYL, NZ, NC = 4, 2, 4, 2
bf16 = jnp.bfloat16
f32 = jnp.float32
VMEM_LIMIT = 60 * 1024 * 1024


def dp_of(x, yl, z, c):
    return ((x * NYL + yl) * NZ + z) * NC + c


def coords():
    d = lax.axis_index("dp")
    c = d % NC
    z = (d // NC) % NZ
    yl = (d // (NC * NZ)) % NYL
    x = d // (NC * NZ * NYL)
    return x, yl, z, c, lax.axis_index("tensor")


class Comm:
    def __init__(self, send_sem, recv_sem):
        self.send_sem, self.recv_sem, self.n = send_sem, recv_sem, 0

    def send(self, src, dst, dev):
        i = self.n
        self.n += 1
        copy = pltpu.make_async_remote_copy(
            src_ref=src,
            dst_ref=dst,
            send_sem=self.send_sem.at[i],
            recv_sem=self.recv_sem.at[i],
            device_id=dev,
            device_id_type=MESH,
        )
        copy.start()
        return copy


def z_offsets():
    return list(range(1, NZ))


def zc_offsets():
    return [(kz, kc) for kz in range(NZ) for kc in range(NC) if (kz, kc) != (0, 0)]


def unit_rows(values):
    floats = values.astype(f32)
    inverse = lax.rsqrt(jnp.sum(floats * floats, axis=1, keepdims=True) + 1e-06)
    return (floats * inverse, inverse)


def unit_back(normed, inverse, grad):
    return inverse * (grad - normed * jnp.sum(grad * normed, axis=1, keepdims=True))


def layer_norm(values):
    center = values - jnp.mean(values, axis=1, keepdims=True)
    scale_inv = lax.rsqrt(jnp.mean(center * center, axis=1, keepdims=True) + 1e-05)
    return (center * scale_inv, scale_inv)


def norm_back(grad, normed, scale_inv):
    return scale_inv * (
        grad
        - jnp.mean(grad, axis=1, keepdims=True)
        - normed * jnp.mean(grad * normed, axis=1, keepdims=True)
    )


def contract_last(left, right):
    return lax.dot_general(left, right, (((1,), (1,)), ((), ())), preferred_element_type=f32)


def dot(left, right):
    return jnp.dot(left, right, preferred_element_type=f32)


def at(index, size):
    return pl.ds(pl.multiple_of(index * size, size), size)


def chunks(total, size):
    return [(i, min(size, total - i)) for i in range(0, total, size)]


def to_column(row, n):
    return jnp.transpose(jnp.broadcast_to(row, (128, n)))[:, 0:1]


def to_row(column, n):
    return jnp.transpose(jnp.broadcast_to(column, (n, 128)))[0:1]


def merged_lse(parts, count):
    peak = parts[0, 0:1]
    for i in range(1, count):
        peak = jnp.maximum(peak, parts[i, 0:1])
    total = jnp.zeros_like(peak)
    for i in range(count):
        total = total + parts[i, 1:2] * jnp.exp(parts[i, 0:1] - peak)
    return peak + jnp.log(total)


def body(
    img_ref, txt_ref, lab_ref, lin_ref, g1_ref, g2_ref, up_hbm, down_hbm, proj_hbm,
    text_out, input_out, up_out, proj_out,
    w_up, w_down, w_proj, img_all, txt_all, lab_all, mlp_t, pooled_t, act, slope,
    res_out, res_in, n_in, n_out, logits, row_st, col_st, rows_all, cols_all,
    grad, grad_t, pimg, img_in, img_sum, img_mate, ptxt, sib_in, txo, txi, tyo, tyi, tsum,
    rgrad, cot_t, cot_all, pre_out, pre_all, mg_out, mg_in,
    wp, wu, wpi, wui, wyo, wyi, wsum, wblk_u, wblk_p,
    ss, rs, ls,
):
    x, yl, z, c, t = coords()
    me = lax.axis_index("dp")
    rows, embed = img_ref.shape
    width = lin_ref.shape[1]
    half = rows // 2
    hidden = up_hbm.shape[1]
    hid = hidden // 8
    eh = embed // 2
    ec = eh // 8
    sib, mate, ynb = (dp_of(x, yl, z, 1 - c), t), (me, 1 - t), (dp_of(x, 1 - yl, z, c), t)
    zp = [(dp_of(x, yl, (z + k) % NZ, c), t) for k in range(1, NZ)]
    xp = [(dp_of((x + k) % NX, yl, z, c), t) for k in range(1, NX)]
    zc = [(dp_of(x, yl, (z + kz) % NZ, (c + kc) % NC), t) for kz, kc in zc_offsets()]
    row_peers = [
        (dp_of(x, yl, (z + k) % NZ, c), (t + j) % 2) for k in range(NZ) for j in range(2) if k or j
    ]
    col_peers = [
        (dp_of((x + kx) % NX, (yl + ky) % NYL, z, (c + kc) % NC), t)
        for kx in range(NX)
        for ky in range(NYL)
        for kc in range(NC)
        if kx or ky or kc
    ]
    cross = [p for (kz, kc), p in zip(zc_offsets(), zc) if kz and kc]
    greet = row_peers + col_peers + cross
    entry = pltpu.get_barrier_semaphore()
    for peer in greet:
        pl.semaphore_signal(entry, inc=1, device_id=peer, device_id_type=MESH)
    loads = [
        pltpu.make_async_copy(up_hbm, w_up, ls.at[0]),
        pltpu.make_async_copy(down_hbm, w_down, ls.at[1]),
        pltpu.make_async_copy(proj_hbm, w_proj, ls.at[2]),
    ]
    for copy in loads:
        copy.start()
    my_slot = c * 8 + x * NYL + yl
    img_unit, _ = unit_rows(img_ref[...])
    img_all[at(z, rows)] = img_unit.astype(bf16)
    txt_unit, _ = unit_rows(txt_ref[at(t, half)])
    txt_all[at(my_slot, half)] = txt_unit.astype(bf16)
    lab_all[z] = lab_ref[...]
    cot_all[ec:] = jnp.zeros((128 - ec, 8 * rows), bf16)
    pl.semaphore_wait(entry, len(greet))

    comm = Comm(ss, rs)
    send = comm.send

    def same(ref, index, size, dev):
        return send(ref.at[at(index, size)], ref.at[at(index, size)], dev)

    t_y = same(txt_all, my_slot, half, ynb)
    t_x = [same(txt_all, my_slot, half, p) for p in xp]
    i_z = [same(img_all, z, rows, p) for p in zp]
    l_z = [send(lab_all.at[z], lab_all.at[z], p) for p in zp]
    t_s = [same(txt_all, my_slot, half, sib)]

    inputs = lin_ref[...].astype(f32)
    normed_in, inv_in = layer_norm(inputs)
    n_in[...] = normed_in
    mlp_f = n_in[...] * g1_ref[...]
    mlp_in = mlp_f.astype(bf16)
    my_zc = z * NC + c
    for i, n in chunks(width, 128):
        mlp_t[i : i + n, at(my_zc, 128)] = jnp.transpose(
            n_in[:, i : i + n] * g1_ref[:, i : i + n]
        ).astype(bf16)
    t_y.wait_recv()
    other = c * 8 + x * NYL + (1 - yl)
    f_x = [same(txt_all, other, half, p) for p in xp]
    t_s.append(same(txt_all, other, half, sib))

    loads[0].wait()

    def up_tile(i, _):
        cols = at(i, 256)
        pre = dot(mlp_in, w_up[:, cols])
        phi = 0.5 * (1.0 + lax.erf(pre * 0.7071067811865476))
        act[:, cols] = (pre * phi).astype(bf16)
        slope[:, cols] = phi + pre * jnp.exp(-0.5 * pre * pre) * 0.3989422804014327
        return _

    lax.fori_loop(0, hidden // 256, up_tile, 0)
    for k, copy in zip(range(1, NX), t_x):
        copy.wait_recv()
        t_s.append(same(txt_all, c * 8 + ((x + NX - k) % NX) * NYL + yl, half, sib))
    loads[1].wait()
    acts = act[...]
    for i, n in chunks(width, 256):
        res_out[:, i : i + n] = contract_last(acts, w_down[i : i + n]).astype(bf16)
    res_c = send(res_out, res_in, mate)
    for k, copy in zip(range(1, NX), f_x):
        copy.wait_recv()
        t_s.append(same(txt_all, c * 8 + ((x + NX - k) % NX) * NYL + (1 - yl), half, sib))
    for copy in i_z + l_z:
        copy.wait()
    m_z = [
        send(mlp_t.at[:, at(my_zc, 128)], mlp_t.at[:, at(my_zc, 128)], p) for p in zp
    ]
    for copy in t_s:
        copy.wait()
    t_y.wait_send()
    for copy in t_x + f_x:
        copy.wait_send()

    n_row, n_col = img_all.shape[0], txt_all.shape[0]
    tile = 256

    def logit_tile(i, peak):
        tile_logits = logit_scale * contract_last(img_all[...], txt_all[at(i, tile)])
        logits[:, at(i, tile)] = tile_logits
        return jnp.maximum(peak, jnp.max(tile_logits, axis=1, keepdims=True))

    row_peak = lax.fori_loop(
        0, n_col // tile, logit_tile, jnp.full((n_row, 1), -jnp.inf, f32)
    )

    def total_tile(i, total):
        cols = at(i, tile)
        part = logits[:, cols]
        col_peak = jnp.max(part, axis=0, keepdims=True)
        col_st[0:1, cols] = col_peak
        col_st[1:2, cols] = jnp.sum(jnp.exp(part - col_peak), axis=0, keepdims=True)
        return total + jnp.sum(jnp.exp(part - row_peak), axis=1, keepdims=True)

    row_total = lax.fori_loop(0, n_col // tile, total_tile, jnp.zeros((n_row, 1), f32))
    my_col, my_row = (x * NYL + yl) * NC + c, z * 2 + t
    stats = [send(col_st, cols_all.at[my_col], p) for p in col_peers]
    row_st[0:1] = to_row(row_peak, n_row)
    row_st[1:2] = to_row(row_total, n_row)
    stats += [send(row_st, rows_all.at[my_row], p) for p in row_peers]
    rows_all[my_row] = row_st[...]
    cols_all[my_col] = col_st[...]

    res_c.wait()
    resid = lin_ref[...].astype(f32) + (res_out[...].astype(f32) + res_in[...].astype(f32))
    normed_out, inv_out = layer_norm(resid)
    n_out[...] = normed_out
    for i, n in chunks(width, 128):
        pooled_t[i : i + n, at(my_zc, 128)] = jnp.transpose(
            n_out[:, i : i + n] * g2_ref[:, i : i + n]
        ).astype(bf16)
    for copy in stats:
        copy.wait()

    row_lse = to_column(merged_lse(rows_all, 8), n_row)
    col_st[0:1] = merged_lse(cols_all, 16)
    label_col = jnp.concatenate(
        [to_column(lab_all[i, 0:1].astype(f32), rows) for i in range(NZ)], axis=0
    )

    def grad_tile(i, _):
        cols = at(i, tile)
        part = logits[:, cols]
        place = i * tile + lax.broadcasted_iota(jnp.int32, (1, tile), 1)
        slot = place // half
        index = (((slot % (NX * NYL)) * NZ + z) * NC + slot // (NX * NYL)) * rows
        index = (index + t * half + place % half).astype(f32)
        value = 0.5 * (jnp.exp(part - row_lse) + jnp.exp(part - col_st[0:1, cols]))
        value = value - jnp.where(label_col == index, 1.0, 0.0)
        grad[:, cols] = value.astype(bf16)
        grad_t[at(i, tile)] = jnp.transpose(value).astype(bf16)
        return _

    lax.fori_loop(0, n_col // tile, grad_tile, 0)

    def img_tile(i, _):
        cols = at(i, 256)
        pimg[:, cols] = (logit_scale * dot(grad[...], txt_all[:, cols])).astype(bf16)
        return _

    lax.fori_loop(0, embed // 256, img_tile, 0)
    r_z = [
        send(pimg.at[at((z + k) % NZ, rows)], img_in.at[k - 1], p)
        for k, p in zip(range(1, NZ), zp)
    ]

    def txt_tile(i, _):
        cols = at(i, 256)
        ptxt[:, cols] = (logit_scale * dot(grad_t[...], img_all[:, cols])).astype(bf16)
        return _

    lax.fori_loop(0, embed // 256, txt_tile, 0)
    side = 8 * half
    to_sib = send(ptxt.at[at(1 - c, side)], sib_in, sib)
    m_s = [send(mlp_t.at[:, at(my_zc, 128)], mlp_t.at[:, at(my_zc, 128)], sib)]
    for k, copy in zip(range(1, NZ), m_z):
        copy.wait_recv()
        cols = at(((z + NZ - k) % NZ) * NC + c, 128)
        m_s.append(send(mlp_t.at[:, cols], mlp_t.at[:, cols], sib))
    to_sib.wait()
    pair = 2 * half

    def chip_sum(index, size):
        mine = ptxt[pl.ds(pl.multiple_of(c * side + index * size, size), size)]
        return mine.astype(f32) + sib_in[at(index, size)].astype(f32)

    x_t = []
    for k, p in zip(range(1, NX), xp):
        txo[k - 1] = chip_sum((x + k) % NX, pair).astype(bf16)
        x_t.append(send(txo.at[k - 1], txi.at[k - 1], p))

    for copy in r_z:
        copy.wait()
    total = pimg[at(z, rows)].astype(f32)
    for k in range(NZ - 1):
        total = total + img_in[k].astype(f32)
    img_sum[...] = total.astype(bf16)
    i_m = send(img_sum, img_mate, mate)
    p_z = [
        send(pooled_t.at[:, at(my_zc, 128)], pooled_t.at[:, at(my_zc, 128)], p) for p in zp
    ]
    p_s = [send(pooled_t.at[:, at(my_zc, 128)], pooled_t.at[:, at(my_zc, 128)], sib)]
    loads[2].wait()
    i_m.wait()
    unit_grad = img_sum[...].astype(f32) + img_mate[...].astype(f32)
    img_norm, img_inv = unit_rows(img_ref[...])
    image_grad = unit_back(img_norm, img_inv, unit_grad)
    cotangent = image_grad.astype(bf16)
    cot_t[...] = jnp.transpose(image_grad).astype(bf16)
    own_cot = cot_t[pl.ds(pl.multiple_of(t * eh + my_zc * ec, ec), ec)]
    cot_all[0:ec, at(my_zc, 128)] = own_cot
    for i, n in chunks(width, 256):
        rgrad[:, i : i + n] = (
            contract_last(cotangent, w_proj[i : i + n]) * g2_ref[:, i : i + n]
        )
    rgrad[...] = norm_back(rgrad[...], n_out[...], inv_out)
    resid_cot = rgrad[...].astype(bf16)
    c_sends, g_sends = [], []
    for (kz, kc), p in zip(zc_offsets() + [(0, 0)], zc + [None]):
        slot = ((z + kz) % NZ) * NC + (c + kc) % NC
        cols = at(slot, hid)
        pre_out[:, cols] = (dot(resid_cot, w_down[:, cols]) * slope[:, cols]).astype(bf16)
        if p is None:
            pre_all[at(my_zc, rows)] = pre_out[:, cols]
        else:
            g_sends.append(send(pre_out.at[:, cols], pre_all.at[at(my_zc, rows)], p))
            block = pl.ds(pl.multiple_of(t * eh + slot * ec, ec), ec)
            c_sends.append(
                send(cot_t.at[block], cot_all.at[0:ec, at(my_zc, 128)], p)
            )
    for k, copy in zip(range(1, NZ), p_z):
        copy.wait_recv()
        cols = at(((z + NZ - k) % NZ) * NC + c, 128)
        p_s.append(send(pooled_t.at[:, cols], pooled_t.at[:, cols], sib))
    pre_grad = pre_out[...]
    for i, n in chunks(width, 256):
        mg_out[:, i : i + n] = contract_last(pre_grad, w_up[i : i + n]).astype(bf16)
    g_m = send(mg_out, mg_in, mate)

    for copy in m_s + g_sends:
        copy.wait()
    quarter = width // NX
    wu_x, wp_x = [], []
    for k in [1, 2, 3, 0]:
        b = (x + k) % NX
        wu[b] = dot(mlp_t[at(b, quarter)], pre_all[...]).astype(bf16)
        if k:
            wu_x.append(send(wu.at[b], wui.at[k - 1], xp[k - 1]))
    for copy in c_sends + p_s:
        copy.wait()
    for k in [1, 2, 3, 0]:
        b = (x + k) % NX
        wp[b] = contract_last(pooled_t[at(b, quarter)], cot_all[...]).astype(bf16)
        if k:
            wp_x.append(send(wp.at[b], wpi.at[k - 1], xp[k - 1]))

    for copy in x_t:
        copy.wait()

    def x_total(part):
        mine = ptxt[pl.ds(pl.multiple_of(c * side + (x * NYL + part) * half, half), half)]
        mine = mine.astype(f32) + sib_in[at(x * NYL + part, half)].astype(f32)
        for k in range(NX - 1):
            mine = mine + txi[k, at(part, half)].astype(f32)
        return mine

    tyo[...] = x_total(1 - yl).astype(bf16)
    y_t = send(tyo, tyi, ynb)
    tsum[...] = x_total(yl)
    y_t.wait()
    txt_norm, txt_inv = unit_rows(txt_ref[at(t, half)])
    text_out[at(t, half)] = unit_back(
        txt_norm, txt_inv, tsum[...] + tyi[...].astype(f32)
    ).astype(bf16)
    t_m = same(text_out, t, half, mate)

    g_m.wait()
    dm = (mg_out[...].astype(f32) + mg_in[...].astype(f32)) * g1_ref[...]
    input_out[...] = (rgrad[...] + norm_back(dm, n_in[...], inv_in)).astype(bf16)

    for copy in wu_x + wp_x:
        copy.wait()
    eighth = quarter // 2

    def w_total(own, got, part):
        block = at(part, eighth)
        total = own[x, block].astype(f32)
        for k in range(NX - 1):
            total = total + got[k, block].astype(f32)
        return total

    wyo[:, 0:hid] = w_total(wu, wui, 1 - yl).astype(bf16)
    wyo[:, hid:] = w_total(wp, wpi, 1 - yl).astype(bf16)
    w_y = send(wyo, wyi, ynb)
    wsum[:, 0:hid] = w_total(wu, wui, yl)
    wsum[:, hid:] = w_total(wp, wpi, yl)
    w_y.wait()
    wsum[...] = wsum[...] + wyi[...].astype(f32)
    share = eighth // 8
    for i in range(8):
        wblk_u[i, 0:share] = wsum[share * i : share * (i + 1), 0:hid]
        wblk_p[i, 0:share] = wsum[share * i : share * (i + 1), hid:]
        wblk_u[i, share:] = jnp.zeros((32 - share, hid), f32)
        wblk_p[i, share:] = jnp.zeros((32 - share, 128), f32)
    last = []
    for (kz, kc), p in zip(zc_offsets(), zc):
        slot = ((z + kz) % NZ) * NC + (c + kc) % NC
        last.append(send(wblk_u.at[slot], up_out.at[:, at(my_zc, hid)], p))
        last.append(send(wblk_p.at[slot], proj_out.at[my_zc], p))
    up_out[:, at(my_zc, hid)] = wblk_u[my_zc]
    proj_out[my_zc] = wblk_p[my_zc]
    for copy in m_z + p_z:
        copy.wait_send()
    t_m.wait()
    for copy in last:
        copy.wait()


def local(image_cache, text_cache, labels, layer_input, ln1_gain, ln2_gain, w_up, w_down, proj):
    rows, embed = image_cache.shape
    width = layer_input.shape[1]
    half = rows // 2
    hidden = w_up.shape[1]
    hid = hidden // 8
    ec = embed // 16
    quarter = width // NX
    share = width // 64
    n_sems = 112
    vm = pltpu.VMEM
    scratch = [
        vm(w_up.shape, bf16),
        vm(w_down.shape, bf16),
        vm(proj.shape, bf16),
        vm((NZ * rows, embed), bf16),
        vm((16 * half, embed), bf16),
        vm((NZ, 8, rows), jnp.int32),
        vm((width, 8 * rows), bf16),
        vm((width, 8 * rows), bf16),
        vm((rows, hidden), bf16),
        vm((rows, hidden), f32),
        vm((rows, width), bf16),
        vm((rows, width), bf16),
        vm((rows, width), f32),
        vm((rows, width), f32),
        vm((NZ * rows, 16 * half), f32),
        vm((2, NZ * rows), f32),
        vm((2, 16 * half), f32),
        vm((8, 2, NZ * rows), f32),
        vm((16, 2, 16 * half), f32),
        vm((NZ * rows, 16 * half), bf16),
        vm((16 * half, NZ * rows), bf16),
        vm((NZ * rows, embed), bf16),
        vm((NZ - 1, rows, embed), bf16),
        vm((rows, embed), bf16),
        vm((rows, embed), bf16),
        vm((16 * half, embed), bf16),
        vm((8 * half, embed), bf16),
        vm((NX - 1, 2 * half, embed), bf16),
        vm((NX - 1, 2 * half, embed), bf16),
        vm((half, embed), bf16),
        vm((half, embed), bf16),
        vm((half, embed), f32),
        vm((rows, width), f32),
        vm((embed, rows), bf16),
        vm((128, 8 * rows), bf16),
        vm((rows, hidden), bf16),
        vm((8 * rows, hid), bf16),
        vm((rows, width), bf16),
        vm((rows, width), bf16),
        vm((NX, quarter, 128), bf16),
        vm((NX, quarter, hid), bf16),
        vm((NX - 1, quarter, 128), bf16),
        vm((NX - 1, quarter, hid), bf16),
        vm((quarter // 2, hid + 128), bf16),
        vm((quarter // 2, hid + 128), bf16),
        vm((quarter // 2, hid + 128), f32),
        vm((8, 32, hid), f32),
        vm((8, 32, 128), f32),
        pltpu.SemaphoreType.DMA((n_sems,)),
        pltpu.SemaphoreType.DMA((n_sems,)),
        pltpu.SemaphoreType.DMA((3,)),
    ]
    on_vmem = pl.BlockSpec(memory_space=pltpu.VMEM)
    anywhere = pl.BlockSpec(memory_space=pl.ANY)
    text_grad, input_grad, up, blocks = pl.pallas_call(
        body,
        name="clip_mlp",
        out_shape=[
            jax.ShapeDtypeStruct((rows, embed), bf16),
            jax.ShapeDtypeStruct((rows, width), bf16),
            jax.ShapeDtypeStruct((32, hidden), f32),
            jax.ShapeDtypeStruct((8, 32, 128), f32),
        ],
        in_specs=[on_vmem] * 6 + [anywhere] * 3,
        out_specs=[on_vmem] * 4,
        scratch_shapes=scratch,
        compiler_params=pltpu.CompilerParams(
            collective_id=1, has_side_effects=True, vmem_limit_bytes=VMEM_LIMIT
        ),
    )(
        image_cache,
        text_cache,
        jnp.broadcast_to(labels[None, :], (8, rows)),
        layer_input,
        ln1_gain[None, :],
        ln2_gain[None, :],
        w_up,
        w_down,
        proj,
    )
    up_grad = up[:share]
    proj_grad = blocks[:, :share, :ec].transpose(1, 0, 2).reshape(share, 8 * ec)
    return (text_grad, input_grad, up_grad, proj_grad)


def solution(mesh):
    in_specs = (
        P("dp", None),
        P("dp", None),
        P("dp"),
        P("dp", None),
        P(),
        P(),
        P(None, "tensor"),
        P(None, "tensor"),
        P(),
    )
    out_specs = (P("dp", None), P("dp", None), P("dp", "tensor"), P("dp", "tensor"))
    return jax.shard_map(local, mesh=mesh, in_specs=in_specs, out_specs=out_specs, check_vma=False)
```

```python
import jax
import jax.numpy as jnp
from jax import lax
from jax.experimental import pallas as pl
from jax.experimental.pallas import tpu as pltpu
from jax.sharding import PartitionSpec as P

logit_scale = 100.0
MESH = pl.DeviceIdType.MESH
NX, NYL, NZ, NC = 4, 2, 4, 2
bf16 = jnp.bfloat16
f32 = jnp.float32
VMEM_LIMIT = 60 * 1024 * 1024


def dp_of(x, yl, z, c):
    return ((x * NYL + yl) * NZ + z) * NC + c


def coords():
    d = lax.axis_index("dp")
    c = d % NC
    z = (d // NC) % NZ
    yl = (d // (NC * NZ)) % NYL
    x = d // (NC * NZ * NYL)
    return x, yl, z, c, lax.axis_index("tensor")


class Comm:
    def __init__(self, send_sem, recv_sem):
        self.send_sem, self.recv_sem, self.n = send_sem, recv_sem, 0

    def make(self, src, dst, dev):
        i = self.n
        self.n += 1
        return pltpu.make_async_remote_copy(
            src_ref=src,
            dst_ref=dst,
            send_sem=self.send_sem.at[i],
            recv_sem=self.recv_sem.at[i],
            device_id=dev,
            device_id_type=MESH,
        )

    def send(self, src, dst, dev):
        copy = self.make(src, dst, dev)
        copy.start()
        return copy


def z_offsets():
    return list(range(1, NZ))


def zc_offsets():
    return [(kz, kc) for kz in range(NZ) for kc in range(NC) if (kz, kc) != (0, 0)]


def unit_rows(values):
    floats = values.astype(f32)
    inverse = lax.rsqrt(jnp.sum(floats * floats, axis=1, keepdims=True) + 1e-06)
    return (floats * inverse, inverse)


def unit_back(normed, inverse, grad):
    return inverse * (grad - normed * jnp.sum(grad * normed, axis=1, keepdims=True))


def layer_norm(values):
    center = values - jnp.mean(values, axis=1, keepdims=True)
    scale_inv = lax.rsqrt(jnp.mean(center * center, axis=1, keepdims=True) + 1e-05)
    return (center * scale_inv, scale_inv)


def norm_back(grad, normed, scale_inv):
    return scale_inv * (
        grad
        - jnp.mean(grad, axis=1, keepdims=True)
        - normed * jnp.mean(grad * normed, axis=1, keepdims=True)
    )


def contract_last(left, right):
    return lax.dot_general(left, right, (((1,), (1,)), ((), ())), preferred_element_type=f32)


def dot(left, right):
    return jnp.dot(left, right, preferred_element_type=f32)


def at(index, size):
    return pl.ds(pl.multiple_of(index * size, size), size)


def chunks(total, size):
    return [(i, min(size, total - i)) for i in range(0, total, size)]


def to_column(row, n):
    return jnp.transpose(jnp.broadcast_to(row, (128, n)))[:, 0:1]


def to_row(column, n):
    return jnp.transpose(jnp.broadcast_to(column, (n, 128)))[0:1]


def merged_lse(parts, count):
    peak = parts[0, 0:1]
    for i in range(1, count):
        peak = jnp.maximum(peak, parts[i, 0:1])
    total = jnp.zeros_like(peak)
    for i in range(count):
        total = total + parts[i, 1:2] * jnp.exp(parts[i, 0:1] - peak)
    return peak + jnp.log(total)


def body(
    img_ref, txt_ref, lab_ref, lin_ref, g1_ref, g2_ref, up_hbm, down_hbm, proj_hbm,
    text_out, input_out, up_out, proj_out,
    w_up, w_down, w_proj, img_all, txt_all, lab_all, mlp_t, pooled_t, act, slope,
    res_out, res_in, n_in, n_out, logits, row_st, col_st, rows_all, cols_all,
    grad, grad_t, pimg, img_in, img_sum, img_mate, ptxt, sib_in, txo, txi, tyo, tyi, tsum,
    rgrad, cot, pre_out, pre_all, mg_out, mg_in,
    wp, wps, wpo, wpi, wp_sum, wpy, wpyi, wpz, wpzi, wpl, wu, wui, wyo, wyi, wsum, wblk,
    ss, rs, ls,
):
    x, yl, z, c, t = coords()
    me = lax.axis_index("dp")
    gain1, gain2 = g1_ref[...][None, :], g2_ref[...][None, :]
    rows, embed = img_ref.shape
    width = lin_ref.shape[1]
    half = rows // 2
    hidden = up_hbm.shape[1]
    hid = hidden // 8
    eh = embed // 2
    sib, mate, ynb = (dp_of(x, yl, z, 1 - c), t), (me, 1 - t), (dp_of(x, 1 - yl, z, c), t)
    zp = [(dp_of(x, yl, (z + k) % NZ, c), t) for k in range(1, NZ)]
    xp = [(dp_of((x + k) % NX, yl, z, c), t) for k in range(1, NX)]
    zc = [(dp_of(x, yl, (z + kz) % NZ, (c + kc) % NC), t) for kz, kc in zc_offsets()]
    row_peers = [
        (dp_of(x, yl, (z + k) % NZ, c), (t + j) % 2) for k in range(NZ) for j in range(2) if k or j
    ]
    col_peers = [
        (dp_of((x + kx) % NX, (yl + ky) % NYL, z, (c + kc) % NC), t)
        for kx in range(NX)
        for ky in range(NYL)
        for kc in range(NC)
        if kx or ky or kc
    ]
    cross = [p for (kz, kc), p in zip(zc_offsets(), zc) if kz and kc]
    greet = row_peers + col_peers + cross
    entry = pltpu.get_barrier_semaphore()
    for peer in greet:
        pl.semaphore_signal(entry, inc=1, device_id=peer, device_id_type=MESH)
    loads = [
        pltpu.make_async_copy(up_hbm, w_up, ls.at[0]),
        pltpu.make_async_copy(down_hbm, w_down, ls.at[1]),
        pltpu.make_async_copy(proj_hbm, w_proj, ls.at[2]),
    ]
    for copy in loads:
        copy.start()
    my_slot = c * 8 + x * NYL + yl
    img_unit, _ = unit_rows(img_ref[...])
    img_all[at(z, rows)] = img_unit.astype(bf16)
    txt_unit, _ = unit_rows(txt_ref[at(t, half)])
    txt_all[at(my_slot, half)] = txt_unit.astype(bf16)
    lab_all[z] = jnp.broadcast_to(lab_ref[...][None, :], (8, rows))
    pl.semaphore_wait(entry, len(greet))

    comm = Comm(ss, rs)
    send = comm.send

    def same(ref, index, size, dev):
        return send(ref.at[at(index, size)], ref.at[at(index, size)], dev)

    t_y = same(txt_all, my_slot, half, ynb)
    t_x = [same(txt_all, my_slot, half, p) for p in xp]
    i_z = [same(img_all, z, rows, p) for p in zp]
    l_z = [send(lab_all.at[z], lab_all.at[z], p) for p in zp]
    t_s = [same(txt_all, my_slot, half, sib)]

    inputs = lin_ref[...].astype(f32)
    normed_in, inv_in = layer_norm(inputs)
    n_in[...] = normed_in
    mlp_in = (n_in[...] * gain1).astype(bf16)
    my_zc = z * NC + c
    for i, n in chunks(width, 128):
        mlp_t[i : i + n, at(my_zc, 128)] = jnp.transpose(
            n_in[:, i : i + n] * gain1[:, i : i + n]
        ).astype(bf16)
    loads[0].wait()

    def up_tile(i, _):
        cols = at(i, 256)
        pre = dot(mlp_in, w_up[:, cols])
        phi = 0.5 * (1.0 + lax.erf(pre * 0.7071067811865476))
        act[:, cols] = (pre * phi).astype(bf16)
        slope[:, cols] = phi + pre * jnp.exp(-0.5 * pre * pre) * 0.3989422804014327
        return _

    lax.fori_loop(0, hidden // 256, up_tile, 0)
    t_y.wait_recv()
    other = c * 8 + x * NYL + (1 - yl)
    f_x = [same(txt_all, other, half, p) for p in xp]
    t_s.append(same(txt_all, other, half, sib))

    for k, copy in zip(range(1, NX), t_x):
        copy.wait_recv()
        t_s.append(same(txt_all, c * 8 + ((x + NX - k) % NX) * NYL + yl, half, sib))
    loads[1].wait()
    acts = act[...]
    for i, n in chunks(width, 256):
        res_out[:, i : i + n] = contract_last(acts, w_down[i : i + n]).astype(bf16)
    res_c = send(res_out, res_in, mate)
    for k, copy in zip(range(1, NX), f_x):
        copy.wait_recv()
        t_s.append(same(txt_all, c * 8 + ((x + NX - k) % NX) * NYL + (1 - yl), half, sib))
    for copy in i_z + l_z:
        copy.wait()
    m_z, m_s = [], []

    def share_mlp(first, size):
        ref = mlp_t.at[first : first + size, at(my_zc, 128)]
        m_z.append((first, size, [send(ref, ref, p) for p in zp]))
        m_s.append(send(ref, ref, sib))

    def pass_mlp():
        for first, size, copies in m_z:
            for k, copy in zip(range(1, NZ), copies):
                copy.wait()
                ref = mlp_t.at[first : first + size, at(((z + NZ - k) % NZ) * NC + c, 128)]
                m_s.append(send(ref, ref, sib))
        m_z.clear()

    cut_a, cut_b = 640, 1152
    share_mlp(0, cut_a)
    for copy in t_s:
        copy.wait()
    t_y.wait_send()
    for copy in t_x + f_x:
        copy.wait_send()

    n_row, n_col = img_all.shape[0], txt_all.shape[0]
    tile = 256

    def logit_tile(i, peak):
        tile_logits = logit_scale * contract_last(img_all[...], txt_all[at(i, tile)])
        logits[:, at(i, tile)] = tile_logits
        return jnp.maximum(peak, jnp.max(tile_logits, axis=1, keepdims=True))

    row_peak = lax.fori_loop(
        0, n_col // tile, logit_tile, jnp.full((n_row, 1), -jnp.inf, f32)
    )

    def total_tile(i, total):
        cols = at(i, tile)
        part = logits[:, cols]
        col_peak = jnp.max(part, axis=0, keepdims=True)
        col_st[0:1, cols] = col_peak
        col_st[1:2, cols] = jnp.sum(jnp.exp(part - col_peak), axis=0, keepdims=True)
        return total + jnp.sum(jnp.exp(part - row_peak), axis=1, keepdims=True)

    row_total = lax.fori_loop(0, n_col // tile, total_tile, jnp.zeros((n_row, 1), f32))
    my_col, my_row = (x * NYL + yl) * NC + c, z * 2 + t
    stats = [send(col_st, cols_all.at[my_col], p) for p in col_peers]
    row_st[0:1] = to_row(row_peak, n_row)
    row_st[1:2] = to_row(row_total, n_row)
    stats += [send(row_st, rows_all.at[my_row], p) for p in row_peers]
    rows_all[my_row] = row_st[...]
    cols_all[my_col] = col_st[...]

    res_c.wait()
    resid = lin_ref[...].astype(f32) + (res_out[...].astype(f32) + res_in[...].astype(f32))
    normed_out, inv_out = layer_norm(resid)
    n_out[...] = normed_out
    for i, n in chunks(width, 128):
        pooled_t[i : i + n] = jnp.transpose(
            n_out[:, i : i + n] * gain2[:, i : i + n]
        ).astype(bf16)
    for copy in stats:
        copy.wait()
    share_mlp(cut_a, cut_b - cut_a)

    row_lse = to_column(merged_lse(rows_all, 8), n_row)
    col_st[0:1] = merged_lse(cols_all, 16)
    label_col = jnp.concatenate(
        [to_column(lab_all[i, 0:1].astype(f32), rows) for i in range(NZ)], axis=0
    )

    def grad_tile(i, _):
        cols = at(i, tile)
        part = logits[:, cols]
        place = i * tile + lax.broadcasted_iota(jnp.int32, (1, tile), 1)
        slot = place // half
        index = (((slot % (NX * NYL)) * NZ + z) * NC + slot // (NX * NYL)) * rows
        index = (index + t * half + place % half).astype(f32)
        value = 0.5 * (jnp.exp(part - row_lse) + jnp.exp(part - col_st[0:1, cols]))
        value = value - jnp.where(label_col == index, 1.0, 0.0)
        grad[:, cols] = value.astype(bf16)
        grad_t[at(i, tile)] = jnp.transpose(value).astype(bf16)
        return _

    lax.fori_loop(0, n_col // tile, grad_tile, 0)

    def img_tile(i, _):
        cols = at(i, 256)
        pimg[:, cols] = (logit_scale * dot(grad[...], txt_all[:, cols])).astype(bf16)
        return _

    lax.fori_loop(0, embed // 256, img_tile, 0)
    r_z = [
        send(pimg.at[at((z + k) % NZ, rows)], img_in.at[k - 1], p)
        for k, p in zip(range(1, NZ), zp)
    ]

    def txt_tile(i, _):
        cols = at(i, 256)
        ptxt[:, cols] = (logit_scale * dot(grad_t[...], img_all[:, cols])).astype(bf16)
        return _

    lax.fori_loop(0, embed // 256, txt_tile, 0)
    side = 8 * half
    to_sib = send(ptxt.at[at(1 - c, side)], sib_in, sib)
    to_sib.wait()
    pair = 2 * half

    def chip_sum(index, size):
        mine = ptxt[pl.ds(pl.multiple_of(c * side + index * size, size), size)]
        return mine.astype(f32) + sib_in[at(index, size)].astype(f32)

    x_t = []
    for k, p in zip(range(1, NX), xp):
        txo[k - 1] = chip_sum((x + k) % NX, pair).astype(bf16)
        x_t.append(send(txo.at[k - 1], txi.at[k - 1], p))

    for copy in r_z:
        copy.wait()
    total = pimg[at(z, rows)].astype(f32)
    for k in range(NZ - 1):
        total = total + img_in[k].astype(f32)
    img_sum[...] = total.astype(bf16)
    i_m = send(img_sum, img_mate, mate)
    share_mlp(cut_b, width - cut_b)
    loads[2].wait()
    i_m.wait()
    unit_grad = img_sum[...].astype(f32) + img_mate[...].astype(f32)
    img_norm, img_inv = unit_rows(img_ref[...])
    image_grad = unit_back(img_norm, img_inv, unit_grad)
    cotangent = image_grad.astype(bf16)
    cot[...] = cotangent
    eighth = width // 8
    cot_half = cot[:, at(t, eh)]
    for q in range(2):
        for i in range(NX):
            first = (2 * i + q) * eighth
            wp[q, i] = dot(pooled_t[first : first + eighth], cot_half).astype(bf16)
    p_s = send(wp.at[1 - c], wps, sib)
    for i, n in chunks(width, 256):
        rgrad[:, i : i + n] = (
            contract_last(cotangent, w_proj[i : i + n]) * gain2[:, i : i + n]
        )
    rgrad[...] = norm_back(rgrad[...], n_out[...], inv_out)
    pass_mlp()
    p_s.wait()
    p_x = []
    for k, p in zip(range(1, NX), xp):
        b = (x + k) % NX
        wpo[k - 1] = (wp[c, b].astype(f32) + wps[b].astype(f32)).astype(bf16)
        p_x.append(send(wpo.at[k - 1], wpi.at[k - 1], p))
    resid_cot = rgrad[...].astype(bf16)
    g_sends = []
    for (kz, kc), p in zip(zc_offsets() + [(0, 0)], zc + [None]):
        slot = ((z + kz) % NZ) * NC + (c + kc) % NC
        cols = at(slot, hid)
        pre_out[:, cols] = (dot(resid_cot, w_down[:, cols]) * slope[:, cols]).astype(bf16)
        if p is None:
            pre_all[at(my_zc, rows)] = pre_out[:, cols]
        else:
            g_sends.append(send(pre_out.at[:, cols], pre_all.at[at(my_zc, rows)], p))
    pre_grad = pre_out[...]
    for i, n in chunks(width, 256):
        mg_out[:, i : i + n] = contract_last(pre_grad, w_up[i : i + n]).astype(bf16)
    g_m = send(mg_out, mg_in, mate)

    for copy in m_s + g_sends:
        copy.wait()
    wu_x = []
    for part in (1 - yl, yl):
        for k in range(NX):
            b = ((x + k) % NX) * NYL + part
            wu[b] = dot(mlp_t[at(b, eighth)], pre_all[...]).astype(bf16)
            if k:
                wu_x.append(send(wu.at[b], wui.at[len(wu_x)], xp[k - 1]))

    for copy in x_t:
        copy.wait()

    def x_total(part):
        mine = ptxt[pl.ds(pl.multiple_of(c * side + (x * NYL + part) * half, half), half)]
        mine = mine.astype(f32) + sib_in[at(x * NYL + part, half)].astype(f32)
        for k in range(NX - 1):
            mine = mine + txi[k, at(part, half)].astype(f32)
        return mine

    tyo[...] = x_total(1 - yl).astype(bf16)
    y_t = send(tyo, tyi, ynb)
    tsum[...] = x_total(yl)
    y_t.wait()
    txt_norm, txt_inv = unit_rows(txt_ref[at(t, half)])
    text_out[at(t, half)] = unit_back(
        txt_norm, txt_inv, tsum[...] + tyi[...].astype(f32)
    ).astype(bf16)
    t_m = same(text_out, t, half, mate)

    g_m.wait()
    dm = (mg_out[...].astype(f32) + mg_in[...].astype(f32)) * gain1
    input_out[...] = (rgrad[...] + norm_back(dm, n_in[...], inv_in)).astype(bf16)

    for copy in p_x:
        copy.wait()
    total = wp[c, x].astype(f32) + wps[x].astype(f32)
    for k in range(NX - 1):
        total = total + wpi[k].astype(f32)
    wp_sum[...] = total
    wpy[...] = total.astype(bf16)
    p_y = comm.make(wpy, wpyi, ynb)
    p_z = [comm.make(wpz.at[(z + k) % NZ], wpzi.at[k - 1], p) for k, p in zip(range(1, NZ), zp)]
    p_l = comm.make(wpl.at[1 - c], proj_out, sib)

    @pl.when(c != yl)
    def _():
        p_y.start()

    def w_total(first, part):
        total = wu[x * NYL + part].astype(f32)
        for k in range(NX - 1):
            total = total + wui[first + k].astype(f32)
        return total

    for copy in wu_x[: NX - 1]:
        copy.wait()
    wyo[...] = w_total(0, 1 - yl).astype(bf16)
    w_y = send(wyo, wyi, ynb)
    share = eighth // 8

    @pl.when(c == yl)
    def _():
        p_y.wait_recv()
        wp_sum[...] = wp_sum[...] + wpyi[...].astype(f32)
        for i in range(NZ):
            wpz[i, 0 : 2 * share] = wp_sum[2 * share * i : 2 * share * (i + 1)].astype(bf16)
            wpz[i, 2 * share :] = jnp.zeros((64 - 2 * share, eh), bf16)
        for copy in p_z:
            copy.start()

    for copy in wu_x[NX - 1 :]:
        copy.wait()
    wsum[...] = w_total(NX - 1, yl)
    w_y.wait()
    wsum[...] = wsum[...] + wyi[...].astype(f32)
    for i in range(8):
        wblk[i, 0:share] = wsum[share * i : share * (i + 1)].astype(bf16)
        wblk[i, share:] = jnp.zeros((32 - share, hid), bf16)
    last = []
    for (kz, kc), p in zip(zc_offsets(), zc):
        slot = ((z + kz) % NZ) * NC + (c + kc) % NC
        last.append(send(wblk.at[slot], up_out.at[:, at(my_zc, hid)], p))
    up_out[:, at(my_zc, hid)] = wblk[my_zc]

    @pl.when(c == yl)
    def _():
        for copy in p_z:
            copy.wait()
        total = wpz[z].astype(f32)
        for k in range(NZ - 1):
            total = total + wpzi[k].astype(f32)
        wp_sum[0:64] = total
        for i in range(NC):
            wpl[i, 0:share] = wp_sum[share * i : share * (i + 1)]
            wpl[i, share:] = jnp.zeros((32 - share, eh), f32)
        p_l.start()
        proj_out[...] = wpl[c]
        p_l.wait_send()

    @pl.when(c != yl)
    def _():
        p_y.wait_send()
        p_l.wait_recv()

    t_m.wait()
    for copy in last:
        copy.wait()


def finish(text_ref, input_ref, up_ref, proj_ref, text_out, input_out, up_out, proj_out):
    text_out[...] = text_ref[...]
    input_out[...] = input_ref[...]
    up_out[...] = up_ref[0 : up_out.shape[0]].astype(f32)
    proj_out[...] = proj_ref[0 : proj_out.shape[0]]


def local(image_cache, text_cache, labels, layer_input, ln1_gain, ln2_gain, w_up, w_down, proj):
    rows, embed = image_cache.shape
    width = layer_input.shape[1]
    half = rows // 2
    hidden = w_up.shape[1]
    hid = hidden // 8
    eh = embed // 2
    eighth = width // 8
    share = width // 64
    n_sems = 128
    vm = pltpu.VMEM
    scratch = [
        vm(w_up.shape, bf16),
        vm(w_down.shape, bf16),
        vm(proj.shape, bf16),
        vm((NZ * rows, embed), bf16),
        vm((16 * half, embed), bf16),
        vm((NZ, 8, rows), jnp.int32),
        vm((width, 8 * rows), bf16),
        vm((width, rows), bf16),
        vm((rows, hidden), bf16),
        vm((rows, hidden), f32),
        vm((rows, width), bf16),
        vm((rows, width), bf16),
        vm((rows, width), f32),
        vm((rows, width), f32),
        vm((NZ * rows, 16 * half), f32),
        vm((2, NZ * rows), f32),
        vm((2, 16 * half), f32),
        vm((8, 2, NZ * rows), f32),
        vm((16, 2, 16 * half), f32),
        vm((NZ * rows, 16 * half), bf16),
        vm((16 * half, NZ * rows), bf16),
        vm((NZ * rows, embed), bf16),
        vm((NZ - 1, rows, embed), bf16),
        vm((rows, embed), bf16),
        vm((rows, embed), bf16),
        vm((16 * half, embed), bf16),
        vm((8 * half, embed), bf16),
        vm((NX - 1, 2 * half, embed), bf16),
        vm((NX - 1, 2 * half, embed), bf16),
        vm((half, embed), bf16),
        vm((half, embed), bf16),
        vm((half, embed), f32),
        vm((rows, width), f32),
        vm((rows, embed), bf16),
        vm((rows, hidden), bf16),
        vm((8 * rows, hid), bf16),
        vm((rows, width), bf16),
        vm((rows, width), bf16),
        vm((NYL, NX, eighth, eh), bf16),
        vm((NX, eighth, eh), bf16),
        vm((NX - 1, eighth, eh), bf16),
        vm((NX - 1, eighth, eh), bf16),
        vm((eighth, eh), f32),
        vm((eighth, eh), bf16),
        vm((eighth, eh), bf16),
        vm((NZ, 64, eh), bf16),
        vm((NZ - 1, 64, eh), bf16),
        vm((NC, 32, eh), f32),
        vm((8, eighth, hid), bf16),
        vm((2 * NX - 2, eighth, hid), bf16),
        vm((eighth, hid), bf16),
        vm((eighth, hid), bf16),
        vm((eighth, hid), f32),
        vm((8, 32, hid), bf16),
        pltpu.SemaphoreType.DMA((n_sems,)),
        pltpu.SemaphoreType.DMA((n_sems,)),
        pltpu.SemaphoreType.DMA((3,)),
    ]
    on_vmem = pl.BlockSpec(memory_space=pltpu.VMEM)
    anywhere = pl.BlockSpec(memory_space=pl.ANY)
    parts = pl.pallas_call(
        body,
        name="clip_mlp",
        out_shape=[
            jax.ShapeDtypeStruct((rows, embed), bf16),
            jax.ShapeDtypeStruct((rows, width), bf16),
            jax.ShapeDtypeStruct((32, hidden), bf16),
            jax.ShapeDtypeStruct((32, eh), f32),
        ],
        in_specs=[on_vmem] * 6 + [anywhere] * 3,
        out_specs=[on_vmem] * 4,
        scratch_shapes=scratch,
        compiler_params=pltpu.CompilerParams(
            collective_id=1, has_side_effects=True, vmem_limit_bytes=VMEM_LIMIT
        ),
    )(
        image_cache,
        text_cache,
        labels,
        layer_input,
        ln1_gain,
        ln2_gain,
        w_up,
        w_down,
        proj,
    )
    return pl.pallas_call(
        finish,
        name="finish",
        out_shape=[
            jax.ShapeDtypeStruct((rows, embed), bf16),
            jax.ShapeDtypeStruct((rows, width), bf16),
            jax.ShapeDtypeStruct((share, hidden), f32),
            jax.ShapeDtypeStruct((share, eh), f32),
        ],
        in_specs=[on_vmem] * 4,
        out_specs=[on_vmem] * 4,
    )(*parts)


def solution(mesh):
    in_specs = (
        P("dp", None),
        P("dp", None),
        P("dp"),
        P("dp", None),
        P(),
        P(),
        P(None, "tensor"),
        P(None, "tensor"),
        P(),
    )
    out_specs = (P("dp", None), P("dp", None), P("dp", "tensor"), P("dp", "tensor"))
    return jax.shard_map(local, mesh=mesh, in_specs=in_specs, out_specs=out_specs, check_vma=False)
```

```python
import jax
import jax.numpy as jnp
from jax import lax
from jax.experimental import pallas as pl
from jax.experimental.pallas import tpu as pltpu
from jax.sharding import PartitionSpec as P

logit_scale = 100.0
MESH = pl.DeviceIdType.MESH
NX, NYL, NZ, NC = 4, 2, 4, 2
bf16 = jnp.bfloat16
f32 = jnp.float32
VMEM_LIMIT = 60 * 1024 * 1024


def dp_of(x, yl, z, c):
    return ((x * NYL + yl) * NZ + z) * NC + c


def coords():
    d = lax.axis_index("dp")
    c = d % NC
    z = (d // NC) % NZ
    yl = (d // (NC * NZ)) % NYL
    x = d // (NC * NZ * NYL)
    return x, yl, z, c, lax.axis_index("tensor")


class Ring:
    def __init__(self, send, ref, size, slot, pos, peers):
        self.send, self.ref, self.size, self.slot, self.pos = send, ref, size, slot, pos
        self.right, self.left = peers[0], peers[2]
        self.right_top = self.push(0, 0, self.right)
        self.left_low = self.push(0, 1, self.left)
        self.right_low = self.push(0, 1, self.right)
        self.left_top = self.push(0, 0, self.left)

    def push(self, offset, part, dev):
        n = self.size // 2
        first = pl.multiple_of(self.slot((self.pos + offset) % 4) * self.size + part * n, n)
        ref = self.ref.at[pl.ds(first, n)]
        return self.send(ref, ref, dev)

    def forward(self):
        self.right_top.wait_recv()
        self.right_far = self.push(3, 0, self.right)
        self.left_low.wait_recv()
        self.left_far = self.push(1, 1, self.left)

    def near(self):
        self.right_low.wait_recv()
        self.left_top.wait_recv()

    def far(self):
        self.right_far.wait_recv()
        self.left_far.wait_recv()

    def drain(self):
        for copy in (self.right_top, self.left_low, self.right_low, self.left_top):
            copy.wait_send()
        self.right_far.wait_send()
        self.left_far.wait_send()


class Comm:
    def __init__(self, send_sem, recv_sem):
        self.send_sem, self.recv_sem, self.n = send_sem, recv_sem, 0

    def make(self, src, dst, dev):
        i = self.n
        self.n += 1
        return pltpu.make_async_remote_copy(
            src_ref=src,
            dst_ref=dst,
            send_sem=self.send_sem.at[i],
            recv_sem=self.recv_sem.at[i],
            device_id=dev,
            device_id_type=MESH,
        )

    def send(self, src, dst, dev):
        copy = self.make(src, dst, dev)
        copy.start()
        return copy


def z_offsets():
    return list(range(1, NZ))


def zc_offsets():
    return [(kz, kc) for kz in range(NZ) for kc in range(NC) if (kz, kc) != (0, 0)]


def unit_rows(values):
    floats = values.astype(f32)
    inverse = lax.rsqrt(jnp.sum(floats * floats, axis=1, keepdims=True) + 1e-06)
    return (floats * inverse, inverse)


def unit_back(normed, inverse, grad):
    return inverse * (grad - normed * jnp.sum(grad * normed, axis=1, keepdims=True))


def layer_norm(values):
    center = values - jnp.mean(values, axis=1, keepdims=True)
    scale_inv = lax.rsqrt(jnp.mean(center * center, axis=1, keepdims=True) + 1e-05)
    return (center * scale_inv, scale_inv)


def norm_back(grad, normed, scale_inv):
    return scale_inv * (
        grad
        - jnp.mean(grad, axis=1, keepdims=True)
        - normed * jnp.mean(grad * normed, axis=1, keepdims=True)
    )


def contract_last(left, right):
    return lax.dot_general(left, right, (((1,), (1,)), ((), ())), preferred_element_type=f32)


def dot(left, right):
    return jnp.dot(left, right, preferred_element_type=f32)


def at(index, size):
    return pl.ds(pl.multiple_of(index * size, size), size)


def chunks(total, size):
    return [(i, min(size, total - i)) for i in range(0, total, size)]


def to_column(row, n):
    return jnp.transpose(jnp.broadcast_to(row, (128, n)))[:, 0:1]


def to_row(column, n):
    return jnp.transpose(jnp.broadcast_to(column, (n, 128)))[0:1]


def merged_lse(parts, count):
    peak = parts[0, 0:1]
    for i in range(1, count):
        peak = jnp.maximum(peak, parts[i, 0:1])
    total = jnp.zeros_like(peak)
    for i in range(count):
        total = total + parts[i, 1:2] * jnp.exp(parts[i, 0:1] - peak)
    return peak + jnp.log(total)


def body(
    img_hbm, txt_hbm, lab_hbm, lin_hbm, g1_hbm, g2_hbm, up_hbm, down_hbm, proj_hbm,
    text_hbm, input_hbm, up_grad_hbm, proj_grad_hbm,
    img_ref, txt_ref, lab_ref, lin_ref, g1_ref, g2_ref, text_out, input_out, up_out, proj_out,
    w_up, w_down, w_proj, img_all, txt_all, lab_all, mlp_t, pooled_t, act, slope,
    res_out, res_in, n_in, n_out, logits, row_st, col_st, rows_all, cols_all,
    grad, grad_t, pimg, r_first, r_near, r_sum, r_last, img_sum, img_mate, ptxt, sib_in, txo, txi, tyo, tyi, tsum,
    rgrad, cot, pre_out, pre_all, mg_out, mg_in,
    wp, wps, wpo, wpi, wp_sum, wpy, wpyi, wpz, wpzi, wpl, wu, wui, wyo, wyi, wsum, wblk,
    ss, rs, ls,
):
    x, yl, z, c, t = coords()
    me = lax.axis_index("dp")
    rows, embed = img_ref.shape
    width = lin_ref.shape[1]
    half = rows // 2
    hidden = up_hbm.shape[1]
    hid = hidden // 8
    eh = embed // 2
    sib, mate, ynb = (dp_of(x, yl, z, 1 - c), t), (me, 1 - t), (dp_of(x, 1 - yl, z, c), t)
    zp = [(dp_of(x, yl, (z + k) % NZ, c), t) for k in range(1, NZ)]
    xp = [(dp_of((x + k) % NX, yl, z, c), t) for k in range(1, NX)]
    zc = [(dp_of(x, yl, (z + kz) % NZ, (c + kc) % NC), t) for kz, kc in zc_offsets()]
    row_peers = [
        (dp_of(x, yl, (z + k) % NZ, c), (t + j) % 2) for k in range(NZ) for j in range(2) if k or j
    ]
    col_peers = [
        (dp_of((x + kx) % NX, (yl + ky) % NYL, z, (c + kc) % NC), t)
        for kx in range(NX)
        for ky in range(NYL)
        for kc in range(NC)
        if kx or ky or kc
    ]
    cross = [p for (kz, kc), p in zip(zc_offsets(), zc) if kz and kc]
    greet = row_peers + col_peers + cross
    entry = pltpu.get_barrier_semaphore()
    small = [
        pltpu.make_async_copy(src, dst, ls.at[i])
        for i, (src, dst) in enumerate(
            [
                (img_hbm, img_ref),
                (txt_hbm, txt_ref),
                (lab_hbm, lab_ref),
                (lin_hbm, lin_ref),
                (g1_hbm, g1_ref),
                (g2_hbm, g2_ref),
            ]
        )
    ]
    loads = [
        pltpu.make_async_copy(up_hbm, w_up, ls.at[6]),
        pltpu.make_async_copy(down_hbm, w_down, ls.at[7]),
        pltpu.make_async_copy(proj_hbm, w_proj, ls.at[8]),
    ]
    for copy in small + loads:
        copy.start()
    for peer in greet:
        pl.semaphore_signal(entry, inc=1, device_id=peer, device_id_type=MESH)
    for copy in small:
        copy.wait()
    gain1, gain2 = g1_ref[...][None, :], g2_ref[...][None, :]
    my_slot = c * 8 + x * NYL + yl
    img_unit, _ = unit_rows(img_ref[...])
    img_all[at(z, rows)] = img_unit.astype(bf16)
    txt_unit, _ = unit_rows(txt_ref[at(t, half)])
    txt_all[at(my_slot, half)] = txt_unit.astype(bf16)
    lab_all[z] = jnp.broadcast_to(lab_ref[...][None, :], (8, rows))
    pl.semaphore_wait(entry, len(greet))

    comm = Comm(ss, rs)
    send = comm.send

    def same(ref, index, size, dev):
        return send(ref.at[at(index, size)], ref.at[at(index, size)], dev)

    t_y = same(txt_all, my_slot, half, ynb)

    def txt_slot(part):
        return lambda pos: c * 8 + pos * NYL + part

    t_x = Ring(send, txt_all, half, txt_slot(yl), x, xp)
    i_z = Ring(send, img_all, rows, lambda pos: pos, z, zp)
    l_z = [send(lab_all.at[z], lab_all.at[z], p) for p in zp]
    t_s = [same(txt_all, my_slot, half, sib)]

    inputs = lin_ref[...].astype(f32)
    normed_in, inv_in = layer_norm(inputs)
    n_in[...] = normed_in
    mlp_in = (n_in[...] * gain1).astype(bf16)
    my_zc = z * NC + c
    for i, n in chunks(width, 128):
        mlp_t[i : i + n, at(my_zc, 128)] = jnp.transpose(
            n_in[:, i : i + n] * gain1[:, i : i + n]
        ).astype(bf16)
    loads[0].wait()

    def up_tile(i, _):
        cols = at(i, 256)
        pre = dot(mlp_in, w_up[:, cols])
        phi = 0.5 * (1.0 + lax.erf(pre * 0.7071067811865476))
        act[:, cols] = (pre * phi).astype(bf16)
        slope[:, cols] = phi + pre * jnp.exp(-0.5 * pre * pre) * 0.3989422804014327
        return _

    lax.fori_loop(0, hidden // 256, up_tile, 0)
    def to_sibling(part, offsets):
        for k in offsets:
            t_s.append(same(txt_all, txt_slot(part)((x + k) % NX), half, sib))

    t_x.forward()
    t_y.wait_recv()
    f_x = Ring(send, txt_all, half, txt_slot(1 - yl), x, xp)
    to_sibling(1 - yl, [0])
    i_z.forward()
    loads[1].wait()
    acts = act[...]
    for i, n in chunks(width, 256):
        if i == 768:
            f_x.forward()
        res_out[:, i : i + n] = contract_last(acts, w_down[i : i + n]).astype(bf16)
    res_c = send(res_out, res_in, mate)
    t_x.near()
    to_sibling(yl, [1, 3])
    t_x.far()
    to_sibling(yl, [2])
    f_x.near()
    to_sibling(1 - yl, [1, 3])
    i_z.near()
    f_x.far()
    to_sibling(1 - yl, [2])
    i_z.far()
    m_z, m_s = [], []

    def share_mlp(first, size):
        ref = mlp_t.at[first : first + size, at(my_zc, 128)]
        m_z.append((first, size, [send(ref, ref, p) for p in zp]))
        m_s.append(send(ref, ref, sib))

    def pass_mlp():
        for first, size, copies in m_z:
            for k, copy in zip(range(1, NZ), copies):
                copy.wait()
                ref = mlp_t.at[first : first + size, at(((z + NZ - k) % NZ) * NC + c, 128)]
                m_s.append(send(ref, ref, sib))
        m_z.clear()

    cut_a, cut_b = 512, 768
    share_mlp(0, cut_a)
    for copy in t_s + l_z:
        copy.wait()
    t_y.wait_send()
    for ring in (t_x, f_x, i_z):
        ring.drain()

    n_row, n_col = img_all.shape[0], txt_all.shape[0]
    tile = 256

    def logit_tile(i, peak):
        tile_logits = logit_scale * contract_last(img_all[...], txt_all[at(i, tile)])
        logits[:, at(i, tile)] = tile_logits
        return jnp.maximum(peak, jnp.max(tile_logits, axis=1, keepdims=True))

    row_peak = lax.fori_loop(
        0, n_col // tile, logit_tile, jnp.full((n_row, 1), -jnp.inf, f32)
    )

    def total_tile(i, total):
        cols = at(i, tile)
        part = logits[:, cols]
        col_peak = jnp.max(part, axis=0, keepdims=True)
        col_st[0:1, cols] = col_peak
        col_st[1:2, cols] = jnp.sum(jnp.exp(part - col_peak), axis=0, keepdims=True)
        return total + jnp.sum(jnp.exp(part - row_peak), axis=1, keepdims=True)

    row_total = lax.fori_loop(0, n_col // tile, total_tile, jnp.zeros((n_row, 1), f32))
    my_col, my_row = (x * NYL + yl) * NC + c, z * 2 + t
    stats = [send(col_st, cols_all.at[my_col], p) for p in col_peers]
    row_st[0:1] = to_row(row_peak, n_row)
    row_st[1:2] = to_row(row_total, n_row)
    stats += [send(row_st, rows_all.at[my_row], p) for p in row_peers]
    rows_all[my_row] = row_st[...]
    cols_all[my_col] = col_st[...]

    res_c.wait()
    resid = lin_ref[...].astype(f32) + (res_out[...].astype(f32) + res_in[...].astype(f32))
    normed_out, inv_out = layer_norm(resid)
    n_out[...] = normed_out
    for i, n in chunks(width, 128):
        pooled_t[i : i + n] = jnp.transpose(
            n_out[:, i : i + n] * gain2[:, i : i + n]
        ).astype(bf16)
    for copy in stats:
        copy.wait()
    share_mlp(cut_a, cut_b - cut_a)

    row_lse = to_column(merged_lse(rows_all, 8), n_row)
    col_st[0:1] = merged_lse(cols_all, 16)
    label_col = jnp.concatenate(
        [to_column(lab_all[i, 0:1].astype(f32), rows) for i in range(NZ)], axis=0
    )

    def grad_tile(i, _):
        cols = at(i, tile)
        part = logits[:, cols]
        place = i * tile + lax.broadcasted_iota(jnp.int32, (1, tile), 1)
        slot = place // half
        index = (((slot % (NX * NYL)) * NZ + z) * NC + slot // (NX * NYL)) * rows
        index = (index + t * half + place % half).astype(f32)
        value = 0.5 * (jnp.exp(part - row_lse) + jnp.exp(part - col_st[0:1, cols]))
        value = value - jnp.where(label_col == index, 1.0, 0.0)
        grad[:, cols] = value.astype(bf16)
        grad_t[at(i, tile)] = jnp.transpose(value).astype(bf16)
        return _

    lax.fori_loop(0, n_col // tile, grad_tile, 0)

    right, left = zp[0], zp[2]
    z_right, z_left, z_far = (z + 1) % NZ, (z + 3) % NZ, (z + 2) % NZ

    def strip(pos, part, cols):
        return pl.ds(pl.multiple_of(pos * rows + part * half, half), half), cols

    parts = [slice(i, i + 256) for i in range(0, embed, 256)]
    first_r, first_l, near_r, near_l = [], [], [], []
    for cols in parts:
        pimg[:, cols] = (logit_scale * dot(grad[...], txt_all[:, cols])).astype(bf16)
        first_r.append(send(pimg.at[strip(z_far, 0, cols)], r_first.at[0, :, cols], right))
        first_l.append(send(pimg.at[strip(z_far, 1, cols)], r_first.at[1, :, cols], left))
    for cols in parts:
        near_r.append(send(pimg.at[strip(z_right, 1, cols)], r_near.at[0, :, cols], right))
        near_l.append(send(pimg.at[strip(z_left, 0, cols)], r_near.at[1, :, cols], left))

    def txt_tile(i, _):
        cols = at(i, 256)
        ptxt[:, cols] = (logit_scale * dot(grad_t[...], img_all[:, cols])).astype(bf16)
        return _

    lax.fori_loop(0, embed // 256, txt_tile, 0)
    side = 8 * half
    to_sib = send(ptxt.at[at(1 - c, side)], sib_in, sib)
    sum_r, sum_l = [], []
    for cols, copy_r, copy_l in zip(parts, first_r, first_l):
        copy_r.wait()
        r_sum[0, :, cols] = (
            pimg[strip(z_right, 0, cols)].astype(f32) + r_first[0, :, cols].astype(f32)
        ).astype(bf16)
        sum_r.append(send(r_sum.at[0, :, cols], r_last.at[0, :, cols], right))
        copy_l.wait()
        r_sum[1, :, cols] = (
            pimg[strip(z_left, 1, cols)].astype(f32) + r_first[1, :, cols].astype(f32)
        ).astype(bf16)
        sum_l.append(send(r_sum.at[1, :, cols], r_last.at[1, :, cols], left))
    share_mlp(cut_b, width - cut_b)
    to_sib.wait()
    pair = 2 * half

    def chip_sum(index, size):
        mine = ptxt[pl.ds(pl.multiple_of(c * side + index * size, size), size)]
        return mine.astype(f32) + sib_in[at(index, size)].astype(f32)

    x_t = []
    for k, p in zip(range(1, NX), xp):
        txo[k - 1] = chip_sum((x + k) % NX, pair).astype(bf16)
        x_t.append(send(txo.at[k - 1], txi.at[k - 1], p))

    i_m = []
    for i, cols in enumerate(parts):
        near_l[i].wait()
        sum_r[i].wait()
        img_sum[0:half, cols] = (
            pimg[strip(z, 0, cols)].astype(f32)
            + r_last[0, :, cols].astype(f32)
            + r_near[1, :, cols].astype(f32)
        ).astype(bf16)
        near_r[i].wait()
        sum_l[i].wait()
        img_sum[half:, cols] = (
            pimg[strip(z, 1, cols)].astype(f32)
            + r_last[1, :, cols].astype(f32)
            + r_near[0, :, cols].astype(f32)
        ).astype(bf16)
        i_m.append(send(img_sum.at[:, cols], img_mate.at[:, cols], mate))
    loads[2].wait()
    for copy in i_m:
        copy.wait()
    unit_grad = img_sum[...].astype(f32) + img_mate[...].astype(f32)
    img_norm, img_inv = unit_rows(img_ref[...])
    image_grad = unit_back(img_norm, img_inv, unit_grad)
    cotangent = image_grad.astype(bf16)
    cot[...] = cotangent
    eighth = width // 8
    cot_half = cot[:, at(t, eh)]
    for q in range(2):
        for i in range(NX):
            first = (2 * i + q) * eighth
            wp[q, i] = dot(pooled_t[first : first + eighth], cot_half).astype(bf16)
    p_s = send(wp.at[1 - c], wps, sib)
    for i, n in chunks(width, 256):
        rgrad[:, i : i + n] = (
            contract_last(cotangent, w_proj[i : i + n]) * gain2[:, i : i + n]
        )
    rgrad[...] = norm_back(rgrad[...], n_out[...], inv_out)
    resid_cot = rgrad[...].astype(bf16)
    g_sends = []
    p_x = []
    for i, ((kz, kc), p) in enumerate(zip(zc_offsets() + [(0, 0)], zc + [None])):
        if i == 3:
            p_s.wait()
            for k, peer in zip(range(1, NX), xp):
                b = (x + k) % NX
                wpo[k - 1] = (wp[c, b].astype(f32) + wps[b].astype(f32)).astype(bf16)
                p_x.append(send(wpo.at[k - 1], wpi.at[k - 1], peer))
        slot = ((z + kz) % NZ) * NC + (c + kc) % NC
        cols = at(slot, hid)
        pre_out[:, cols] = (dot(resid_cot, w_down[:, cols]) * slope[:, cols]).astype(bf16)
        if p is None:
            pre_all[at(my_zc, rows)] = pre_out[:, cols]
        else:
            g_sends.append(send(pre_out.at[:, cols], pre_all.at[at(my_zc, rows)], p))
    for copy in x_t:
        copy.wait()

    def x_total(part):
        mine = ptxt[pl.ds(pl.multiple_of(c * side + (x * NYL + part) * half, half), half)]
        mine = mine.astype(f32) + sib_in[at(x * NYL + part, half)].astype(f32)
        for k in range(NX - 1):
            mine = mine + txi[k, at(part, half)].astype(f32)
        return mine

    tyo[...] = x_total(1 - yl).astype(bf16)
    y_t = send(tyo, tyi, ynb)
    tsum[...] = x_total(yl)
    pre_grad = pre_out[...]
    for i, n in chunks(width, 256):
        mg_out[:, i : i + n] = contract_last(pre_grad, w_up[i : i + n]).astype(bf16)
    g_m = send(mg_out, mg_in, mate)

    pass_mlp()
    y_t.wait()
    txt_norm, txt_inv = unit_rows(txt_ref[at(t, half)])
    text_out[at(t, half)] = unit_back(
        txt_norm, txt_inv, tsum[...] + tyi[...].astype(f32)
    ).astype(bf16)
    for copy in m_s + g_sends:
        copy.wait()
    wu_x = []
    for part in (1 - yl, yl):
        for k in range(NX):
            b = ((x + k) % NX) * NYL + part
            wu[b] = dot(mlp_t[at(b, eighth)], pre_all[...]).astype(bf16)
            if k:
                wu_x.append(send(wu.at[b], wui.at[len(wu_x)], xp[k - 1]))

    for copy in p_x:
        copy.wait()
    total = wp[c, x].astype(f32) + wps[x].astype(f32)
    for k in range(NX - 1):
        total = total + wpi[k].astype(f32)
    wp_sum[...] = total
    wpy[...] = total.astype(bf16)
    p_y = comm.make(wpy, wpyi, ynb)
    p_z = [comm.make(wpz.at[(z + k) % NZ], wpzi.at[k - 1], p) for k, p in zip(range(1, NZ), zp)]
    p_l = comm.make(wpl.at[1 - c], proj_out, sib)

    @pl.when(c != yl)
    def _():
        p_y.start()

    g_m.wait()
    dm = (mg_out[...].astype(f32) + mg_in[...].astype(f32)) * gain1
    input_out[...] = (rgrad[...] + norm_back(dm, n_in[...], inv_in)).astype(bf16)
    stores = [
        pltpu.make_async_copy(src, dst, ls.at[9 + i])
        for i, (src, dst) in enumerate(
            [
                (input_out, input_hbm),
                (text_out, text_hbm),
                (up_out, up_grad_hbm),
                (proj_out, proj_grad_hbm),
            ]
        )
    ]
    stores[0].start()

    def w_total(first, part):
        total = wu[x * NYL + part].astype(f32)
        for k in range(NX - 1):
            total = total + wui[first + k].astype(f32)
        return total

    for copy in wu_x[: NX - 1]:
        copy.wait()
    wyo[...] = w_total(0, 1 - yl).astype(bf16)
    w_y = send(wyo, wyi, ynb)
    t_m = same(text_out, t, half, mate)
    share = eighth // 8

    @pl.when(c == yl)
    def _():
        p_y.wait_recv()
        wp_sum[...] = wp_sum[...] + wpyi[...].astype(f32)
        for i in range(NZ):
            wpz[i, 0 : 2 * share] = wp_sum[2 * share * i : 2 * share * (i + 1)].astype(bf16)
            wpz[i, 2 * share :] = jnp.zeros((64 - 2 * share, eh), bf16)
        for copy in p_z:
            copy.start()

    for copy in wu_x[NX - 1 :]:
        copy.wait()
    wsum[...] = w_total(NX - 1, yl)
    w_y.wait()
    wsum[...] = wsum[...] + wyi[...].astype(f32)
    for i in range(8):
        wblk[i, 0:share] = wsum[share * i : share * (i + 1)].astype(bf16)
        wblk[i, share:] = jnp.zeros((32 - share, hid), bf16)
    last = []
    for (kz, kc), p in zip(zc_offsets(), zc):
        slot = ((z + kz) % NZ) * NC + (c + kc) % NC
        last.append(send(wblk.at[slot], up_out.at[:, at(my_zc, hid)], p))
    up_out[:, at(my_zc, hid)] = wblk[my_zc]

    @pl.when(c == yl)
    def _():
        for copy in p_z:
            copy.wait()
        total = wpz[z].astype(f32)
        for k in range(NZ - 1):
            total = total + wpzi[k].astype(f32)
        wp_sum[0:64] = total
        for i in range(NC):
            wpl[i, 0:share] = wp_sum[share * i : share * (i + 1)]
            wpl[i, share:] = jnp.zeros((32 - share, eh), f32)
        p_l.start()
        proj_out[...] = wpl[c]
        p_l.wait_send()

    @pl.when(c != yl)
    def _():
        p_y.wait_send()
        p_l.wait_recv()

    stores[3].start()
    t_m.wait()
    stores[1].start()
    for copy in last:
        copy.wait()
    stores[2].start()
    for copy in stores:
        copy.wait()


def finish(text_ref, input_ref, up_ref, proj_ref, text_out, input_out, up_out, proj_out):
    text_out[...] = text_ref[...]
    input_out[...] = input_ref[...]
    up_out[...] = up_ref[0 : up_out.shape[0]].astype(f32)
    proj_out[...] = proj_ref[0 : proj_out.shape[0]]


def local(image_cache, text_cache, labels, layer_input, ln1_gain, ln2_gain, w_up, w_down, proj):
    rows, embed = image_cache.shape
    width = layer_input.shape[1]
    half = rows // 2
    hidden = w_up.shape[1]
    hid = hidden // 8
    eh = embed // 2
    eighth = width // 8
    share = width // 64
    n_sems = 192
    vm = pltpu.VMEM
    scratch = [
        vm((rows, embed), bf16),
        vm((rows, embed), bf16),
        vm((rows,), jnp.int32),
        vm((rows, width), bf16),
        vm((width,), f32),
        vm((width,), f32),
        vm((rows, embed), bf16),
        vm((rows, width), bf16),
        vm((32, hidden), bf16),
        vm((32, eh), f32),
        vm(w_up.shape, bf16),
        vm(w_down.shape, bf16),
        vm(proj.shape, bf16),
        vm((NZ * rows, embed), bf16),
        vm((16 * half, embed), bf16),
        vm((NZ, 8, rows), jnp.int32),
        vm((width, 8 * rows), bf16),
        vm((width, rows), bf16),
        vm((rows, hidden), bf16),
        vm((rows, hidden), f32),
        vm((rows, width), bf16),
        vm((rows, width), bf16),
        vm((rows, width), f32),
        vm((rows, width), f32),
        vm((NZ * rows, 16 * half), f32),
        vm((2, NZ * rows), f32),
        vm((2, 16 * half), f32),
        vm((8, 2, NZ * rows), f32),
        vm((16, 2, 16 * half), f32),
        vm((NZ * rows, 16 * half), bf16),
        vm((16 * half, NZ * rows), bf16),
        vm((NZ * rows, embed), bf16),
        vm((2, half, embed), bf16),
        vm((2, half, embed), bf16),
        vm((2, half, embed), bf16),
        vm((2, half, embed), bf16),
        vm((rows, embed), bf16),
        vm((rows, embed), bf16),
        vm((16 * half, embed), bf16),
        vm((8 * half, embed), bf16),
        vm((NX - 1, 2 * half, embed), bf16),
        vm((NX - 1, 2 * half, embed), bf16),
        vm((half, embed), bf16),
        vm((half, embed), bf16),
        vm((half, embed), f32),
        vm((rows, width), f32),
        vm((rows, embed), bf16),
        vm((rows, hidden), bf16),
        vm((8 * rows, hid), bf16),
        vm((rows, width), bf16),
        vm((rows, width), bf16),
        vm((NYL, NX, eighth, eh), bf16),
        vm((NX, eighth, eh), bf16),
        vm((NX - 1, eighth, eh), bf16),
        vm((NX - 1, eighth, eh), bf16),
        vm((eighth, eh), f32),
        vm((eighth, eh), bf16),
        vm((eighth, eh), bf16),
        vm((NZ, 64, eh), bf16),
        vm((NZ - 1, 64, eh), bf16),
        vm((NC, 32, eh), f32),
        vm((8, eighth, hid), bf16),
        vm((2 * NX - 2, eighth, hid), bf16),
        vm((eighth, hid), bf16),
        vm((eighth, hid), bf16),
        vm((eighth, hid), f32),
        vm((8, 32, hid), bf16),
        pltpu.SemaphoreType.DMA((n_sems,)),
        pltpu.SemaphoreType.DMA((n_sems,)),
        pltpu.SemaphoreType.DMA((13,)),
    ]
    on_vmem = pl.BlockSpec(memory_space=pltpu.VMEM)
    anywhere = pl.BlockSpec(memory_space=pl.ANY)
    parts = pl.pallas_call(
        body,
        name="clip_mlp",
        out_shape=[
            jax.ShapeDtypeStruct((rows, embed), bf16),
            jax.ShapeDtypeStruct((rows, width), bf16),
            jax.ShapeDtypeStruct((32, hidden), bf16),
            jax.ShapeDtypeStruct((32, eh), f32),
        ],
        in_specs=[anywhere] * 9,
        out_specs=[anywhere] * 4,
        scratch_shapes=scratch,
        compiler_params=pltpu.CompilerParams(
            collective_id=1, has_side_effects=True, vmem_limit_bytes=VMEM_LIMIT
        ),
    )(
        image_cache,
        text_cache,
        labels,
        layer_input,
        ln1_gain,
        ln2_gain,
        w_up,
        w_down,
        proj,
    )
    return pl.pallas_call(
        finish,
        name="finish",
        out_shape=[
            jax.ShapeDtypeStruct((rows, embed), bf16),
            jax.ShapeDtypeStruct((rows, width), bf16),
            jax.ShapeDtypeStruct((share, hidden), f32),
            jax.ShapeDtypeStruct((share, eh), f32),
        ],
        in_specs=[on_vmem] * 4,
        out_specs=[on_vmem] * 4,
    )(*parts)


def solution(mesh):
    in_specs = (
        P("dp", None),
        P("dp", None),
        P("dp"),
        P("dp", None),
        P(),
        P(),
        P(None, "tensor"),
        P(None, "tensor"),
        P(),
    )
    out_specs = (P("dp", None), P("dp", None), P("dp", "tensor"), P("dp", "tensor"))
    return jax.shard_map(local, mesh=mesh, in_specs=in_specs, out_specs=out_specs, check_vma=False)
```

```python
import jax
import jax.numpy as jnp
from jax import lax
from jax.experimental import pallas as pl
from jax.experimental.pallas import tpu as pltpu
from jax.sharding import PartitionSpec as P

logit_scale = 100.0
MESH = pl.DeviceIdType.MESH
NX, NYL, NZ, NC = 4, 2, 4, 2
bf16 = jnp.bfloat16
f32 = jnp.float32
VMEM_LIMIT = 60 * 1024 * 1024


def dp_of(x, yl, z, c):
    return ((x * NYL + yl) * NZ + z) * NC + c


def coords():
    d = lax.axis_index("dp")
    c = d % NC
    z = (d // NC) % NZ
    yl = (d // (NC * NZ)) % NYL
    x = d // (NC * NZ * NYL)
    return x, yl, z, c, lax.axis_index("tensor")


class Comm:
    def __init__(self, sems):
        self.sems, self.n = sems, 0

    def new(self):
        self.n += 1
        return self.sems.at[self.n - 1]

    def make(self, src, dst, dev, sent=None, got=None):
        return pltpu.make_async_remote_copy(
            src_ref=src,
            dst_ref=dst,
            send_sem=self.new() if sent is None else sent,
            recv_sem=self.new() if got is None else got,
            device_id=dev,
            device_id_type=MESH,
        )

    def send(self, src, dst, dev, sent=None, got=None):
        copy = self.make(src, dst, dev, sent, got)
        copy.start()
        return copy


def wait_all(sem, ref):
    pltpu.make_async_copy(ref, ref, sem).wait()


class Ring:
    def __init__(self, comm, ref, size, slot, pos, peers, sent):
        self.comm, self.ref, self.size, self.slot, self.pos = comm, ref, size, slot, pos
        self.right, self.left, self.sent = peers[0], peers[2], sent
        self.got_near, self.got_far = comm.new(), comm.new()
        self.right_top = self.push(0, 0, self.right)
        self.left_low = self.push(0, 1, self.left)
        self.push(0, 1, self.right, self.got_near)
        self.push(0, 0, self.left, self.got_near)

    def push(self, offset, part, dev, got=None):
        n = self.size // 2
        first = pl.multiple_of(self.slot((self.pos + offset) % 4) * self.size + part * n, n)
        ref = self.ref.at[pl.ds(first, n)]
        return self.comm.send(ref, ref, dev, self.sent, got)

    def forward(self):
        self.right_top.wait_recv()
        self.push(3, 0, self.right, self.got_far)
        self.left_low.wait_recv()
        self.push(1, 1, self.left, self.got_far)

    def near(self):
        wait_all(self.got_near, self.ref.at[0 : self.size])

    def far(self):
        wait_all(self.got_far, self.ref.at[0 : self.size])


class RingSum:
    def __init__(self, comm, top, low, held, pos, peers, sent, two_blocks):
        self.comm, self.top, self.low, self.held, self.pos = comm, top, low, held, pos
        self.right, self.left, self.sent = peers[0], peers[2], sent
        self.two_blocks, self.got = two_blocks, comm.new()

    def at(self, offset):
        pos = (self.pos + offset) % 4
        return self.top(pos), self.low(pos)

    def first(self):
        top, low = self.at(2)
        self.first_r = self.comm.send(top, self.held(0, 0), self.right, self.sent)
        self.first_l = self.comm.send(low, self.held(0, 1), self.left, self.sent)

    def near(self):
        self.comm.send(self.at(1)[1], self.held(1, 1), self.right, self.sent, self.got)
        self.comm.send(self.at(3)[0], self.held(1, 0), self.left, self.sent, self.got)

    def pass_on(self):
        self.first_r.wait_recv()
        added = self.at(1)[0][...].astype(f32) + self.held(0, 0)[...].astype(f32)
        self.held(2, 0)[...] = added.astype(bf16)
        self.comm.send(self.held(2, 0), self.held(3, 0), self.right, self.sent, self.got)
        self.first_l.wait_recv()
        added = self.at(3)[1][...].astype(f32) + self.held(0, 1)[...].astype(f32)
        self.held(2, 1)[...] = added.astype(bf16)
        self.comm.send(self.held(2, 1), self.held(3, 1), self.left, self.sent, self.got)

    def total(self):
        wait_all(self.got, self.two_blocks)
        return [
            own[...].astype(f32)
            + self.held(3, i)[...].astype(f32)
            + self.held(1, i)[...].astype(f32)
            for i, own in enumerate(self.at(0))
        ]


def z_offsets():
    return list(range(1, NZ))


def zc_offsets():
    return [(kz, kc) for kz in range(NZ) for kc in range(NC) if (kz, kc) != (0, 0)]


def unit_rows(values):
    floats = values.astype(f32)
    inverse = lax.rsqrt(jnp.sum(floats * floats, axis=1, keepdims=True) + 1e-06)
    return (floats * inverse, inverse)


def unit_back(normed, inverse, grad):
    return inverse * (grad - normed * jnp.sum(grad * normed, axis=1, keepdims=True))


def layer_norm(values):
    center = values - jnp.mean(values, axis=1, keepdims=True)
    scale_inv = lax.rsqrt(jnp.mean(center * center, axis=1, keepdims=True) + 1e-05)
    return (center * scale_inv, scale_inv)


def norm_back(grad, normed, scale_inv):
    return scale_inv * (
        grad
        - jnp.mean(grad, axis=1, keepdims=True)
        - normed * jnp.mean(grad * normed, axis=1, keepdims=True)
    )


def contract_last(left, right):
    return lax.dot_general(left, right, (((1,), (1,)), ((), ())), preferred_element_type=f32)


def contract_first(left, right):
    return lax.dot_general(left, right, (((0,), (0,)), ((), ())), preferred_element_type=f32)


def dot(left, right):
    return jnp.dot(left, right, preferred_element_type=f32)


def at(index, size):
    return pl.ds(pl.multiple_of(index * size, size), size)


def chunks(total, size):
    return [(i, min(size, total - i)) for i in range(0, total, size)]


def to_column(row, n):
    return jnp.transpose(jnp.broadcast_to(row, (128, n)))[:, 0:1]


def to_row(column, n):
    return jnp.transpose(jnp.broadcast_to(column, (n, 128)))[0:1]


def merged_lse(parts, count):
    peak = parts[0, 0:1]
    for i in range(1, count):
        peak = jnp.maximum(peak, parts[i, 0:1])
    total = jnp.zeros_like(peak)
    for i in range(count):
        total = total + parts[i, 1:2] * jnp.exp(parts[i, 0:1] - peak)
    return peak + jnp.log(total)


def body(
    img_hbm, txt_hbm, lab_hbm, lin_hbm, g1_hbm, g2_hbm, up_hbm, down_hbm, proj_hbm,
    text_hbm, input_hbm, up_grad_hbm, proj_grad_hbm,
    img_ref, txt_ref, lab_ref, lin_ref, g1_ref, g2_ref, text_out, input_out, up_out, proj_out, up_f, proj_f,
    w_up, w_down, w_proj, img_all, txt_all, lab_all, mlp_t, pooled_t, act, slope,
    res_out, res_in, n_in, n_out, logits, row_st, col_st, col_lse, rows_all, cols_all,
    grad, pimg, r_held, img_sum, img_mate, ptxt, sib_in, txo, t_held, tyo, tyi, tsum,
    rgrad, cot, cot_two, pre_out, pre_all, mg_out, mg_in,
    wpo, wpi, wp_sum, wpy, wpyi, wpz, wpzi, wpl, wu, wui, wyo, wyi, wsum, wblk,
    sems, ls,
):
    x, yl, z, c, t = coords()
    me = lax.axis_index("dp")
    rows, embed = img_ref.shape
    width = lin_ref.shape[1]
    half = rows // 2
    hidden = up_hbm.shape[1]
    hid = hidden // 8
    eh = embed // 2
    sib, mate, ynb = (dp_of(x, yl, z, 1 - c), t), (me, 1 - t), (dp_of(x, 1 - yl, z, c), t)
    zp = [(dp_of(x, yl, (z + k) % NZ, c), t) for k in range(1, NZ)]
    xp = [(dp_of((x + k) % NX, yl, z, c), t) for k in range(1, NX)]
    zc = [(dp_of(x, yl, (z + kz) % NZ, (c + kc) % NC), t) for kz, kc in zc_offsets()]
    row_peers = [
        (dp_of(x, yl, (z + k) % NZ, c), (t + j) % 2) for k in range(NZ) for j in range(2) if k or j
    ]
    col_peers = [
        (dp_of((x + kx) % NX, (yl + ky) % NYL, z, (c + kc) % NC), t)
        for kx in range(NX)
        for ky in range(NYL)
        for kc in range(NC)
        if kx or ky or kc
    ]
    cross = [p for (kz, kc), p in zip(zc_offsets(), zc) if kz and kc]
    greet = row_peers + col_peers + cross
    entry = pltpu.get_barrier_semaphore()
    small = [
        pltpu.make_async_copy(src, dst, ls.at[i])
        for i, (src, dst) in enumerate(
            [
                (img_hbm, img_ref),
                (txt_hbm, txt_ref),
                (lab_hbm, lab_ref),
                (lin_hbm, lin_ref),
                (g1_hbm, g1_ref),
                (g2_hbm, g2_ref),
            ]
        )
    ]
    loads = [
        pltpu.make_async_copy(up_hbm, w_up, ls.at[6]),
        pltpu.make_async_copy(down_hbm, w_down, ls.at[7]),
        pltpu.make_async_copy(proj_hbm, w_proj, ls.at[8]),
    ]
    for copy in small + loads:
        copy.start()
    for peer in greet:
        pl.semaphore_signal(entry, inc=1, device_id=peer, device_id_type=MESH)
    for copy in small:
        copy.wait()
    gain1, gain2 = g1_ref[...][None, :], g2_ref[...][None, :]
    my_slot = c * 8 + x * NYL + yl
    img_unit, _ = unit_rows(img_ref[...])
    img_all[at(z, rows)] = img_unit.astype(bf16)
    txt_unit, _ = unit_rows(txt_ref[at(t, half)])
    txt_all[at(my_slot, half)] = txt_unit.astype(bf16)
    lab_all[z] = jnp.broadcast_to(lab_ref[...][None, :], (8, rows))
    pl.semaphore_wait(entry, len(greet))

    comm = Comm(sems)
    send, new = comm.send, comm.new

    def same(ref, index, size, dev, sent=None, got=None):
        return send(ref.at[at(index, size)], ref.at[at(index, size)], dev, sent, got)

    txt_sent, img_sent, lab_sent, sib_got, lab_got = [new() for _ in range(5)]
    t_y = same(txt_all, my_slot, half, ynb, txt_sent)

    def txt_slot(part):
        return lambda pos: c * 8 + pos * NYL + part

    t_x = Ring(comm, txt_all, half, txt_slot(yl), x, xp, txt_sent)
    i_z = Ring(comm, img_all, rows, lambda pos: pos, z, zp, img_sent)
    for p in zp:
        send(lab_all.at[z], lab_all.at[z], p, lab_sent, lab_got)
    same(txt_all, my_slot, half, sib, txt_sent, sib_got)

    inputs = lin_ref[...].astype(f32)
    normed_in, inv_in = layer_norm(inputs)
    n_in[...] = normed_in
    mlp_in = (n_in[...] * gain1).astype(bf16)
    my_zc = z * NC + c
    for i, n in chunks(width, 128):
        mlp_t[i : i + n, at(my_zc, 128)] = jnp.transpose(
            n_in[:, i : i + n] * gain1[:, i : i + n]
        ).astype(bf16)
    loads[0].wait()

    def up_tile(i, _):
        cols = at(i, 512)
        pre = dot(mlp_in, w_up[:, cols])
        phi = 0.5 * (1.0 + lax.erf(pre * 0.7071067811865476))
        act[:, cols] = (pre * phi).astype(bf16)
        slope[:, cols] = phi + pre * jnp.exp(-0.5 * pre * pre) * 0.3989422804014327
        return _

    lax.fori_loop(0, hidden // 512, up_tile, 0)
    def to_sibling(part, offsets):
        for k in offsets:
            same(txt_all, txt_slot(part)((x + k) % NX), half, sib, txt_sent, sib_got)

    t_x.forward()
    t_y.wait_recv()
    f_x = Ring(comm, txt_all, half, txt_slot(1 - yl), x, xp, txt_sent)
    to_sibling(1 - yl, [0])
    i_z.forward()
    loads[1].wait()
    acts = act[...]
    for i, n in chunks(width, width // 2):
        if i:
            f_x.forward()
        res_out[:, i : i + n] = contract_last(acts, w_down[i : i + n]).astype(bf16)
    res_c = send(res_out, res_in, mate)
    t_x.near()
    to_sibling(yl, [1, 3])
    t_x.far()
    to_sibling(yl, [2])
    f_x.near()
    to_sibling(1 - yl, [1, 3])
    i_z.near()
    f_x.far()
    to_sibling(1 - yl, [2])
    i_z.far()
    mlp_sent, mlp_got, mlp_z = new(), new(), []

    def share_mlp(first, size):
        ref = mlp_t.at[first : first + size, at(my_zc, 128)]
        mlp_z.append((first, size, new()))
        for p in zp:
            send(ref, ref, p, mlp_sent, mlp_z[-1][2])
        send(ref, ref, sib, mlp_sent, mlp_got)

    def pass_mlp():
        for first, size, got in mlp_z:
            wait_all(got, mlp_t.at[first : first + size, 0:384])
            for k in range(1, NZ):
                ref = mlp_t.at[first : first + size, at(((z + k) % NZ) * NC + c, 128)]
                send(ref, ref, sib, mlp_sent, mlp_got)

    cut_a, cut_b = 512, 768
    share_mlp(0, cut_a)
    n_row, n_col = img_all.shape[0], txt_all.shape[0]
    tile = 256

    col_sent, col_got, row_sent, row_got = [new() for _ in range(4)]
    my_col = (x * NYL + yl) * NC + c
    wide = 2 * tile

    def side_totals(order):
        index = (c + order) % 2
        cols = at(index, wide)
        part = logit_scale * contract_last(img_all[...], txt_all[cols])
        logits[:, cols] = part
        col_peak = jnp.max(part, axis=0, keepdims=True)
        col_st[index, 0:1] = col_peak
        col_st[index, 1:2] = jnp.sum(jnp.exp(part - col_peak), axis=0, keepdims=True)
        for p in col_peers:
            send(col_st.at[index], cols_all.at[my_col, index], p, col_sent, col_got)
        peak = jnp.max(part, axis=1, keepdims=True)
        return peak, jnp.sum(jnp.exp(part - peak), axis=1, keepdims=True)

    peak_a, total_a = side_totals(0)
    wait_all(sib_got, txt_all.at[0 : 8 * half])
    wait_all(lab_got, lab_all.at[0:3])
    peak_b, total_b = side_totals(1)
    row_peak = jnp.maximum(peak_a, peak_b)
    row_total = total_a * jnp.exp(peak_a - row_peak) + total_b * jnp.exp(peak_b - row_peak)
    my_row = z * 2 + t
    row_st[0:1] = to_row(row_peak, n_row)
    row_st[1:2] = to_row(row_total, n_row)
    for p in row_peers:
        send(row_st, rows_all.at[my_row], p, row_sent, row_got)
    rows_all[my_row] = row_st[...]
    cols_all[my_col] = col_st[...]

    wait_all(col_got, cols_all.at[0:15])
    res_c.wait()
    resid = lin_ref[...].astype(f32) + (res_out[...].astype(f32) + res_in[...].astype(f32))
    normed_out, inv_out = layer_norm(resid)
    n_out[...] = normed_out
    for i, n in chunks(width, 128):
        pooled_t[i : i + n, at(c, rows)] = jnp.transpose(
            n_out[:, i : i + n] * gain2[:, i : i + n]
        ).astype(bf16)
    pool_s = send(
        pooled_t.at[:, at(c, rows)], pooled_t.at[:, at(c, rows)], sib
    )
    wait_all(row_got, rows_all.at[0:7])
    share_mlp(cut_a, cut_b - cut_a)

    row_lse = to_column(merged_lse(rows_all, 8), n_row)
    for i in range(2):
        col_lse[:, wide * i : wide * (i + 1)] = merged_lse(cols_all[:, i], 16)
    label_col = jnp.concatenate(
        [to_column(lab_all[i, 0:1].astype(f32), rows) for i in range(NZ)], axis=0
    )

    def grad_tile(i, _):
        cols = at(i, tile)
        part = logits[:, cols]
        place = i * tile + lax.broadcasted_iota(jnp.int32, (1, tile), 1)
        slot = place // half
        index = (((slot % (NX * NYL)) * NZ + z) * NC + slot // (NX * NYL)) * rows
        index = (index + t * half + place % half).astype(f32)
        value = 0.5 * (jnp.exp(part - row_lse) + jnp.exp(part - col_lse[:, cols]))
        value = value - jnp.where(label_col == index, 1.0, 0.0)
        grad[:, cols] = value.astype(bf16)
        return _

    lax.fori_loop(0, n_col // tile, grad_tile, 0)

    def strip(part, cols):
        return lambda pos: pimg.at[
            pl.ds(pl.multiple_of(pos * rows + part * half, half), half), cols
        ]

    def image_held(cols):
        return lambda kind, part: r_held.at[kind, part, :, cols]

    parts = [slice(0, 384), slice(384, 768), slice(768, 1024), slice(1024, embed)]
    ring_sent = new()
    sums = [
        RingSum(
            comm, strip(0, cols), strip(1, cols), image_held(cols), z, zp, ring_sent,
            pimg.at[0 : 2 * rows, cols],
        )
        for cols in parts
    ]
    for cols, ring in zip(parts, sums):
        pimg[:, cols] = (logit_scale * dot(grad[...], txt_all[:, cols])).astype(bf16)
        ring.first()
    for cols, ring in zip(parts, sums):
        ring.near()
        ptxt[:, cols] = (logit_scale * contract_first(grad[...], img_all[:, cols])).astype(bf16)
        ring.pass_on()
    share_mlp(cut_b, width - cut_b)

    side = 8 * half
    def text_sum():
        to_sib.wait()
        for pos in range(NX):
            mine = ptxt[pl.ds(pl.multiple_of(c * side + pos * pair, pair), pair)]
            txo[pos] = (
                mine.astype(f32) + sib_in[pos * pair : (pos + 1) * pair].astype(f32)
            ).astype(bf16)
        text_ring.first()
        text_ring.near()

    pair = 2 * half
    text_sent = new()
    text_ring = RingSum(
        comm,
        lambda pos: txo.at[pos, 0:half],
        lambda pos: txo.at[pos, half:],
        lambda kind, part: t_held.at[kind, part],
        x,
        xp,
        text_sent,
        txo.at[0:2],
    )
    mate_sent, mate_got = new(), new()

    def image_part(i):
        cols = parts[i]
        top, low = sums[i].total()
        img_sum[0:half, cols] = top.astype(bf16)
        img_sum[half:, cols] = low.astype(bf16)
        send(img_sum.at[:, cols], img_mate.at[:, cols], mate, mate_sent, mate_got)

    to_sib = send(ptxt.at[at(1 - c, side)], sib_in, sib)
    image_part(0)
    image_part(1)
    text_sum()
    image_part(2)
    image_part(3)
    loads[2].wait()
    wait_all(mate_got, img_mate)
    unit_grad = img_sum[...].astype(f32) + img_mate[...].astype(f32)
    img_norm, img_inv = unit_rows(img_ref[...])
    image_grad = unit_back(img_norm, img_inv, unit_grad)
    cotangent = image_grad.astype(bf16)
    cot[...] = cotangent
    cot_two[at(c, rows)] = cot[:, at(t, eh)]
    c_s = send(cot_two.at[at(c, rows)], cot_two.at[at(c, rows)], sib)
    eighth = width // 8
    rgrad[...] = contract_last(cotangent, w_proj[...]) * gain2
    p_cut = 112
    p_rows = (slice(0, p_cut), slice(p_cut, eighth))
    p_sent = new()
    p_ring = RingSum(
        comm,
        lambda pos: wpo.at[pos, p_rows[0]],
        lambda pos: wpo.at[pos, p_rows[1]],
        lambda kind, part: wpi.at[kind, p_rows[part]],
        x,
        xp,
        p_sent,
        wpo.at[0:2],
    )
    text_ring.pass_on()
    rgrad[...] = norm_back(rgrad[...], n_out[...], inv_out)
    resid_cot = rgrad[...].astype(bf16)
    g_sent, g_got = new(), new()
    for k in (2, 1, 3, 0):
        if k == 3:
            pool_s.wait()
            c_s.wait()
            for pos in range(NX):
                first = pl.multiple_of((2 * pos + c) * eighth, eighth)
                wpo[pos] = dot(pooled_t[pl.ds(first, eighth)], cot_two[...]).astype(bf16)
            p_ring.first()
            p_ring.near()
        other_z = (z + k) % NZ
        cols = at(other_z, 2 * hid)
        pre_out[:, cols] = (dot(resid_cot, w_down[:, cols]) * slope[:, cols]).astype(bf16)
        for j in range(NC):
            core = (c + j) % NC
            block = at(other_z * NC + core, hid)
            if k or j:
                send(
                    pre_out.at[:, block],
                    pre_all.at[at(my_zc, rows)],
                    (dp_of(x, yl, other_z, core), t),
                    g_sent,
                    g_got,
                )
            else:
                pre_all[at(my_zc, rows)] = pre_out[:, block]
    pass_mlp()
    pre_grad = pre_out[...]
    mg_sent, mg_got = new(), new()
    for i, n in chunks(width, 896):
        cols = slice(i, i + n)
        mg_out[:, cols] = contract_last(pre_grad, w_up[cols]).astype(bf16)
        send(mg_out.at[:, cols], mg_in.at[:, cols], mate, mg_sent, mg_got)
        if i == 0:
            tsum[0], tsum[1] = text_ring.total()
            tyo[...] = tsum[1 - yl].astype(bf16)
            y_t = send(tyo, tyi, ynb)
    p_ring.pass_on()

    wait_all(mlp_got, mlp_t.at[:, 0:512])
    wait_all(g_got, pre_all.at[0 : 7 * rows])

    wu_sent = new()

    def wu_ring(part, q):
        return RingSum(
            comm,
            lambda pos: wu.at[pos * NYL + part, :, 0:128],
            lambda pos: wu.at[pos * NYL + part, :, 128:],
            lambda kind, side: wui.at[q, kind, :, 128 * side : 128 * (side + 1)],
            x,
            xp,
            wu_sent,
            wu.at[0:2],
        )

    def wu_block(offset):
        pos = (x + offset) % NX
        wide = dot(mlp_t[at(pos, 2 * eighth)], pre_all[...]).astype(bf16)
        wu[NYL * pos], wu[NYL * pos + 1] = wide[0:eighth], wide[eighth:]

    ring_a, ring_b = wu_ring(1 - yl, 0), wu_ring(yl, 1)
    wu_block(2)
    ring_a.first()
    wu_block(1)
    wu_block(3)
    ring_a.near()
    ring_b.first()
    wu_block(0)
    for i, total in enumerate(p_ring.total()):
        wp_sum[p_rows[i]] = total
    share = eighth // 8
    for i in range(NZ):
        wpz[i, 0 : 2 * share] = wp_sum[2 * share * i : 2 * share * (i + 1)].astype(bf16)
        wpz[i, 2 * share :] = jnp.zeros((64 - 2 * share, eh), bf16)
    pz_sent, pz_got = new(), new()
    for k, p in zip(range(1, NZ), zp):
        send(wpz.at[(z + k) % NZ], wpzi.at[k - 1], p, pz_sent, pz_got)
    p_y = comm.make(wpy, wpyi, ynb)
    p_l = comm.make(wpl.at[1 - c], proj_out, sib)

    ring_a.pass_on()
    ring_b.near()
    y_t.wait()
    txt_norm, txt_inv = unit_rows(txt_ref[at(t, half)])
    text_out[at(t, half)] = unit_back(
        txt_norm, txt_inv, tsum[yl] + tyi[...].astype(f32)
    ).astype(bf16)
    t_m = same(text_out, t, half, mate)
    ring_b.pass_on()

    top, low = ring_a.total()
    wyo[:, 0:128] = top.astype(bf16)
    wyo[:, 128:] = low.astype(bf16)
    w_y = send(wyo, wyi, ynb)
    wait_all(mg_got, mg_in)
    dm = (mg_out[...].astype(f32) + mg_in[...].astype(f32)) * gain1
    input_out[...] = (rgrad[...] + norm_back(dm, n_in[...], inv_in)).astype(bf16)
    stores = [
        pltpu.make_async_copy(src, dst, ls.at[9 + i])
        for i, (src, dst) in enumerate(
            [
                (input_out, input_hbm),
                (text_out, text_hbm),
                (up_f, up_grad_hbm),
                (proj_f, proj_grad_hbm),
            ]
        )
    ]
    stores[0].start()

    wait_all(pz_got, wpzi)
    total = wpz[z].astype(f32)
    for k in range(NZ - 1):
        total = total + wpzi[k].astype(f32)
    wp_sum[0:64] = total
    wpy[...] = total.astype(bf16)

    @pl.when(c != yl)
    def _():
        p_y.start()

    top, low = ring_b.total()
    wsum[:, 0:128] = top
    wsum[:, 128:] = low
    w_y.wait()
    wsum[...] = wsum[...] + wyi[...].astype(f32)
    for i in range(8):
        wblk[i, 0:share] = wsum[share * i : share * (i + 1)].astype(bf16)
        wblk[i, share:] = jnp.zeros((32 - share, hid), bf16)
    last_sent, last_got = new(), new()
    for (kz, kc), p in zip(zc_offsets(), zc):
        slot = ((z + kz) % NZ) * NC + (c + kc) % NC
        send(wblk.at[slot], up_out.at[:, at(my_zc, hid)], p, last_sent, last_got)
    up_out[:, at(my_zc, hid)] = wblk[my_zc]

    @pl.when(c == yl)
    def _():
        p_y.wait_recv()
        wp_sum[0:64] = wp_sum[0:64] + wpyi[...].astype(f32)
        for i in range(NC):
            wpl[i, 0:share] = wp_sum[share * i : share * (i + 1)]
            wpl[i, share:] = jnp.zeros((32 - share, eh), f32)
        p_l.start()
        proj_out[...] = wpl[c]
        p_l.wait_send()

    @pl.when(c != yl)
    def _():
        p_y.wait_send()
        p_l.wait_recv()

    proj_f[...] = proj_out[0:share]
    stores[3].start()
    t_m.wait()
    stores[1].start()
    wait_all(last_got, up_out.at[:, 0 : 7 * hid])
    up_f[...] = up_out[0:share].astype(f32)
    stores[2].start()
    for sem, ref in (
        (txt_sent, txt_all.at[0 : 15 * half]),
        (img_sent, img_all.at[0 : 3 * rows]),
        (lab_sent, lab_all.at[0:3]),
        (mlp_sent, mlp_t.at[:, 0 : 7 * 128]),
        (col_sent, cols_all.at[0:15]),
        (row_sent, rows_all.at[0:7]),
        (ring_sent, pimg.at[0 : 3 * rows]),
        (mate_sent, img_mate),
        (text_sent, txo.at[0:3]),
        (p_sent, wpo.at[0:3]),
        (g_sent, pre_all.at[0 : 7 * rows]),
        (mg_sent, mg_in),
        (wu_sent, wu.at[0:6]),
        (pz_sent, wpzi),
        (last_sent, up_out.at[:, 0 : 7 * hid]),
    ):
        wait_all(sem, ref)
    for copy in stores:
        copy.wait()


def finish(*refs):
    for src, dst in zip(refs[:4], refs[4:]):
        dst[...] = src[...]


def local(image_cache, text_cache, labels, layer_input, ln1_gain, ln2_gain, w_up, w_down, proj):
    rows, embed = image_cache.shape
    width = layer_input.shape[1]
    half = rows // 2
    hidden = w_up.shape[1]
    hid = hidden // 8
    eh = embed // 2
    eighth = width // 8
    share = width // 64
    n_sems = 83
    vm = pltpu.VMEM
    scratch = [
        vm((rows, embed), bf16),
        vm((rows, embed), bf16),
        vm((rows,), jnp.int32),
        vm((rows, width), bf16),
        vm((width,), f32),
        vm((width,), f32),
        vm((rows, embed), bf16),
        vm((rows, width), bf16),
        vm((32, hidden), bf16),
        vm((32, eh), f32),
        vm((width // 64, hidden), f32),
        vm((width // 64, eh), f32),
        vm(w_up.shape, bf16),
        vm(w_down.shape, bf16),
        vm(proj.shape, bf16),
        vm((NZ * rows, embed), bf16),
        vm((16 * half, embed), bf16),
        vm((NZ, 8, rows), jnp.int32),
        vm((width, 8 * rows), bf16),
        vm((width, 2 * rows), bf16),
        vm((rows, hidden), bf16),
        vm((rows, hidden), f32),
        vm((rows, width), bf16),
        vm((rows, width), bf16),
        vm((rows, width), f32),
        vm((rows, width), f32),
        vm((NZ * rows, 16 * half), f32),
        vm((2, NZ * rows), f32),
        vm((2, 2, 8 * half), f32),
        vm((1, 16 * half), f32),
        vm((8, 2, NZ * rows), f32),
        vm((16, 2, 2, 8 * half), f32),
        vm((NZ * rows, 16 * half), bf16),
        vm((NZ * rows, embed), bf16),
        vm((4, 2, half, embed), bf16),
        vm((rows, embed), bf16),
        vm((rows, embed), bf16),
        vm((16 * half, embed), bf16),
        vm((8 * half, embed), bf16),
        vm((NX, 2 * half, embed), bf16),
        vm((4, 2, half, embed), bf16),
        vm((half, embed), bf16),
        vm((half, embed), bf16),
        vm((2, half, embed), f32),
        vm((rows, width), f32),
        vm((rows, embed), bf16),
        vm((2 * rows, eh), bf16),
        vm((rows, hidden), bf16),
        vm((8 * rows, hid), bf16),
        vm((rows, width), bf16),
        vm((rows, width), bf16),
        vm((NX, eighth, eh), bf16),
        vm((4, eighth, eh), bf16),
        vm((eighth, eh), f32),
        vm((64, eh), bf16),
        vm((64, eh), bf16),
        vm((NZ, 64, eh), bf16),
        vm((NZ - 1, 64, eh), bf16),
        vm((NC, 32, eh), f32),
        vm((8, eighth, hid), bf16),
        vm((2, 4, eighth, hid), bf16),
        vm((eighth, hid), bf16),
        vm((eighth, hid), bf16),
        vm((eighth, hid), f32),
        vm((8, 32, hid), bf16),
        pltpu.SemaphoreType.DMA((n_sems,)),
        pltpu.SemaphoreType.DMA((13,)),
    ]
    anywhere = pl.BlockSpec(memory_space=pl.ANY)
    on_vmem = pl.BlockSpec(memory_space=pltpu.VMEM)
    parts = pl.pallas_call(
        body,
        name="clip_mlp",
        out_shape=[
            jax.ShapeDtypeStruct((rows, embed), bf16),
            jax.ShapeDtypeStruct((rows, width), bf16),
            jax.ShapeDtypeStruct((width // 64, hidden), f32),
            jax.ShapeDtypeStruct((width // 64, eh), f32),
        ],
        in_specs=[anywhere] * 9,
        out_specs=[anywhere] * 4,
        scratch_shapes=scratch,
        compiler_params=pltpu.CompilerParams(
            collective_id=1, has_side_effects=True, vmem_limit_bytes=VMEM_LIMIT
        ),
    )(
        image_cache,
        text_cache,
        labels,
        layer_input,
        ln1_gain,
        ln2_gain,
        w_up,
        w_down,
        proj,
    )
    return pl.pallas_call(
        finish,
        name="finish",
        out_shape=[
            jax.ShapeDtypeStruct((rows, embed), bf16),
            jax.ShapeDtypeStruct((rows, width), bf16),
            jax.ShapeDtypeStruct((share, hidden), f32),
            jax.ShapeDtypeStruct((share, eh), f32),
        ],
        in_specs=[on_vmem] * 4,
        out_specs=[on_vmem] * 4,
    )(*parts)


def solution(mesh):
    in_specs = (
        P("dp", None),
        P("dp", None),
        P("dp"),
        P("dp", None),
        P(),
        P(),
        P(None, "tensor"),
        P(None, "tensor"),
        P(),
    )
    out_specs = (P("dp", None), P("dp", None), P("dp", "tensor"), P("dp", "tensor"))
    return jax.shard_map(local, mesh=mesh, in_specs=in_specs, out_specs=out_specs, check_vma=False)
```

```python
import jax
import jax.numpy as jnp
from jax import lax
from jax.experimental import pallas as pl
from jax.experimental.pallas import tpu as pltpu
from jax.sharding import PartitionSpec as P

logit_scale = 100.0
MESH = pl.DeviceIdType.MESH
NX, NYL, NZ, NC = 4, 2, 4, 2
bf16 = jnp.bfloat16
f32 = jnp.float32
VMEM_LIMIT = 60 * 1024 * 1024


def dp_of(x, yl, z, c):
    return ((x * NYL + yl) * NZ + z) * NC + c


def coords():
    d = lax.axis_index("dp")
    c = d % NC
    z = (d // NC) % NZ
    yl = (d // (NC * NZ)) % NYL
    x = d // (NC * NZ * NYL)
    return x, yl, z, c, lax.axis_index("tensor")


class Comm:
    def __init__(self, sems):
        self.sems, self.n = sems, 0

    def new(self):
        self.n += 1
        return self.sems.at[self.n - 1]

    def make(self, src, dst, dev, sent=None, got=None):
        return pltpu.make_async_remote_copy(
            src_ref=src,
            dst_ref=dst,
            send_sem=self.new() if sent is None else sent,
            recv_sem=self.new() if got is None else got,
            device_id=dev,
            device_id_type=MESH,
        )

    def send(self, src, dst, dev, sent=None, got=None):
        copy = self.make(src, dst, dev, sent, got)
        copy.start()
        return copy


def wait_all(sem, ref):
    pltpu.make_async_copy(ref, ref, sem).wait()


class Ring:
    def __init__(self, comm, ref, size, slot, pos, peers, sent):
        self.comm, self.ref, self.size, self.slot, self.pos = comm, ref, size, slot, pos
        self.right, self.left, self.sent = peers[0], peers[2], sent
        self.got_near, self.got_far = comm.new(), comm.new()
        self.right_top = self.push(0, 0, self.right)
        self.left_low = self.push(0, 1, self.left)
        self.push(0, 1, self.right, self.got_near)
        self.push(0, 0, self.left, self.got_near)

    def push(self, offset, part, dev, got=None):
        n = self.size // 2
        first = pl.multiple_of(self.slot((self.pos + offset) % 4) * self.size + part * n, n)
        ref = self.ref.at[pl.ds(first, n)]
        return self.comm.send(ref, ref, dev, self.sent, got)

    def forward(self):
        self.right_top.wait_recv()
        self.push(3, 0, self.right, self.got_far)
        self.left_low.wait_recv()
        self.push(1, 1, self.left, self.got_far)

    def near(self):
        wait_all(self.got_near, self.ref.at[0 : self.size])

    def far(self):
        wait_all(self.got_far, self.ref.at[0 : self.size])


class RingSum:
    def __init__(self, comm, top, low, held, pos, peers, sent, two_blocks):
        self.comm, self.top, self.low, self.held, self.pos = comm, top, low, held, pos
        self.right, self.left, self.sent = peers[0], peers[2], sent
        self.two_blocks, self.got = two_blocks, comm.new()

    def at(self, offset):
        pos = (self.pos + offset) % 4
        return self.top(pos), self.low(pos)

    def first(self):
        top, low = self.at(2)
        self.first_r = self.comm.send(top, self.held(0, 0), self.right, self.sent)
        self.first_l = self.comm.send(low, self.held(0, 1), self.left, self.sent)

    def near(self):
        self.comm.send(self.at(1)[1], self.held(1, 1), self.right, self.sent, self.got)
        self.comm.send(self.at(3)[0], self.held(1, 0), self.left, self.sent, self.got)

    def pass_on(self):
        self.first_r.wait_recv()
        added = self.at(1)[0][...].astype(f32) + self.held(0, 0)[...].astype(f32)
        self.held(2, 0)[...] = added.astype(bf16)
        self.comm.send(self.held(2, 0), self.held(3, 0), self.right, self.sent, self.got)
        self.first_l.wait_recv()
        added = self.at(3)[1][...].astype(f32) + self.held(0, 1)[...].astype(f32)
        self.held(2, 1)[...] = added.astype(bf16)
        self.comm.send(self.held(2, 1), self.held(3, 1), self.left, self.sent, self.got)

    def total(self):
        wait_all(self.got, self.two_blocks)
        return [
            own[...].astype(f32)
            + self.held(3, i)[...].astype(f32)
            + self.held(1, i)[...].astype(f32)
            for i, own in enumerate(self.at(0))
        ]


def z_offsets():
    return list(range(1, NZ))


def zc_offsets():
    return [(kz, kc) for kz in range(NZ) for kc in range(NC) if (kz, kc) != (0, 0)]


def unit_rows(values):
    floats = values.astype(f32)
    inverse = lax.rsqrt(jnp.sum(floats * floats, axis=1, keepdims=True) + 1e-06)
    return (floats * inverse, inverse)


def unit_back(normed, inverse, grad):
    return inverse * (grad - normed * jnp.sum(grad * normed, axis=1, keepdims=True))


def layer_norm(values):
    center = values - jnp.mean(values, axis=1, keepdims=True)
    scale_inv = lax.rsqrt(jnp.mean(center * center, axis=1, keepdims=True) + 1e-05)
    return (center * scale_inv, scale_inv)


def norm_back(grad, normed, scale_inv):
    return scale_inv * (
        grad
        - jnp.mean(grad, axis=1, keepdims=True)
        - normed * jnp.mean(grad * normed, axis=1, keepdims=True)
    )


def contract_last(left, right):
    return lax.dot_general(left, right, (((1,), (1,)), ((), ())), preferred_element_type=f32)


def contract_first(left, right):
    return lax.dot_general(left, right, (((0,), (0,)), ((), ())), preferred_element_type=f32)


def dot(left, right):
    return jnp.dot(left, right, preferred_element_type=f32)


def at(index, size):
    return pl.ds(pl.multiple_of(index * size, size), size)


def chunks(total, size):
    return [(i, min(size, total - i)) for i in range(0, total, size)]


def to_column(row, n):
    return jnp.transpose(jnp.broadcast_to(row, (128, n)))[:, 0:1]


def to_row(column, n):
    return jnp.transpose(jnp.broadcast_to(column, (n, 128)))[0:1]


def merged_lse(parts, count):
    peak = parts[0, 0:1]
    for i in range(1, count):
        peak = jnp.maximum(peak, parts[i, 0:1])
    total = jnp.zeros_like(peak)
    for i in range(count):
        total = total + parts[i, 1:2] * jnp.exp(parts[i, 0:1] - peak)
    return peak + jnp.log(total)


def body(
    img_hbm, txt_hbm, lab_hbm, lin_hbm, g1_hbm, g2_hbm, up_hbm, down_hbm, proj_hbm,
    text_hbm, input_hbm, up_grad_hbm, proj_grad_hbm,
    img_ref, txt_ref, lab_ref, lin_ref, g1_ref, g2_ref, text_out, input_out, up_out, proj_out, up_f, proj_f,
    w_up, w_down, w_proj, img_all, txt_all, lab_all, mlp_t, pooled_t, act, slope,
    res_out, res_in, n_in, n_out, logits, row_st, col_st, col_lse, rows_all, cols_all,
    grad, pimg, r_held, img_sum, img_mate, ptxt, sib_in, txo, t_held, tyo, tyi, tsum,
    rgrad, cot, cot_two, pre_out, pre_all, mg_out, mg_in,
    wpo, wpi, wp_sum, wpy, wpyi, wpz, wpzi, wpl, wu, wui, wyo, wyi, wsum, wblk,
    sems, ls,
):
    x, yl, z, c, t = coords()
    me = lax.axis_index("dp")
    rows, embed = img_ref.shape
    width = lin_ref.shape[1]
    half = rows // 2
    hidden = up_hbm.shape[1]
    hid = hidden // 8
    eh = embed // 2
    sib, mate, ynb = (dp_of(x, yl, z, 1 - c), t), (me, 1 - t), (dp_of(x, 1 - yl, z, c), t)
    zp = [(dp_of(x, yl, (z + k) % NZ, c), t) for k in range(1, NZ)]
    xp = [(dp_of((x + k) % NX, yl, z, c), t) for k in range(1, NX)]
    zc = [(dp_of(x, yl, (z + kz) % NZ, (c + kc) % NC), t) for kz, kc in zc_offsets()]
    row_peers = [
        (dp_of(x, yl, (z + k) % NZ, c), (t + j) % 2) for k in range(NZ) for j in range(2) if k or j
    ]
    col_peers = [
        (dp_of((x + kx) % NX, (yl + ky) % NYL, z, (c + kc) % NC), t)
        for kx in range(NX)
        for ky in range(NYL)
        for kc in range(NC)
        if kx or ky or kc
    ]
    cross = [p for (kz, kc), p in zip(zc_offsets(), zc) if kz and kc]
    greet = row_peers + col_peers + cross
    entry = pltpu.get_barrier_semaphore()
    small = [
        pltpu.make_async_copy(src, dst, ls.at[i])
        for i, (src, dst) in enumerate(
            [
                (img_hbm, img_ref),
                (txt_hbm, txt_ref),
                (lab_hbm, lab_ref),
                (lin_hbm, lin_ref),
                (g1_hbm, g1_ref),
                (g2_hbm, g2_ref),
            ]
        )
    ]
    loads = [
        pltpu.make_async_copy(up_hbm, w_up, ls.at[6]),
        pltpu.make_async_copy(down_hbm, w_down, ls.at[7]),
        pltpu.make_async_copy(proj_hbm, w_proj, ls.at[8]),
    ]
    for copy in small + loads:
        copy.start()
    for peer in greet:
        pl.semaphore_signal(entry, inc=1, device_id=peer, device_id_type=MESH)
    for copy in small:
        copy.wait()
    gain1, gain2 = g1_ref[...][None, :], g2_ref[...][None, :]
    my_slot = c * 8 + x * NYL + yl
    img_unit, _ = unit_rows(img_ref[...])
    img_all[at(z, rows)] = img_unit.astype(bf16)
    txt_unit, _ = unit_rows(txt_ref[at(t, half)])
    txt_all[at(my_slot, half)] = txt_unit.astype(bf16)
    lab_all[z] = jnp.broadcast_to(lab_ref[...][None, :], (8, rows))
    pl.semaphore_wait(entry, len(greet))

    comm = Comm(sems)
    send, new = comm.send, comm.new

    def same(ref, index, size, dev, sent=None, got=None):
        return send(ref.at[at(index, size)], ref.at[at(index, size)], dev, sent, got)

    txt_sent, img_sent, lab_sent, sib_got, lab_got = [new() for _ in range(5)]
    t_y = same(txt_all, my_slot, half, ynb, txt_sent)

    def txt_slot(part):
        return lambda pos: c * 8 + pos * NYL + part

    t_x = Ring(comm, txt_all, half, txt_slot(yl), x, xp, txt_sent)
    i_z = Ring(comm, img_all, rows, lambda pos: pos, z, zp, img_sent)
    for p in zp:
        send(lab_all.at[z], lab_all.at[z], p, lab_sent, lab_got)
    same(txt_all, my_slot, half, sib, txt_sent, sib_got)

    inputs = lin_ref[...].astype(f32)
    normed_in, inv_in = layer_norm(inputs)
    n_in[...] = normed_in
    mlp_in = (n_in[...] * gain1).astype(bf16)
    my_zc = z * NC + c
    for i, n in chunks(width, 128):
        mlp_t[i : i + n, at(my_zc, 128)] = jnp.transpose(
            n_in[:, i : i + n] * gain1[:, i : i + n]
        ).astype(bf16)
    loads[0].wait()

    def up_tile(i, _):
        cols = at(i, 512)
        pre = dot(mlp_in, w_up[:, cols])
        phi = 0.5 * (1.0 + lax.erf(pre * 0.7071067811865476))
        act[:, cols] = (pre * phi).astype(bf16)
        slope[:, cols] = phi + pre * jnp.exp(-0.5 * pre * pre) * 0.3989422804014327
        return _

    lax.fori_loop(0, hidden // 512, up_tile, 0)
    def to_sibling(part, offsets):
        for k in offsets:
            same(txt_all, txt_slot(part)((x + k) % NX), half, sib, txt_sent, sib_got)

    t_x.forward()
    t_y.wait_recv()
    f_x = Ring(comm, txt_all, half, txt_slot(1 - yl), x, xp, txt_sent)
    to_sibling(1 - yl, [0])
    i_z.forward()
    loads[1].wait()
    acts = act[...]
    for i, n in chunks(width, width // 2):
        if i:
            f_x.forward()
        res_out[:, i : i + n] = contract_last(acts, w_down[i : i + n]).astype(bf16)
    res_c = send(res_out, res_in, mate)
    t_x.near()
    to_sibling(yl, [1, 3])
    t_x.far()
    to_sibling(yl, [2])
    f_x.near()
    to_sibling(1 - yl, [1, 3])
    i_z.near()
    f_x.far()
    to_sibling(1 - yl, [2])
    i_z.far()
    mlp_sent, mlp_got, mlp_z = new(), new(), []

    def share_mlp(first, size):
        ref = mlp_t.at[first : first + size, at(my_zc, 128)]
        mlp_z.append((first, size, new()))
        for p in zp:
            send(ref, ref, p, mlp_sent, mlp_z[-1][2])
        send(ref, ref, sib, mlp_sent, mlp_got)

    def pass_mlp():
        for first, size, got in mlp_z:
            wait_all(got, mlp_t.at[first : first + size, 0:384])
            for k in range(1, NZ):
                ref = mlp_t.at[first : first + size, at(((z + k) % NZ) * NC + c, 128)]
                send(ref, ref, sib, mlp_sent, mlp_got)

    cut_a, cut_b = 512, 1152
    share_mlp(0, cut_a)
    n_row, n_col = img_all.shape[0], txt_all.shape[0]
    tile = 256

    col_sent, col_got, row_sent, row_got = [new() for _ in range(4)]
    my_col = (x * NYL + yl) * NC + c
    wide = 2 * tile

    def side_totals(order):
        index = (c + order) % 2
        cols = at(index, wide)
        part = logit_scale * contract_last(img_all[...], txt_all[cols])
        logits[:, cols] = part
        col_peak = jnp.max(part, axis=0, keepdims=True)
        col_st[index, 0:1] = col_peak
        col_st[index, 1:2] = jnp.sum(jnp.exp(part - col_peak), axis=0, keepdims=True)
        for p in col_peers:
            send(col_st.at[index], cols_all.at[my_col, index], p, col_sent, col_got)
        peak = jnp.max(part, axis=1, keepdims=True)
        return peak, jnp.sum(jnp.exp(part - peak), axis=1, keepdims=True)

    peak_a, total_a = side_totals(0)
    wait_all(sib_got, txt_all.at[0 : 8 * half])
    wait_all(lab_got, lab_all.at[0:3])
    peak_b, total_b = side_totals(1)
    row_peak = jnp.maximum(peak_a, peak_b)
    row_total = total_a * jnp.exp(peak_a - row_peak) + total_b * jnp.exp(peak_b - row_peak)
    my_row = z * 2 + t
    row_st[0:1] = to_row(row_peak, n_row)
    row_st[1:2] = to_row(row_total, n_row)
    for p in row_peers:
        send(row_st, rows_all.at[my_row], p, row_sent, row_got)
    share_mlp(cut_a, cut_b - cut_a)
    rows_all[my_row] = row_st[...]
    cols_all[my_col] = col_st[...]

    wait_all(col_got, cols_all.at[0:15])
    res_c.wait()
    resid = lin_ref[...].astype(f32) + (res_out[...].astype(f32) + res_in[...].astype(f32))
    normed_out, inv_out = layer_norm(resid)
    n_out[...] = normed_out
    for i, n in chunks(width, 128):
        pooled_t[i : i + n, at(c, rows)] = jnp.transpose(
            n_out[:, i : i + n] * gain2[:, i : i + n]
        ).astype(bf16)
    pool_s = send(
        pooled_t.at[:, at(c, rows)], pooled_t.at[:, at(c, rows)], sib
    )
    wait_all(row_got, rows_all.at[0:7])

    row_lse = to_column(merged_lse(rows_all, 8), n_row)
    for i in range(2):
        col_lse[:, wide * i : wide * (i + 1)] = merged_lse(cols_all[:, i], 16)
    label_col = jnp.concatenate(
        [to_column(lab_all[i, 0:1].astype(f32), rows) for i in range(NZ)], axis=0
    )

    def grad_tile(i, _):
        cols = at(i, tile)
        part = logits[:, cols]
        place = i * tile + lax.broadcasted_iota(jnp.int32, (1, tile), 1)
        slot = place // half
        index = (((slot % (NX * NYL)) * NZ + z) * NC + slot // (NX * NYL)) * rows
        index = (index + t * half + place % half).astype(f32)
        value = 0.5 * (jnp.exp(part - row_lse) + jnp.exp(part - col_lse[:, cols]))
        value = value - jnp.where(label_col == index, 1.0, 0.0)
        grad[:, cols] = value.astype(bf16)
        return _

    lax.fori_loop(0, n_col // tile, grad_tile, 0)

    def strip(part, cols):
        return lambda pos: pimg.at[
            pl.ds(pl.multiple_of(pos * rows + part * half, half), half), cols
        ]

    def image_held(cols):
        return lambda kind, part: r_held.at[kind, part, :, cols]

    parts = [slice(0, 384), slice(384, 768), slice(768, 1152), slice(1152, embed)]
    ring_sent = new()
    sums = [
        RingSum(
            comm, strip(0, cols), strip(1, cols), image_held(cols), z, zp, ring_sent,
            pimg.at[0 : 2 * rows, cols],
        )
        for cols in parts
    ]
    for cols, ring in zip(parts, sums):
        pimg[:, cols] = (logit_scale * dot(grad[...], txt_all[:, cols])).astype(bf16)
        ring.first()
    side = 8 * half
    part_sent, part_got = new(), new()
    for cols, ring in zip(parts, sums):
        ring.near()
        ptxt[:, cols] = (logit_scale * contract_first(grad[...], img_all[:, cols])).astype(bf16)
        send(ptxt.at[at(1 - c, side), cols], sib_in.at[:, cols], sib, part_sent, part_got)
        ring.pass_on()

    def text_sum():
        wait_all(part_got, sib_in)
        for pos in range(NX):
            mine = ptxt[pl.ds(pl.multiple_of(c * side + pos * pair, pair), pair)]
            txo[pos] = (
                mine.astype(f32) + sib_in[pos * pair : (pos + 1) * pair].astype(f32)
            ).astype(bf16)
        text_ring.first()
        text_ring.near()

    pair = 2 * half
    text_sent = new()
    text_ring = RingSum(
        comm,
        lambda pos: txo.at[pos, 0:half],
        lambda pos: txo.at[pos, half:],
        lambda kind, part: t_held.at[kind, part],
        x,
        xp,
        text_sent,
        txo.at[0:2],
    )
    mate_sent, mate_got = new(), new()

    def image_part(i):
        cols = parts[i]
        top, low = sums[i].total()
        img_sum[0:half, cols] = top.astype(bf16)
        img_sum[half:, cols] = low.astype(bf16)
        send(img_sum.at[:, cols], img_mate.at[:, cols], mate, mate_sent, mate_got)

    image_part(0)
    text_sum()
    image_part(1)
    image_part(2)
    image_part(3)
    share_mlp(cut_b, width - cut_b)
    loads[2].wait()
    text_ring.pass_on()
    wait_all(mate_got, img_mate)
    unit_grad = img_sum[...].astype(f32) + img_mate[...].astype(f32)
    img_norm, img_inv = unit_rows(img_ref[...])
    image_grad = unit_back(img_norm, img_inv, unit_grad)
    cotangent = image_grad.astype(bf16)
    cot[...] = cotangent
    cot_two[at(c, rows)] = cot[:, at(t, eh)]
    c_s = send(cot_two.at[at(c, rows)], cot_two.at[at(c, rows)], sib)
    eighth = width // 8
    rgrad[...] = contract_last(cotangent, w_proj[...]) * gain2
    p_cut = 112
    p_rows = (slice(0, p_cut), slice(p_cut, eighth))
    p_sent = new()
    p_ring = RingSum(
        comm,
        lambda pos: wpo.at[pos, p_rows[0]],
        lambda pos: wpo.at[pos, p_rows[1]],
        lambda kind, part: wpi.at[kind, p_rows[part]],
        x,
        xp,
        p_sent,
        wpo.at[0:2],
    )
    rgrad[...] = norm_back(rgrad[...], n_out[...], inv_out)
    resid_cot = rgrad[...].astype(bf16)
    g_sent, g_got = new(), new()
    for k in (2, 1, 3, 0):
        if k == 3:
            pool_s.wait()
            c_s.wait()
            for pos in range(NX):
                first = pl.multiple_of((2 * pos + c) * eighth, eighth)
                wpo[pos] = dot(pooled_t[pl.ds(first, eighth)], cot_two[...]).astype(bf16)
            p_ring.first()
            p_ring.near()
        other_z = (z + k) % NZ
        cols = at(other_z, 2 * hid)
        pre_out[:, cols] = (dot(resid_cot, w_down[:, cols]) * slope[:, cols]).astype(bf16)
        for j in range(NC):
            core = (c + j) % NC
            block = at(other_z * NC + core, hid)
            if k or j:
                send(
                    pre_out.at[:, block],
                    pre_all.at[at(my_zc, rows)],
                    (dp_of(x, yl, other_z, core), t),
                    g_sent,
                    g_got,
                )
            else:
                pre_all[at(my_zc, rows)] = pre_out[:, block]
    tsum[0], tsum[1] = text_ring.total()
    tyo[...] = tsum[1 - yl].astype(bf16)
    y_t = send(tyo, tyi, ynb)
    pass_mlp()
    pre_grad = pre_out[...]
    mg_sent, mg_got = new(), new()
    for i, n in chunks(width, 896):
        cols = slice(i, i + n)
        mg_out[:, cols] = contract_last(pre_grad, w_up[cols]).astype(bf16)
        send(mg_out.at[:, cols], mg_in.at[:, cols], mate, mg_sent, mg_got)
    p_ring.pass_on()

    y_t.wait()
    txt_norm, txt_inv = unit_rows(txt_ref[at(t, half)])
    text_out[at(t, half)] = unit_back(
        txt_norm, txt_inv, tsum[yl] + tyi[...].astype(f32)
    ).astype(bf16)

    wait_all(mlp_got, mlp_t.at[:, 0:512])
    wait_all(g_got, pre_all.at[0 : 7 * rows])

    wu_sent = new()

    def wu_ring(part, q):
        return RingSum(
            comm,
            lambda pos: wu.at[pos * NYL + part, :, 0:128],
            lambda pos: wu.at[pos * NYL + part, :, 128:],
            lambda kind, side: wui.at[q, kind, :, 128 * side : 128 * (side + 1)],
            x,
            xp,
            wu_sent,
            wu.at[0:2],
        )

    def wu_block(offset):
        pos = (x + offset) % NX
        wide = dot(mlp_t[at(pos, 2 * eighth)], pre_all[...]).astype(bf16)
        wu[NYL * pos], wu[NYL * pos + 1] = wide[0:eighth], wide[eighth:]

    ring_a, ring_b = wu_ring(1 - yl, 0), wu_ring(yl, 1)
    wu_block(2)
    ring_a.first()
    wu_block(1)
    wu_block(3)
    ring_a.near()
    ring_b.first()
    wu_block(0)
    ring_a.pass_on()
    ring_b.near()
    for i, total in enumerate(p_ring.total()):
        wp_sum[p_rows[i]] = total
    share = eighth // 8
    for i in range(NZ):
        wpz[i, 0 : 2 * share] = wp_sum[2 * share * i : 2 * share * (i + 1)].astype(bf16)
        wpz[i, 2 * share :] = jnp.zeros((64 - 2 * share, eh), bf16)
    pz_sent, pz_got = new(), new()
    for k, p in zip(range(1, NZ), zp):
        send(wpz.at[(z + k) % NZ], wpzi.at[k - 1], p, pz_sent, pz_got)
    p_y = comm.make(wpy, wpyi, ynb)
    p_l = comm.make(wpl.at[1 - c], proj_out, sib)

    ring_b.pass_on()

    top, low = ring_a.total()
    wyo[:, 0:128] = top.astype(bf16)
    wyo[:, 128:] = low.astype(bf16)
    w_y = send(wyo, wyi, ynb)
    t_m = same(text_out, t, half, mate)
    wait_all(mg_got, mg_in)
    dm = (mg_out[...].astype(f32) + mg_in[...].astype(f32)) * gain1
    input_out[...] = (rgrad[...] + norm_back(dm, n_in[...], inv_in)).astype(bf16)
    stores = [
        pltpu.make_async_copy(src, dst, ls.at[9 + i])
        for i, (src, dst) in enumerate(
            [
                (input_out, input_hbm),
                (text_out, text_hbm),
                (up_f, up_grad_hbm),
                (proj_f, proj_grad_hbm),
            ]
        )
    ]
    stores[0].start()

    wait_all(pz_got, wpzi)
    total = wpz[z].astype(f32)
    for k in range(NZ - 1):
        total = total + wpzi[k].astype(f32)
    wp_sum[0:64] = total
    wpy[...] = total.astype(bf16)

    @pl.when(c != yl)
    def _():
        p_y.start()

    top, low = ring_b.total()
    wsum[:, 0:128] = top
    wsum[:, 128:] = low
    w_y.wait()
    wsum[...] = wsum[...] + wyi[...].astype(f32)
    for i in range(8):
        wblk[i, 0:share] = wsum[share * i : share * (i + 1)].astype(bf16)
        wblk[i, share:] = jnp.zeros((32 - share, hid), bf16)
    last_sent, last_got = new(), new()
    for (kz, kc), p in zip(zc_offsets(), zc):
        slot = ((z + kz) % NZ) * NC + (c + kc) % NC
        send(wblk.at[slot], up_out.at[:, at(my_zc, hid)], p, last_sent, last_got)
    up_out[:, at(my_zc, hid)] = wblk[my_zc]

    @pl.when(c == yl)
    def _():
        p_y.wait_recv()
        wp_sum[0:64] = wp_sum[0:64] + wpyi[...].astype(f32)
        for i in range(NC):
            wpl[i, 0:share] = wp_sum[share * i : share * (i + 1)]
            wpl[i, share:] = jnp.zeros((32 - share, eh), f32)
        p_l.start()
        proj_out[...] = wpl[c]
        p_l.wait_send()

    @pl.when(c != yl)
    def _():
        p_y.wait_send()
        p_l.wait_recv()

    proj_f[...] = proj_out[0:share]
    stores[3].start()
    t_m.wait()
    stores[1].start()
    wait_all(last_got, up_out.at[:, 0 : 7 * hid])
    up_f[...] = up_out[0:share].astype(f32)
    stores[2].start()
    for sem, ref in (
        (txt_sent, txt_all.at[0 : 15 * half]),
        (img_sent, img_all.at[0 : 3 * rows]),
        (lab_sent, lab_all.at[0:3]),
        (mlp_sent, mlp_t.at[:, 0 : 7 * 128]),
        (col_sent, cols_all.at[0:15]),
        (row_sent, rows_all.at[0:7]),
        (ring_sent, pimg.at[0 : 3 * rows]),
        (mate_sent, img_mate),
        (part_sent, sib_in),
        (text_sent, txo.at[0:3]),
        (p_sent, wpo.at[0:3]),
        (g_sent, pre_all.at[0 : 7 * rows]),
        (mg_sent, mg_in),
        (wu_sent, wu.at[0:6]),
        (pz_sent, wpzi),
        (last_sent, up_out.at[:, 0 : 7 * hid]),
    ):
        wait_all(sem, ref)
    for copy in stores:
        copy.wait()


def finish(*refs):
    for src, dst in zip(refs[:4], refs[4:]):
        dst[...] = src[...]


def local(image_cache, text_cache, labels, layer_input, ln1_gain, ln2_gain, w_up, w_down, proj):
    rows, embed = image_cache.shape
    width = layer_input.shape[1]
    half = rows // 2
    hidden = w_up.shape[1]
    hid = hidden // 8
    eh = embed // 2
    eighth = width // 8
    share = width // 64
    n_sems = 83
    vm = pltpu.VMEM
    scratch = [
        vm((rows, embed), bf16),
        vm((rows, embed), bf16),
        vm((rows,), jnp.int32),
        vm((rows, width), bf16),
        vm((width,), f32),
        vm((width,), f32),
        vm((rows, embed), bf16),
        vm((rows, width), bf16),
        vm((32, hidden), bf16),
        vm((32, eh), f32),
        vm((width // 64, hidden), f32),
        vm((width // 64, eh), f32),
        vm(w_up.shape, bf16),
        vm(w_down.shape, bf16),
        vm(proj.shape, bf16),
        vm((NZ * rows, embed), bf16),
        vm((16 * half, embed), bf16),
        vm((NZ, 8, rows), jnp.int32),
        vm((width, 8 * rows), bf16),
        vm((width, 2 * rows), bf16),
        vm((rows, hidden), bf16),
        vm((rows, hidden), f32),
        vm((rows, width), bf16),
        vm((rows, width), bf16),
        vm((rows, width), f32),
        vm((rows, width), f32),
        vm((NZ * rows, 16 * half), f32),
        vm((2, NZ * rows), f32),
        vm((2, 2, 8 * half), f32),
        vm((1, 16 * half), f32),
        vm((8, 2, NZ * rows), f32),
        vm((16, 2, 2, 8 * half), f32),
        vm((NZ * rows, 16 * half), bf16),
        vm((NZ * rows, embed), bf16),
        vm((4, 2, half, embed), bf16),
        vm((rows, embed), bf16),
        vm((rows, embed), bf16),
        vm((16 * half, embed), bf16),
        vm((8 * half, embed), bf16),
        vm((NX, 2 * half, embed), bf16),
        vm((4, 2, half, embed), bf16),
        vm((half, embed), bf16),
        vm((half, embed), bf16),
        vm((2, half, embed), f32),
        vm((rows, width), f32),
        vm((rows, embed), bf16),
        vm((2 * rows, eh), bf16),
        vm((rows, hidden), bf16),
        vm((8 * rows, hid), bf16),
        vm((rows, width), bf16),
        vm((rows, width), bf16),
        vm((NX, eighth, eh), bf16),
        vm((4, eighth, eh), bf16),
        vm((eighth, eh), f32),
        vm((64, eh), bf16),
        vm((64, eh), bf16),
        vm((NZ, 64, eh), bf16),
        vm((NZ - 1, 64, eh), bf16),
        vm((NC, 32, eh), f32),
        vm((8, eighth, hid), bf16),
        vm((2, 4, eighth, hid), bf16),
        vm((eighth, hid), bf16),
        vm((eighth, hid), bf16),
        vm((eighth, hid), f32),
        vm((8, 32, hid), bf16),
        pltpu.SemaphoreType.DMA((n_sems,)),
        pltpu.SemaphoreType.DMA((13,)),
    ]
    anywhere = pl.BlockSpec(memory_space=pl.ANY)
    on_vmem = pl.BlockSpec(memory_space=pltpu.VMEM)
    parts = pl.pallas_call(
        body,
        name="clip_mlp",
        out_shape=[
            jax.ShapeDtypeStruct((rows, embed), bf16),
            jax.ShapeDtypeStruct((rows, width), bf16),
            jax.ShapeDtypeStruct((width // 64, hidden), f32),
            jax.ShapeDtypeStruct((width // 64, eh), f32),
        ],
        in_specs=[anywhere] * 9,
        out_specs=[anywhere] * 4,
        scratch_shapes=scratch,
        compiler_params=pltpu.CompilerParams(
            collective_id=1, has_side_effects=True, vmem_limit_bytes=VMEM_LIMIT
        ),
    )(
        image_cache,
        text_cache,
        labels,
        layer_input,
        ln1_gain,
        ln2_gain,
        w_up,
        w_down,
        proj,
    )
    return pl.pallas_call(
        finish,
        name="finish",
        out_shape=[
            jax.ShapeDtypeStruct((rows, embed), bf16),
            jax.ShapeDtypeStruct((rows, width), bf16),
            jax.ShapeDtypeStruct((share, hidden), f32),
            jax.ShapeDtypeStruct((share, eh), f32),
        ],
        in_specs=[on_vmem] * 4,
        out_specs=[on_vmem] * 4,
    )(*parts)


def solution(mesh):
    in_specs = (
        P("dp", None),
        P("dp", None),
        P("dp"),
        P("dp", None),
        P(),
        P(),
        P(None, "tensor"),
        P(None, "tensor"),
        P(),
    )
    out_specs = (P("dp", None), P("dp", None), P("dp", "tensor"), P("dp", "tensor"))
    return jax.shard_map(local, mesh=mesh, in_specs=in_specs, out_specs=out_specs, check_vma=False)
```

```python
import jax
import jax.numpy as jnp
from jax import lax
from jax.experimental import pallas as pl
from jax.experimental.pallas import tpu as pltpu
from jax.sharding import PartitionSpec as P

logit_scale = 100.0
MESH = pl.DeviceIdType.MESH
NX, NYL, NZ, NC = 4, 2, 4, 2
bf16 = jnp.bfloat16
f32 = jnp.float32
VMEM_LIMIT = 60 * 1024 * 1024


def dp_of(x, yl, z, c):
    return ((x * NYL + yl) * NZ + z) * NC + c


def coords():
    d = lax.axis_index("dp")
    c = d % NC
    z = (d // NC) % NZ
    yl = (d // (NC * NZ)) % NYL
    x = d // (NC * NZ * NYL)
    return x, yl, z, c, lax.axis_index("tensor")


class Comm:
    def __init__(self, sems):
        self.sems, self.n = sems, 0

    def new(self):
        self.n += 1
        return self.sems.at[self.n - 1]

    def make(self, src, dst, dev, sent=None, got=None):
        return pltpu.make_async_remote_copy(
            src_ref=src,
            dst_ref=dst,
            send_sem=self.new() if sent is None else sent,
            recv_sem=self.new() if got is None else got,
            device_id=dev,
            device_id_type=MESH,
        )

    def send(self, src, dst, dev, sent=None, got=None):
        copy = self.make(src, dst, dev, sent, got)
        copy.start()
        return copy


def wait_all(sem, ref):
    pltpu.make_async_copy(ref, ref, sem).wait()


class Ring:
    def __init__(self, comm, ref, size, slot, pos, peers, sent):
        self.comm, self.ref, self.size, self.slot, self.pos = comm, ref, size, slot, pos
        self.right, self.left, self.sent = peers[0], peers[2], sent
        self.got_near, self.got_far = comm.new(), comm.new()
        self.right_top = self.push(0, 0, self.right)
        self.left_low = self.push(0, 1, self.left)
        self.push(0, 1, self.right, self.got_near)
        self.push(0, 0, self.left, self.got_near)

    def push(self, offset, part, dev, got=None):
        n = self.size // 2
        first = pl.multiple_of(self.slot((self.pos + offset) % 4) * self.size + part * n, n)
        ref = self.ref.at[pl.ds(first, n)]
        return self.comm.send(ref, ref, dev, self.sent, got)

    def forward(self):
        self.right_top.wait_recv()
        self.push(3, 0, self.right, self.got_far)
        self.left_low.wait_recv()
        self.push(1, 1, self.left, self.got_far)

    def near(self):
        wait_all(self.got_near, self.ref.at[0 : self.size])

    def far(self):
        wait_all(self.got_far, self.ref.at[0 : self.size])


class RingSum:
    def __init__(self, comm, top, low, held, pos, peers, sent, two_blocks):
        self.comm, self.top, self.low, self.held, self.pos = comm, top, low, held, pos
        self.right, self.left, self.sent = peers[0], peers[2], sent
        self.two_blocks, self.got = two_blocks, comm.new()

    def at(self, offset):
        pos = (self.pos + offset) % 4
        return self.top(pos), self.low(pos)

    def first(self):
        top, low = self.at(2)
        self.first_r = self.comm.send(top, self.held(0, 0), self.right, self.sent)
        self.first_l = self.comm.send(low, self.held(0, 1), self.left, self.sent)

    def near(self):
        self.comm.send(self.at(1)[1], self.held(1, 1), self.right, self.sent, self.got)
        self.comm.send(self.at(3)[0], self.held(1, 0), self.left, self.sent, self.got)

    def pass_on(self):
        self.first_r.wait_recv()
        added = self.at(1)[0][...].astype(f32) + self.held(0, 0)[...].astype(f32)
        self.held(2, 0)[...] = added.astype(bf16)
        self.comm.send(self.held(2, 0), self.held(3, 0), self.right, self.sent, self.got)
        self.first_l.wait_recv()
        added = self.at(3)[1][...].astype(f32) + self.held(0, 1)[...].astype(f32)
        self.held(2, 1)[...] = added.astype(bf16)
        self.comm.send(self.held(2, 1), self.held(3, 1), self.left, self.sent, self.got)

    def total(self):
        wait_all(self.got, self.two_blocks)
        return [
            own[...].astype(f32)
            + self.held(3, i)[...].astype(f32)
            + self.held(1, i)[...].astype(f32)
            for i, own in enumerate(self.at(0))
        ]


def z_offsets():
    return list(range(1, NZ))


def zc_offsets():
    return [(kz, kc) for kz in range(NZ) for kc in range(NC) if (kz, kc) != (0, 0)]


def unit_rows(values):
    floats = values.astype(f32)
    inverse = lax.rsqrt(jnp.sum(floats * floats, axis=1, keepdims=True) + 1e-06)
    return (floats * inverse, inverse)


def unit_back(normed, inverse, grad):
    return inverse * (grad - normed * jnp.sum(grad * normed, axis=1, keepdims=True))


def layer_norm(values):
    center = values - jnp.mean(values, axis=1, keepdims=True)
    scale_inv = lax.rsqrt(jnp.mean(center * center, axis=1, keepdims=True) + 1e-05)
    return (center * scale_inv, scale_inv)


def norm_back(grad, normed, scale_inv):
    return scale_inv * (
        grad
        - jnp.mean(grad, axis=1, keepdims=True)
        - normed * jnp.mean(grad * normed, axis=1, keepdims=True)
    )


def contract_last(left, right):
    return lax.dot_general(left, right, (((1,), (1,)), ((), ())), preferred_element_type=f32)


def contract_first(left, right):
    return lax.dot_general(left, right, (((0,), (0,)), ((), ())), preferred_element_type=f32)


def dot(left, right):
    return jnp.dot(left, right, preferred_element_type=f32)


def at(index, size):
    return pl.ds(pl.multiple_of(index * size, size), size)


def chunks(total, size):
    return [(i, min(size, total - i)) for i in range(0, total, size)]


def to_column(row, n):
    return jnp.transpose(jnp.broadcast_to(row, (128, n)))[:, 0:1]


def to_row(column, n):
    return jnp.transpose(jnp.broadcast_to(column, (n, 128)))[0:1]


def merged_lse(parts, count):
    peak = parts[0, 0:1]
    for i in range(1, count):
        peak = jnp.maximum(peak, parts[i, 0:1])
    total = jnp.zeros_like(peak)
    for i in range(count):
        total = total + parts[i, 1:2] * jnp.exp(parts[i, 0:1] - peak)
    return peak + jnp.log(total)


def body(
    img_hbm, txt_hbm, lab_hbm, lin_hbm, g1_hbm, g2_hbm, up_hbm, down_hbm, proj_hbm,
    text_hbm, input_hbm, up_grad_hbm, proj_grad_hbm,
    img_ref, txt_ref, lab_ref, lin_ref, g1_ref, g2_ref, text_out, input_out, up_out, proj_out, up_f, proj_f,
    w_up, w_down, w_proj_t, img_all, txt_all, lab_all, mlp_t, pooled_t, act, slope,
    res_out, res_in, n_in, n_out, logits, row_st, col_st, col_lse, rows_all, cols_all,
    grad, pimg, r_held, img_sum, img_mate, ptxt, sib_in, txo, t_held, tyo, tyi, tsum,
    rgrad, cot, cot_two, pre_out, pre_all, mg_out, mg_in,
    wpo, wpi, wp_sum, wpy, wpyi, wpz, wpzi, wpl, wu, wui, wyo, wyi, wsum, wblk,
    sems, ls,
):
    x, yl, z, c, t = coords()
    me = lax.axis_index("dp")
    rows, embed = img_ref.shape
    width = lin_ref.shape[1]
    half = rows // 2
    hidden = up_hbm.shape[1]
    hid = hidden // 8
    eh = embed // 2
    sib, mate, ynb = (dp_of(x, yl, z, 1 - c), t), (me, 1 - t), (dp_of(x, 1 - yl, z, c), t)
    zp = [(dp_of(x, yl, (z + k) % NZ, c), t) for k in range(1, NZ)]
    xp = [(dp_of((x + k) % NX, yl, z, c), t) for k in range(1, NX)]
    zc = [(dp_of(x, yl, (z + kz) % NZ, (c + kc) % NC), t) for kz, kc in zc_offsets()]
    row_peers = [
        (dp_of(x, yl, (z + k) % NZ, c), (t + j) % 2) for k in range(NZ) for j in range(2) if k or j
    ]
    col_peers = [
        (dp_of((x + kx) % NX, (yl + ky) % NYL, z, (c + kc) % NC), t)
        for kx in range(NX)
        for ky in range(NYL)
        for kc in range(NC)
        if kx or ky or kc
    ]
    cross = [p for (kz, kc), p in zip(zc_offsets(), zc) if kz and kc]
    greet = row_peers + col_peers + cross
    entry = pltpu.get_barrier_semaphore()
    small = [
        pltpu.make_async_copy(src, dst, ls.at[i])
        for i, (src, dst) in enumerate(
            [
                (img_hbm, img_ref),
                (txt_hbm, txt_ref),
                (lab_hbm, lab_ref),
                (lin_hbm, lin_ref),
                (g1_hbm, g1_ref),
                (g2_hbm, g2_ref),
            ]
        )
    ]
    loads = [
        pltpu.make_async_copy(up_hbm, w_up, ls.at[6]),
        pltpu.make_async_copy(down_hbm, w_down, ls.at[7]),
    ]
    homes = [(0, ptxt), (ptxt.shape[0], pimg), (ptxt.shape[0] + pimg.shape[0], img_sum)]
    for i, (first, home) in enumerate(homes):
        block = proj_hbm.at[first : first + home.shape[0]]
        loads.append(pltpu.make_async_copy(block, home, ls.at[(8, 13, 14)[i]]))
    for copy in small + loads:
        copy.start()
    for peer in greet:
        pl.semaphore_signal(entry, inc=1, device_id=peer, device_id_type=MESH)
    for copy in small:
        copy.wait()
    gain1, gain2 = g1_ref[...][None, :], g2_ref[...][None, :]
    my_slot = c * 8 + x * NYL + yl
    img_unit, _ = unit_rows(img_ref[...])
    img_all[at(z, rows)] = img_unit.astype(bf16)
    txt_unit, _ = unit_rows(txt_ref[at(t, half)])
    txt_all[at(my_slot, half)] = txt_unit.astype(bf16)
    lab_all[z] = jnp.broadcast_to(lab_ref[...][None, :], (8, rows))
    pl.semaphore_wait(entry, len(greet))

    comm = Comm(sems)
    send, new = comm.send, comm.new

    def same(ref, index, size, dev, sent=None, got=None):
        return send(ref.at[at(index, size)], ref.at[at(index, size)], dev, sent, got)

    txt_sent, img_sent, lab_sent, sib_got, lab_got = [new() for _ in range(5)]
    t_y = same(txt_all, my_slot, half, ynb, txt_sent)

    def txt_slot(part):
        return lambda pos: c * 8 + pos * NYL + part

    t_x = Ring(comm, txt_all, half, txt_slot(yl), x, xp, txt_sent)
    i_z = Ring(comm, img_all, rows, lambda pos: pos, z, zp, img_sent)
    for p in zp:
        send(lab_all.at[z], lab_all.at[z], p, lab_sent, lab_got)
    same(txt_all, my_slot, half, sib, txt_sent, sib_got)

    inputs = lin_ref[...].astype(f32)
    normed_in, inv_in = layer_norm(inputs)
    n_in[...] = normed_in
    mlp_in = (n_in[...] * gain1).astype(bf16)
    my_zc = z * NC + c
    for i, n in chunks(width, 128):
        mlp_t[i : i + n, at(my_zc, 128)] = jnp.transpose(
            n_in[:, i : i + n] * gain1[:, i : i + n]
        ).astype(bf16)
    loads[0].wait()

    def up_tile(i, _):
        cols = at(i, 512)
        pre = dot(mlp_in, w_up[:, cols])
        phi = 0.5 * (1.0 + lax.erf(pre * 0.7071067811865476))
        act[:, cols] = (pre * phi).astype(bf16)
        slope[:, cols] = phi + pre * jnp.exp(-0.5 * pre * pre) * 0.3989422804014327
        return _

    lax.fori_loop(0, hidden // 512, up_tile, 0)
    def to_sibling(part, offsets):
        for k in offsets:
            same(txt_all, txt_slot(part)((x + k) % NX), half, sib, txt_sent, sib_got)

    t_x.forward()
    t_y.wait_recv()
    f_x = Ring(comm, txt_all, half, txt_slot(1 - yl), x, xp, txt_sent)
    to_sibling(1 - yl, [0])
    i_z.forward()
    loads[1].wait()
    acts = act[...]
    for i, n in chunks(width, width // 2):
        res_out[:, i : i + n] = contract_last(acts, w_down[i : i + n]).astype(bf16)
    res_c = send(res_out, res_in, mate)
    f_x.forward()
    t_x.near()
    to_sibling(yl, [1, 3])
    t_x.far()
    to_sibling(yl, [2])
    f_x.near()
    to_sibling(1 - yl, [1, 3])
    i_z.near()
    f_x.far()
    to_sibling(1 - yl, [2])
    i_z.far()
    mlp_sent, mlp_got, mlp_z = new(), new(), []

    def share_mlp(first, size):
        ref = mlp_t.at[first : first + size, at(my_zc, 128)]
        mlp_z.append((first, size, new()))
        for p in zp:
            send(ref, ref, p, mlp_sent, mlp_z[-1][2])
        send(ref, ref, sib, mlp_sent, mlp_got)

    def pass_mlp():
        for first, size, got in mlp_z:
            wait_all(got, mlp_t.at[first : first + size, 0:384])
            for k in range(1, NZ):
                ref = mlp_t.at[first : first + size, at(((z + k) % NZ) * NC + c, 128)]
                send(ref, ref, sib, mlp_sent, mlp_got)

    cut_a, cut_b = 512, 960
    share_mlp(0, cut_a)
    n_row, n_col = img_all.shape[0], txt_all.shape[0]
    tile = 256

    col_sent, col_got, row_sent, row_got = [new() for _ in range(4)]
    my_col, my_row = (x * NYL + yl) * NC + c, z * 2 + t
    wide = 2 * tile

    def side_totals(order):
        index = (c + order) % 2
        cols = at(index, wide)
        part = logit_scale * contract_last(img_all[...], txt_all[cols])
        logits[:, cols] = part
        peak = jnp.max(part, axis=1, keepdims=True)
        total = jnp.sum(jnp.exp(part - peak), axis=1, keepdims=True)
        if order:
            row_peak = jnp.maximum(peak_a, peak)
            row_st[0:1] = to_row(row_peak, n_row)
            row_st[1:2] = to_row(
                total_a * jnp.exp(peak_a - row_peak) + total * jnp.exp(peak - row_peak), n_row
            )
            for p in row_peers:
                send(row_st, rows_all.at[my_row], p, row_sent, row_got)
        col_peak = jnp.max(part, axis=0, keepdims=True)
        col_st[index, 0:1] = col_peak
        col_st[index, 1:2] = jnp.sum(jnp.exp(part - col_peak), axis=0, keepdims=True)
        for p in col_peers:
            send(col_st.at[index], cols_all.at[my_col, index], p, col_sent, col_got)
        return peak, total

    peak_a, total_a = side_totals(0)
    wait_all(sib_got, txt_all.at[0 : 8 * half])
    wait_all(lab_got, lab_all.at[0:3])
    side_totals(1)
    share_mlp(cut_a, cut_b - cut_a)
    rows_all[my_row] = row_st[...]
    cols_all[my_col] = col_st[...]

    for copy in loads[2:]:
        copy.wait()
    for first, home in homes:

        def turn_tile(i, _):
            w_proj_t[:, at(first // 128 + i, 128)] = jnp.transpose(home[at(i, 128)])
            return _

        lax.fori_loop(0, home.shape[0] // 128, turn_tile, 0)
    label_col = jnp.concatenate(
        [to_column(lab_all[i, 0:1].astype(f32), rows) for i in range(NZ)], axis=0
    )
    wait_all(col_got, cols_all.at[0:15])
    res_c.wait()
    resid = lin_ref[...].astype(f32) + (res_out[...].astype(f32) + res_in[...].astype(f32))
    normed_out, inv_out = layer_norm(resid)
    n_out[...] = normed_out
    for i, n in chunks(width, 128):
        pooled_t[i : i + n, at(c, rows)] = jnp.transpose(
            n_out[:, i : i + n] * gain2[:, i : i + n]
        ).astype(bf16)
    pool_s = send(
        pooled_t.at[:, at(c, rows)], pooled_t.at[:, at(c, rows)], sib
    )
    wait_all(row_got, rows_all.at[0:7])

    row_lse = to_column(merged_lse(rows_all, 8), n_row)
    for i in range(2):
        col_lse[:, wide * i : wide * (i + 1)] = merged_lse(cols_all[:, i], 16)

    def grad_tile(i, _):
        cols = at(i, tile)
        part = logits[:, cols]
        place = i * tile + lax.broadcasted_iota(jnp.int32, (1, tile), 1)
        slot = place // half
        index = (((slot % (NX * NYL)) * NZ + z) * NC + slot // (NX * NYL)) * rows
        index = (index + t * half + place % half).astype(f32)
        value = 0.5 * (jnp.exp(part - row_lse) + jnp.exp(part - col_lse[:, cols]))
        value = value - jnp.where(label_col == index, 1.0, 0.0)
        grad[:, cols] = value.astype(bf16)
        return _

    lax.fori_loop(0, n_col // tile, grad_tile, 0)

    def strip(part, cols):
        return lambda pos: pimg.at[
            pl.ds(pl.multiple_of(pos * rows + part * half, half), half), cols
        ]

    def image_held(cols):
        return lambda kind, part: r_held.at[kind, part, :, cols]

    parts = [slice(0, 384), slice(384, 768), slice(768, 1152), slice(1152, embed)]
    ring_sent = new()
    sums = [
        RingSum(
            comm, strip(0, cols), strip(1, cols), image_held(cols), z, zp, ring_sent,
            pimg.at[0 : 2 * rows, cols],
        )
        for cols in parts
    ]
    for cols, ring in zip(parts, sums):
        pimg[:, cols] = (logit_scale * dot(grad[...], txt_all[:, cols])).astype(bf16)
        ring.first()
    side = 8 * half
    part_sent, part_got = new(), new()
    for cols, ring in zip(parts, sums):
        ring.near()
        ptxt[:, cols] = (logit_scale * contract_first(grad[...], img_all[:, cols])).astype(bf16)
        send(ptxt.at[at(1 - c, side), cols], sib_in.at[:, cols], sib, part_sent, part_got)
        ring.pass_on()

    def text_sum():
        wait_all(part_got, sib_in)
        for pos in range(NX):
            mine = ptxt[pl.ds(pl.multiple_of(c * side + pos * pair, pair), pair)]
            txo[pos] = (
                mine.astype(f32) + sib_in[pos * pair : (pos + 1) * pair].astype(f32)
            ).astype(bf16)
        text_ring.first()
        text_ring.near()

    pair = 2 * half
    text_sent = new()
    text_ring = RingSum(
        comm,
        lambda pos: txo.at[pos, 0:half],
        lambda pos: txo.at[pos, half:],
        lambda kind, part: t_held.at[kind, part],
        x,
        xp,
        text_sent,
        txo.at[0:2],
    )
    mate_sent, mate_got = new(), new()

    def image_part(i):
        cols = parts[i]
        top, low = sums[i].total()
        img_sum[0:half, cols] = top.astype(bf16)
        img_sum[half:, cols] = low.astype(bf16)
        send(img_sum.at[:, cols], img_mate.at[:, cols], mate, mate_sent, mate_got)

    image_part(0)
    text_sum()
    image_part(1)
    image_part(2)
    image_part(3)
    share_mlp(cut_b, width - cut_b)
    text_ring.pass_on()
    img_norm, img_inv = unit_rows(img_ref[...])
    wait_all(mate_got, img_mate)
    unit_grad = img_sum[...].astype(f32) + img_mate[...].astype(f32)
    image_grad = unit_back(img_norm, img_inv, unit_grad)
    cotangent = image_grad.astype(bf16)
    cot[...] = cotangent
    cot_two[at(c, rows)] = cot[:, at(t, eh)]
    c_s = send(cot_two.at[at(c, rows)], cot_two.at[at(c, rows)], sib)
    eighth = width // 8
    rgrad[...] = dot(cotangent, w_proj_t[...]) * gain2
    p_cut = 112
    p_rows = (slice(0, p_cut), slice(p_cut, eighth))
    p_sent = new()
    p_ring = RingSum(
        comm,
        lambda pos: wpo.at[pos, p_rows[0]],
        lambda pos: wpo.at[pos, p_rows[1]],
        lambda kind, part: wpi.at[kind, p_rows[part]],
        x,
        xp,
        p_sent,
        wpo.at[0:2],
    )
    rgrad[...] = norm_back(rgrad[...], n_out[...], inv_out)
    resid_cot = rgrad[...].astype(bf16)
    g_sent, g_got = new(), new()
    for k in (2, 1, 3, 0):
        if k == 3:
            pool_s.wait()
            c_s.wait()
            for pos in range(NX):
                first = pl.multiple_of((2 * pos + c) * eighth, eighth)
                wpo[pos] = dot(pooled_t[pl.ds(first, eighth)], cot_two[...]).astype(bf16)
            p_ring.first()
            p_ring.near()
        other_z = (z + k) % NZ
        cols = at(other_z, 2 * hid)
        pre_out[:, cols] = (dot(resid_cot, w_down[:, cols]) * slope[:, cols]).astype(bf16)
        for j in range(NC):
            core = (c + j) % NC
            block = at(other_z * NC + core, hid)
            if k or j:
                send(
                    pre_out.at[:, block],
                    pre_all.at[at(my_zc, rows)],
                    (dp_of(x, yl, other_z, core), t),
                    g_sent,
                    g_got,
                )
            else:
                pre_all[at(my_zc, rows)] = pre_out[:, block]
    tsum[0], tsum[1] = text_ring.total()
    tyo[...] = tsum[1 - yl].astype(bf16)
    y_t = send(tyo, tyi, ynb)
    pass_mlp()
    pre_grad = pre_out[...]
    mg_sent, mg_got = new(), new()
    for i, n in chunks(width, 896):
        cols = slice(i, i + n)
        mg_out[:, cols] = contract_last(pre_grad, w_up[cols]).astype(bf16)
        send(mg_out.at[:, cols], mg_in.at[:, cols], mate, mg_sent, mg_got)
    p_ring.pass_on()

    y_t.wait()
    txt_norm, txt_inv = unit_rows(txt_ref[at(t, half)])
    text_out[at(t, half)] = unit_back(
        txt_norm, txt_inv, tsum[yl] + tyi[...].astype(f32)
    ).astype(bf16)

    wait_all(mlp_got, mlp_t.at[:, 0:512])
    wait_all(g_got, pre_all.at[0 : 7 * rows])

    wu_sent = new()

    def wu_ring(part, q):
        return RingSum(
            comm,
            lambda pos: wu.at[at(pos * NYL + part, eighth), 0:128],
            lambda pos: wu.at[at(pos * NYL + part, eighth), 128:],
            lambda kind, side: wui.at[q, kind, :, 128 * side : 128 * (side + 1)],
            x,
            xp,
            wu_sent,
            wu.at[0 : 2 * eighth],
        )

    def wu_block(offset):
        block = at((x + offset) % NX, 2 * eighth)
        wu[block] = dot(mlp_t[block], pre_all[...]).astype(bf16)

    ring_a, ring_b = wu_ring(1 - yl, 0), wu_ring(yl, 1)
    wu_block(2)
    ring_a.first()
    wu_block(1)
    wu_block(3)
    ring_a.near()
    ring_b.first()
    wu_block(0)
    ring_a.pass_on()
    ring_b.near()
    for i, total in enumerate(p_ring.total()):
        wp_sum[p_rows[i]] = total
    share = eighth // 8
    for i in range(NZ):
        wpz[i, 0 : 2 * share] = wp_sum[2 * share * i : 2 * share * (i + 1)].astype(bf16)
        wpz[i, 2 * share :] = jnp.zeros((64 - 2 * share, eh), bf16)
    pz_sent, pz_got = new(), new()
    for k, p in zip(range(1, NZ), zp):
        send(wpz.at[(z + k) % NZ], wpzi.at[k - 1], p, pz_sent, pz_got)
    p_y = comm.make(wpy, wpyi, ynb)
    p_l = comm.make(wpl.at[1 - c], proj_out, sib)

    ring_b.pass_on()

    top, low = ring_a.total()
    wyo[:, 0:128] = top.astype(bf16)
    wyo[:, 128:] = low.astype(bf16)
    w_y = send(wyo, wyi, ynb)
    t_m = same(text_out, t, half, mate)
    wait_all(mg_got, mg_in)
    dm = (mg_out[...].astype(f32) + mg_in[...].astype(f32)) * gain1
    input_out[...] = (rgrad[...] + norm_back(dm, n_in[...], inv_in)).astype(bf16)
    stores = [
        pltpu.make_async_copy(src, dst, ls.at[9 + i])
        for i, (src, dst) in enumerate(
            [
                (input_out, input_hbm),
                (text_out, text_hbm),
                (up_f, up_grad_hbm),
                (proj_f, proj_grad_hbm),
            ]
        )
    ]
    stores[0].start()

    wait_all(pz_got, wpzi)
    total = wpz[z].astype(f32)
    for k in range(NZ - 1):
        total = total + wpzi[k].astype(f32)
    wp_sum[0:64] = total
    wpy[...] = total.astype(bf16)

    @pl.when(c != yl)
    def _():
        p_y.start()

    top, low = ring_b.total()
    wsum[:, 0:128] = top
    wsum[:, 128:] = low
    w_y.wait()
    wsum[...] = wsum[...] + wyi[...].astype(f32)
    for i in range(8):
        wblk[i, 0:share] = wsum[share * i : share * (i + 1)].astype(bf16)
        wblk[i, share:] = jnp.zeros((32 - share, hid), bf16)
    last_sent, last_got = new(), new()
    for (kz, kc), p in zip(zc_offsets(), zc):
        slot = ((z + kz) % NZ) * NC + (c + kc) % NC
        send(wblk.at[slot], up_out.at[:, at(my_zc, hid)], p, last_sent, last_got)
    up_out[:, at(my_zc, hid)] = wblk[my_zc]

    @pl.when(c == yl)
    def _():
        p_y.wait_recv()
        wp_sum[0:64] = wp_sum[0:64] + wpyi[...].astype(f32)
        for i in range(NC):
            wpl[i, 0:share] = wp_sum[share * i : share * (i + 1)]
            wpl[i, share:] = jnp.zeros((32 - share, eh), f32)
        p_l.start()
        proj_out[...] = wpl[c]
        p_l.wait_send()

    @pl.when(c != yl)
    def _():
        p_y.wait_send()
        p_l.wait_recv()

    proj_f[...] = proj_out[0:share]
    stores[3].start()
    t_m.wait()
    stores[1].start()
    wait_all(last_got, up_out.at[:, 0 : 7 * hid])
    up_f[...] = up_out[0:share].astype(f32)
    stores[2].start()
    for sem, ref in (
        (txt_sent, txt_all.at[0 : 15 * half]),
        (img_sent, img_all.at[0 : 3 * rows]),
        (lab_sent, lab_all.at[0:3]),
        (mlp_sent, mlp_t.at[:, 0 : 7 * 128]),
        (col_sent, cols_all.at[0:15]),
        (row_sent, rows_all.at[0:7]),
        (ring_sent, pimg.at[0 : 3 * rows]),
        (mate_sent, img_mate),
        (part_sent, sib_in),
        (text_sent, txo.at[0:3]),
        (p_sent, wpo.at[0:3]),
        (g_sent, pre_all.at[0 : 7 * rows]),
        (mg_sent, mg_in),
        (wu_sent, wu.at[0 : 6 * eighth]),
        (pz_sent, wpzi),
        (last_sent, up_out.at[:, 0 : 7 * hid]),
    ):
        wait_all(sem, ref)
    for copy in stores:
        copy.wait()


def finish(*refs):
    for src, dst in zip(refs[:4], refs[4:]):
        dst[...] = src[...]


def local(image_cache, text_cache, labels, layer_input, ln1_gain, ln2_gain, w_up, w_down, proj):
    rows, embed = image_cache.shape
    width = layer_input.shape[1]
    half = rows // 2
    hidden = w_up.shape[1]
    hid = hidden // 8
    eh = embed // 2
    eighth = width // 8
    share = width // 64
    n_sems = 83
    vm = pltpu.VMEM
    scratch = [
        vm((rows, embed), bf16),
        vm((rows, embed), bf16),
        vm((rows,), jnp.int32),
        vm((rows, width), bf16),
        vm((width,), f32),
        vm((width,), f32),
        vm((rows, embed), bf16),
        vm((rows, width), bf16),
        vm((32, hidden), bf16),
        vm((32, eh), f32),
        vm((width // 64, hidden), f32),
        vm((width // 64, eh), f32),
        vm(w_up.shape, bf16),
        vm(w_down.shape, bf16),
        vm((embed, width), bf16),
        vm((NZ * rows, embed), bf16),
        vm((16 * half, embed), bf16),
        vm((NZ, 8, rows), jnp.int32),
        vm((width, 8 * rows), bf16),
        vm((width, 2 * rows), bf16),
        vm((rows, hidden), bf16),
        vm((rows, hidden), f32),
        vm((rows, width), bf16),
        vm((rows, width), bf16),
        vm((rows, width), f32),
        vm((rows, width), f32),
        vm((NZ * rows, 16 * half), f32),
        vm((2, NZ * rows), f32),
        vm((2, 2, 8 * half), f32),
        vm((1, 16 * half), f32),
        vm((8, 2, NZ * rows), f32),
        vm((16, 2, 2, 8 * half), f32),
        vm((NZ * rows, 16 * half), bf16),
        vm((NZ * rows, embed), bf16),
        vm((4, 2, half, embed), bf16),
        vm((rows, embed), bf16),
        vm((rows, embed), bf16),
        vm((16 * half, embed), bf16),
        vm((8 * half, embed), bf16),
        vm((NX, 2 * half, embed), bf16),
        vm((4, 2, half, embed), bf16),
        vm((half, embed), bf16),
        vm((half, embed), bf16),
        vm((2, half, embed), f32),
        vm((rows, width), f32),
        vm((rows, embed), bf16),
        vm((2 * rows, eh), bf16),
        vm((rows, hidden), bf16),
        vm((8 * rows, hid), bf16),
        vm((rows, width), bf16),
        vm((rows, width), bf16),
        vm((NX, eighth, eh), bf16),
        vm((4, eighth, eh), bf16),
        vm((eighth, eh), f32),
        vm((64, eh), bf16),
        vm((64, eh), bf16),
        vm((NZ, 64, eh), bf16),
        vm((NZ - 1, 64, eh), bf16),
        vm((NC, 32, eh), f32),
        vm((8 * eighth, hid), bf16),
        vm((2, 4, eighth, hid), bf16),
        vm((eighth, hid), bf16),
        vm((eighth, hid), bf16),
        vm((eighth, hid), f32),
        vm((8, 32, hid), bf16),
        pltpu.SemaphoreType.DMA((n_sems,)),
        pltpu.SemaphoreType.DMA((15,)),
    ]
    anywhere = pl.BlockSpec(memory_space=pl.ANY)
    on_vmem = pl.BlockSpec(memory_space=pltpu.VMEM)
    parts = pl.pallas_call(
        body,
        name="clip_mlp",
        out_shape=[
            jax.ShapeDtypeStruct((rows, embed), bf16),
            jax.ShapeDtypeStruct((rows, width), bf16),
            jax.ShapeDtypeStruct((width // 64, hidden), f32),
            jax.ShapeDtypeStruct((width // 64, eh), f32),
        ],
        in_specs=[anywhere] * 9,
        out_specs=[anywhere] * 4,
        scratch_shapes=scratch,
        compiler_params=pltpu.CompilerParams(
            collective_id=1, has_side_effects=True, vmem_limit_bytes=VMEM_LIMIT
        ),
    )(
        image_cache,
        text_cache,
        labels,
        layer_input,
        ln1_gain,
        ln2_gain,
        w_up,
        w_down,
        proj,
    )
    return pl.pallas_call(
        finish,
        name="finish",
        out_shape=[
            jax.ShapeDtypeStruct((rows, embed), bf16),
            jax.ShapeDtypeStruct((rows, width), bf16),
            jax.ShapeDtypeStruct((share, hidden), f32),
            jax.ShapeDtypeStruct((share, eh), f32),
        ],
        in_specs=[on_vmem] * 4,
        out_specs=[on_vmem] * 4,
    )(*parts)


def solution(mesh):
    in_specs = (
        P("dp", None),
        P("dp", None),
        P("dp"),
        P("dp", None),
        P(),
        P(),
        P(None, "tensor"),
        P(None, "tensor"),
        P(),
    )
    out_specs = (P("dp", None), P("dp", None), P("dp", "tensor"), P("dp", "tensor"))
    return jax.shard_map(local, mesh=mesh, in_specs=in_specs, out_specs=out_specs, check_vma=False)
```
